32 devices in a mesh: wide: 8 (over z, x), narrow: 4 (over y, core).
Axes of the slice: x: 2, y: 2, z: 4, core: 2. Of those that a mesh axis runs over, the one named last changes fastest.
Arguments:
- tokens: bfloat16 [16384, 768], P('wide'), may hold values from -1.796875 to 1.796875
- condition: bfloat16 [16, 768], P('wide'), may hold values from -6 to 6
- validity: int32 [16384], P('wide'), may hold values from 0 to 1, as said below
- cotangent: bfloat16 [16384, 768], P('wide'), may hold values from -6 to 6
- w_ada: bfloat16 [768, 4608], replicated, may hold values from -0.21875 to 0.21875
- b_ada: bfloat16 [4608], replicated, may hold values from -3 to 3
- w_qkv: bfloat16 [3, 768, 768], P(None, None, 'narrow'), may hold values from -0.21875 to 0.21875
- b_qkv: bfloat16 [2, 768], P(None, 'narrow'), may hold values from -3 to 3
- w_out: bfloat16 [768, 768], P('narrow'), may hold values from -6 to 6
- b_out: bfloat16 [768], replicated, may hold values from -3 to 3
- w_up: bfloat16 [768, 3072], P(None, 'narrow'), may hold values from -0.21875 to 0.21875
- b_up: bfloat16 [3072], P('narrow'), may hold values from -3 to 3
- conv_w: bfloat16 [9, 3072], P(None, 'narrow'), may hold values from -2 to 2
- conv_b: bfloat16 [3072], P('narrow'), may hold values from -3 to 3
- w_down: bfloat16 [3072, 768], P('narrow'), may hold values from -0.109375 to 0.109375
- b_down: bfloat16 [768], replicated, may hold values from -0.59765625 to 0.59765625
Outputs:
- block_out: bfloat16 [16384, 768], P('wide')
- grad_tokens: float32 [16384, 768], P('wide')
- grad_condition: float32 [16, 768], P('wide')
- grad_w_ada: float32 [768, 4608], P('wide')
- grad_b_ada: float32 [4608], P('wide')
- grad_w_qkv: float32 [3, 768, 768], P(None, 'wide', 'narrow')
- grad_b_qkv: float32 [2, 768], P(None, 'narrow')
- grad_w_out: float32 [768, 768], P('narrow', 'wide')
- grad_b_out: float32 [768], P('wide')
- grad_w_up: float32 [768, 3072], P('wide', 'narrow')
- grad_b_up: float32 [3072], P('narrow')
- grad_conv_w: float32 [9, 3072], P(None, 'narrow')
- grad_conv_b: float32 [3072], P('narrow')
- grad_w_down: float32 [3072, 768], P('narrow', 'wide')
- grad_b_down: float32 [768], P('wide')
The draws below stay inside these ranges and needn't reach their ends.
Inputs may be any that keep to these rules, and one draw needn't show every extreme that they name: `validity`: each latent's tokens are its 32 x 32 grid in row-major order; the valid ones are exactly those in the first h rows and the first w columns, h and w between 16 and 32 for each latent.
All inputs are finite; a program needn't handle non-finite values.
Results may differ from the reference program's by a relative error of at most 0.02.
The reference program's roundings to bfloat16 on the way count: a program that leaves them out, or rounds other values in their place, can miss the bound.
Values may be sent and summed in bfloat16 or wider, within the bound.
A program may use at most 256 MiB of HBM per device.

```python
from functools import partial
import jax
import jax.numpy as jnp
from jax import lax

D = 768
HEADS = 12
HEAD_DIM = 64
FF = 3072
GRID = 32
LATENTS = 16
TOKENS = 16384


def draw_validity(key, part):
    key = jax.random.fold_in(key, 11)
    height_key, width_key = jax.random.split(key)
    heights = jax.random.randint(height_key, (LATENTS,), GRID // 2, GRID + 1)
    widths = jax.random.randint(width_key, (LATENTS,), GRID // 2, GRID + 1)
    positions = jnp.arange(GRID)
    inside = (positions[None, :, None] < heights[:, None, None]) & (positions[None, None, :] < widths[:, None, None])
    return inside.astype(jnp.int32).reshape(LATENTS * GRID * GRID)


def draw_b_ada(key, part):
    key = jax.random.fold_in(key, 23)
    base_key, sign_key, size_key = jax.random.split(key, 3)
    count = 6 * D
    section = jnp.arange(count) // D
    base = jnp.clip(0.5 * jax.random.normal(base_key, (count,), jnp.float32), -1.5, 1.5)
    magnitude = jax.random.uniform(size_key, (count,), jnp.float32, 2.0, 3.0)
    signs = jnp.where(jax.random.bernoulli(sign_key, 0.5, (count,)), 1.0, -1.0)
    return jnp.where(section == 5, signs * magnitude, base).astype(jnp.bfloat16)


def strengthened(values, stream_key, source, target, shards_of, factor):
    def block_of(axis_at):
        return (jnp.arange(values.shape[axis_at]) // (values.shape[axis_at] // shards_of)).reshape((-1,) + (1,) * (values.ndim - 1 - axis_at))

    near = jax.random.permutation(stream_key, shards_of)[block_of(target)]
    other_side = (block_of(target) + shards_of // 2) % shards_of
    return jnp.where((block_of(source) == near) | (block_of(source) == other_side), factor * values, values)


def shard_levels(key, extent, cuts, least, high):
    def one(dim, shards_of):
        steps = jax.random.uniform(jax.random.fold_in(jax.random.fold_in(key, 6), dim), (shards_of,), jnp.float32, least / len(cuts), high / len(cuts))
        return jnp.repeat(jnp.exp(steps), extent[dim] // shards_of).reshape((-1,) + (1,) * (len(extent) - dim - 1))

    factor_of = one(*cuts[0])
    for cut in cuts[1:]:
        factor_of = factor_of * one(*cut)
    return factor_of


def centred(rng, shape, scale, reach, cuts=(), dtype=jnp.bfloat16):
    gain = shard_levels(rng, shape, cuts, -0.22, 0.18) if cuts else 1.0
    drawn = jax.random.normal(rng, shape, jnp.float32) * scale * gain
    return jnp.minimum(jnp.maximum(drawn, -reach), reach).astype(dtype)


def heavy_noise(own_key, extent, spread, bound, cuts, heavy, dtype=jnp.bfloat16):
    values = spread * jax.random.normal(own_key, extent, jnp.float32)
    if cuts:
        values = values * shard_levels(own_key, extent, cuts, -0.22, 0.18)
    return jnp.clip(strengthened(values, jax.random.fold_in(own_key, 3), *heavy), -bound, bound).astype(dtype)


def setup_inputs(seed: int = 0) -> dict:
    splits = jax.random.split(jax.random.key(seed), 17)
    tokens = centred(splits[0], (TOKENS, D), 0.3, 1.796875, ((0, 8),))
    condition = centred(splits[1], (LATENTS, D), 1.0, 6.0, ((0, 8),))
    validity = draw_validity(jax.random.fold_in(splits[16], 71), 0)
    cotangent = heavy_noise(splits[3], (TOKENS, D), 1.0, 6.0, ((0, 8),), (0, 1, 8, 2.0))
    w_ada = centred(splits[4], (D, 6 * D), D ** -0.5, 0.21875)
    b_ada = draw_b_ada(jax.random.fold_in(splits[16], 71), 0)
    w_qkv = centred(splits[6], (3, D, D), D ** -0.5, 0.21875, ((2, 4),))
    b_qkv = centred(splits[7], (2, D), 0.5, 3.0, ((1, 4),))
    w_out = centred(splits[8], (D, D), (max(1, D // (GRID * GRID // 2))) ** -0.5, 6.0, ((0, 4),))
    b_out = centred(splits[9], (D,), 0.5, 3.0)
    w_up = centred(splits[10], (D, FF), D ** -0.5, 0.21875, ((1, 4),))
    b_up = centred(splits[11], (FF,), 0.5, 3.0, ((0, 4),))
    conv_w = centred(splits[12], (9, FF), 9 ** -0.5, 2.0, ((1, 4),))
    conv_b = centred(splits[13], (FF,), 0.5, 3.0, ((0, 4),))
    w_down = centred(splits[14], (FF, D), FF ** -0.5, 0.109375, ((0, 4),))
    b_down = centred(splits[15], (D,), 0.1, 0.59765625)
    return {"tokens": tokens, "condition": condition, "validity": validity, "cotangent": cotangent, "w_ada": w_ada, "b_ada": b_ada, "w_qkv": w_qkv, "b_qkv": b_qkv, "w_out": w_out, "b_out": b_out, "w_up": w_up, "b_up": b_up, "conv_w": conv_w, "conv_b": conv_b, "w_down": w_down, "b_down": b_down}


@jax.custom_vjp
def low(v):
    return lax.optimization_barrier(v.astype(jnp.bfloat16)).astype(jnp.float32)

@jax.custom_vjp
def low_back(v):
    return v

def low_keep(v):
    return (low(v), None)

def low_pass(kept, grad):
    return (grad,)

def back_keep(v):
    return (v, None)

def back_low(kept, grad):
    return (low(grad),)
low.defvjp(low_keep, low_pass)
low_back.defvjp(back_keep, back_low)
epsilon = 1e-06
neg_fill = -1000000000.0

def matmul(first_matrix, second_matrix):
    return jnp.dot(first_matrix, second_matrix, precision=lax.Precision.HIGHEST)

def both_round(values):
    return low(low_back(values))

def normalize(values):
    center = lax.optimization_barrier(jnp.mean(values, axis=-1, keepdims=True))
    centered = values - center
    return centered * lax.rsqrt(lax.optimization_barrier(jnp.mean(centered * centered, axis=-1, keepdims=True)) + epsilon)

def depthwise(hidden, conv_w, conv_b):
    padded = jnp.pad(hidden.reshape(GRID, GRID, -1), ((1, 1), (1, 1), (0, 0)))
    summed = conv_b
    for offset in range(9):
        summed = summed + conv_w[offset] * padded[offset // 3:offset // 3 + GRID, offset % 3:offset % 3 + GRID]
    return summed.reshape(GRID * GRID, -1)

def latent_block(params, inputs):
    w_ada, b_ada, w_qkv, b_qkv, w_out, b_out, w_up, b_up, conv_w, conv_b, w_down, b_down = params
    tokens, condition, validity = inputs
    length = GRID * GRID
    modulation = low_back(matmul(low(jax.nn.silu(condition))[None, :], w_ada)[0] + b_ada)
    shift_attn, scale_attn, gate_attn, shift_ffn, scale_ffn, gate_ffn = jnp.split(modulation, 6)
    normed = low(normalize(tokens) * (1.0 + scale_attn) + shift_attn)
    head_shape = (length, HEADS, HEAD_DIM)
    queries = both_round(matmul(normed, w_qkv[0]) + b_qkv[0]).reshape(head_shape)
    key_rows = both_round(matmul(normed, w_qkv[1])).reshape(head_shape)
    value_rows = both_round(matmul(normed, w_qkv[2]) + b_qkv[1]).reshape(head_shape)
    scores = jnp.einsum('qhd,khd->hqk', queries, key_rows, precision=lax.Precision.HIGHEST) * HEAD_DIM ** (-0.5)
    scores = low_back(scores)
    scores = jnp.where(validity[None, None, :] > 0.5, scores, neg_fill)
    weights = low(jax.nn.softmax(scores, axis=-1))
    attended = jnp.einsum('hqk,khd->qhd', weights, value_rows, precision=lax.Precision.HIGHEST)
    attended = both_round(attended.reshape(length, D))
    attn_out = low_back(matmul(attended, w_out) + b_out)
    middle = tokens + gate_attn * attn_out
    normed_ffn = low(normalize(middle) * (1.0 + scale_ffn) + shift_ffn)
    hidden = low_back(matmul(normed_ffn, w_up) + b_up) * validity[:, None]
    activated = low(jax.nn.gelu(depthwise(hidden, conv_w, conv_b), approximate=True))
    ffn_out = low_back(matmul(activated, w_down) + b_down)
    return middle + gate_ffn * ffn_out

def reference(tokens, condition, validity, cotangent, w_ada, b_ada, w_qkv, b_qkv, w_out, b_out, w_up, b_up, conv_w, conv_b, w_down, b_down):
    params = tuple((member.astype(jnp.float32) for member in (w_ada, b_ada, w_qkv, b_qkv, w_out, b_out, w_up, b_up, conv_w, conv_b, w_down, b_down)))
    token_rows = tokens.astype(jnp.float32).reshape(LATENTS, GRID * GRID, D)
    cond_rows = condition.astype(jnp.float32)
    valid_rows = validity.astype(jnp.float32).reshape(LATENTS, GRID * GRID)

    def forward(weights, token_rows, cond_rows):
        per_latent = jax.checkpoint(partial(latent_block, weights))
        return lax.map(per_latent, (token_rows, cond_rows, valid_rows))
    outputs, pullback = jax.vjp(forward, params, token_rows, cond_rows)
    seeded = cotangent.astype(jnp.float32).reshape(LATENTS, GRID * GRID, D) * valid_rows[:, :, None]
    grads, grad_tokens, grad_condition = pullback(seeded)
    return (outputs.reshape(TOKENS, D).astype(jnp.bfloat16), grad_tokens.reshape(TOKENS, D), grad_condition, grads[0], grads[1], grads[2], grads[3], grads[4], grads[5], grads[6], grads[7], grads[8], grads[9], grads[10], grads[11])
```

```python
import functools

import jax
import jax.numpy as jnp
from jax import lax
from jax.experimental import pallas as pl
from jax.experimental.pallas import tpu as pltpu
from jax.sharding import PartitionSpec as P

HEAD_DIM = 64
GRID = 32
LANES = 128
MIB = 2**20

bf16 = jnp.bfloat16
f32 = jnp.float32
epsilon = 1e-06
neg_fill = -1000000000.0

GELU_A = 0.7978845608
GELU_B = 0.044715


def dot(a, b):
    return jnp.dot(a, b, preferred_element_type=f32)


def dot_t(a, b):
    return lax.dot_general(a, b, (((1,), (1,)), ((), ())), preferred_element_type=f32)


def t_dot(a, b):
    return lax.dot_general(a, b, (((0,), (0,)), ((), ())), preferred_element_type=f32)


def norm(values):
    center = jnp.mean(values, axis=-1, keepdims=True)
    centered = values - center
    inv_std = lax.rsqrt(jnp.mean(centered * centered, axis=-1, keepdims=True) + epsilon)
    return centered * inv_std, inv_std


def norm_back(grad_plain, plain, inv_std):
    first_mean = jnp.mean(grad_plain, axis=-1, keepdims=True)
    second_mean = jnp.mean(grad_plain * plain, axis=-1, keepdims=True)
    return inv_std * (grad_plain - first_mean - plain * second_mean)


def wide_lanes(column, width):
    return jnp.concatenate([column] * (width // LANES), axis=1)


def of_head(values, head):
    lane = lax.broadcasted_iota(jnp.int32, values.shape, 1)
    inside = (lane >= head * HEAD_DIM) & (lane < (head + 1) * HEAD_DIM)
    return jnp.where(inside, values, jnp.zeros_like(values))


def cost(us):
    return pl.CostEstimate(flops=int(us * 1e9), bytes_accessed=0, transcendentals=0)


def params(limit=60):
    return pltpu.CompilerParams(vmem_limit_bytes=limit * MIB)


def sds(shape, dtype):
    return jax.ShapeDtypeStruct(shape, dtype)


def whole(shape):
    return pl.BlockSpec(shape, lambda i: tuple(0 for _ in shape), pipeline_mode=pl.Buffered(1))


def rows_of(i, size):
    return pl.ds(pl.multiple_of(i * size, size), size)


def attend(normed, w_ref, b_ref, bias_ref, q_ref, k_ref, v_ref, lse_ref, vm, finish):
    length = normed.shape[0]
    width = w_ref.shape[2]
    heads = width // HEAD_DIM
    block = min(256, length)
    scale = HEAD_DIM ** (-0.5)
    queries = (dot(normed, w_ref[0]) + b_ref[0:1, :].astype(f32)).astype(bf16)
    q_ref[...] = (queries.astype(f32) * scale).astype(bf16)
    k_ref[...] = dot(normed, w_ref[1]).astype(bf16)
    values = (dot(normed, w_ref[2]) + b_ref[1:2, :].astype(f32)).astype(bf16)
    v_ref[...] = values
    for head in range(heads):
        vm[head] = of_head(values, head)

    def body(i, carry):
        rows = rows_of(i, block)
        q = q_ref[rows, :]
        k = k_ref[...]
        total = jnp.zeros((block, width), f32)
        for head in range(heads):
            s = dot_t(of_head(q, head), k) + bias_ref[...]
            top = jnp.max(s, axis=1, keepdims=True)
            raised = jnp.exp(s - top)
            mass = jnp.sum(raised, axis=1, keepdims=True)
            out = dot(raised.astype(bf16), vm[head])
            total = total + out * (1.0 / mass)
            lse_ref[rows, head : head + 1] = top + jnp.log(mass)
        finish(rows, total)
        return carry

    lax.fori_loop(0, length // block, body, 0)


def attn_own_kernel(x_ref, mod_ref, w_ref, b_ref, bias_ref, normed_ref, q_ref, k_ref, v_ref, att_ref, lse_ref, vm):
    length = x_ref.shape[0]

    def prepare(i, carry):
        rows = rows_of(i, 128)
        plain, _ = norm(x_ref[rows, :].astype(f32))
        normed_ref[rows, :] = (plain * (1.0 + mod_ref[1:2, :]) + mod_ref[0:1, :]).astype(bf16)
        return carry

    lax.fori_loop(0, length // 128, prepare, 0)

    def finish(rows, total):
        att_ref[rows, :] = total.astype(bf16)

    attend(normed_ref[...], w_ref, b_ref, bias_ref, q_ref, k_ref, v_ref, lse_ref, vm, finish)


def attn_own(x, mod, w_qkv, b_qkv, bias):
    length, model = x.shape
    width = w_qkv.shape[2]
    return pl.pallas_call(
        attn_own_kernel,
        out_shape=[sds((length, model), bf16)] + [sds((length, width), bf16)] * 4 + [sds((length, 8), f32)],
        scratch_shapes=[pltpu.VMEM((width // HEAD_DIM, length, width), bf16)],
        compiler_params=params(),
        cost_estimate=cost(13),
        name="attn_own",
    )(x, mod, w_qkv, b_qkv, bias)


def attn_other_kernel(
    normed_ref, w_ref, b_ref, bias_ref, att_own_ref, wo_own_ref, wo_oth_ref, q_ref, k_ref, v_ref, att_ref, lse_ref, part_ref, vm
):
    def finish(rows, total):
        rounded = total.astype(bf16)
        att_ref[rows, :] = rounded
        part_ref[rows, :] = (dot(att_own_ref[rows, :], wo_own_ref[...]) + dot(rounded, wo_oth_ref[...])).astype(bf16)

    attend(normed_ref[...], w_ref, b_ref, bias_ref, q_ref, k_ref, v_ref, lse_ref, vm, finish)


def attn_other(normed, w_qkv, b_qkv, bias, att_own, wo_own, wo_oth):
    length, model = normed.shape
    width = w_qkv.shape[2]
    return pl.pallas_call(
        attn_other_kernel,
        out_shape=[sds((length, width), bf16)] * 4 + [sds((length, 8), f32), sds((length, model), bf16)],
        scratch_shapes=[pltpu.VMEM((width // HEAD_DIM, length, width), bf16)],
        compiler_params=params(),
        cost_estimate=cost(12),
        name="attn_other",
    )(normed, w_qkv, b_qkv, bias, att_own, wo_own, wo_oth)


def attn_back_kernel(has_prev, *refs):
    if has_prev:
        q_ref, k_ref, v_ref, do_ref, lse_ref, bias_ref, normed_ref, w_ref, prev_ref = refs[:9]
        gw_ref, gb_ref, dn_ref, dq, dk, dv = refs[9:]
    else:
        q_ref, k_ref, v_ref, do_ref, lse_ref, bias_ref, normed_ref, w_ref = refs[:8]
        gw_ref, gb_ref, dn_ref, dq, dk, dv = refs[8:]
    length, width = q_ref.shape
    heads = width // HEAD_DIM
    block = min(256, length)
    scale = HEAD_DIM ** (-0.5)
    dk[...] = jnp.zeros_like(dk)
    dv[...] = jnp.zeros_like(dv)

    def body(i, carry):
        rows = rows_of(i, block)
        q = q_ref[rows, :]
        grad = do_ref[rows, :]
        k = k_ref[...]
        v = v_ref[...]
        total = jnp.zeros((block, width), f32)
        for head in range(heads):
            qh = of_head(q, head)
            gh = of_head(grad, head)
            weights = jnp.exp(dot_t(qh, k) + bias_ref[...] - lse_ref[rows, head : head + 1])
            grad_weights = dot_t(gh, v)
            inner = jnp.sum(weights * grad_weights, axis=1, keepdims=True)
            grad_scores = (weights * (grad_weights - inner)).astype(bf16)
            dv[...] += t_dot(weights.astype(bf16), gh)
            dk[...] += t_dot(grad_scores, qh)
            total = total + dot(grad_scores, of_head(k, head))
        dq[rows, :] = (total * scale).astype(bf16)
        return carry

    lax.fori_loop(0, length // block, body, 0)
    normed = normed_ref[...]
    dk16 = dk[...].astype(bf16)
    dv16 = dv[...].astype(bf16)
    dq16 = dq[...]
    for part, grad in enumerate((dq16, dk16, dv16)):
        gw_ref[part] = t_dot(normed, grad).astype(bf16)
    gb_ref[...] = jnp.zeros_like(gb_ref)
    gb_ref[0:1, :] = jnp.sum(dq16.astype(f32), axis=0, keepdims=True)
    gb_ref[1:2, :] = jnp.sum(dv16.astype(f32), axis=0, keepdims=True)
    back = dot_t(dq16, w_ref[0]) + dot_t(dk16, w_ref[1]) + dot_t(dv16, w_ref[2])
    if has_prev:
        back = back + prev_ref[...].astype(f32)
    dn_ref[...] = back.astype(bf16)


def attn_back(q, k, v, grad, lse, bias, normed, w_qkv, prev=None):
    length, width = q.shape
    model = normed.shape[1]
    args = (q, k, v, grad, lse, bias, normed, w_qkv) + (() if prev is None else (prev,))
    return pl.pallas_call(
        functools.partial(attn_back_kernel, prev is not None),
        out_shape=[sds((3, model, width), bf16), sds((8, width), f32), sds((length, model), bf16)],
        scratch_shapes=[pltpu.VMEM((length, width), bf16), pltpu.VMEM((length, width), f32), pltpu.VMEM((length, width), f32)],
        compiler_params=params(),
        cost_estimate=cost(18),
        name="attn_back",
    )(*args)


def middle_kernel(x_ref, mine_ref, theirs_ref, cot_ref, val_ref, mod_ref, vec_ref, mid_ref, nf_ref, nft_ref, df_ref, dft_ref, gb_ref):
    model = x_ref.shape[1]
    attn_out = mine_ref[...].astype(f32) + theirs_ref[...].astype(f32) + vec_ref[0:1, :]
    middle = x_ref[...].astype(f32) + mod_ref[2:3, :] * attn_out
    mid_ref[...] = middle
    plain, _ = norm(middle)
    nf = (plain * (1.0 + mod_ref[4:5, :]) + mod_ref[3:4, :]).astype(bf16)
    nf_ref[...] = nf
    nft_ref[...] = nf.T
    grad_out = cot_ref[...].astype(f32) * wide_lanes(val_ref[...], model)
    df = (grad_out * mod_ref[5:6, :]).astype(bf16)
    df_ref[...] = df
    dft_ref[...] = df.T

    @pl.when(pl.program_id(0) == 0)
    def _():
        gb_ref[...] = jnp.zeros_like(gb_ref)

    gb_ref[0:1, :] += jnp.sum(df.astype(f32), axis=0, keepdims=True)


def row_spec(block, width):
    return pl.BlockSpec((block, width), lambda i: (i, 0))


def middle_stage(x, mine, theirs, cot, val, mod, vec):
    length, model = x.shape
    block = 256
    tall = row_spec(block, model)
    flat = pl.BlockSpec((model, block), lambda i: (0, i))
    return pl.pallas_call(
        middle_kernel,
        grid=(length // block,),
        in_specs=[tall, tall, tall, tall, row_spec(block, LANES), whole((8, model)), whole((8, model))],
        out_specs=[tall, tall, flat, tall, flat, whole((8, model))],
        out_shape=[
            sds((length, model), f32),
            sds((length, model), bf16),
            sds((model, length), bf16),
            sds((length, model), bf16),
            sds((model, length), bf16),
            sds((8, model), f32),
        ],
        compiler_params=params(),
        cost_estimate=cost(6),
        name="middle",
    )(x, mine, theirs, cot, val, mod, vec)


def middle_back_kernel(
    mid_ref, mine_ref, theirs_ref, pm_ref, pt_ref, cot_ref, val_ref, mod_ref, vec_ref, ao_ref, at_ref, wo_ref, wt_ref,
    dmid_ref, doo_ref, dot_ref, gwo_ref, gwt_ref, gs_ref, acc_o, acc_t,
):
    step = pl.program_id(0)
    model = mid_ref.shape[1]

    @pl.when(step == 0)
    def _():
        gs_ref[...] = jnp.zeros_like(gs_ref)
        acc_o[...] = jnp.zeros_like(acc_o)
        acc_t[...] = jnp.zeros_like(acc_t)

    grad_nf = mine_ref[...].astype(f32) + theirs_ref[...].astype(f32)
    plain, inv_std = norm(mid_ref[...])
    grad_out = cot_ref[...].astype(f32) * wide_lanes(val_ref[...], model)
    gs_ref[0:1, :] += jnp.sum(grad_nf, axis=0, keepdims=True)
    gs_ref[1:2, :] += jnp.sum(grad_nf * plain, axis=0, keepdims=True)
    d_middle = grad_out + norm_back(grad_nf * (1.0 + mod_ref[4:5, :]), plain, inv_std)
    dmid_ref[...] = d_middle
    attn_out = pm_ref[...].astype(f32) + pt_ref[...].astype(f32) + vec_ref[0:1, :]
    gs_ref[2:3, :] += jnp.sum(d_middle * attn_out, axis=0, keepdims=True)
    d_attn = (d_middle * mod_ref[2:3, :]).astype(bf16)
    gs_ref[3:4, :] += jnp.sum(d_attn.astype(f32), axis=0, keepdims=True)
    doo_ref[...] = dot_t(d_attn, wo_ref[...]).astype(bf16)
    dot_ref[...] = dot_t(d_attn, wt_ref[...]).astype(bf16)
    flipped = d_attn.T
    acc_o[...] += dot(flipped, ao_ref[...])
    acc_t[...] += dot(flipped, at_ref[...])

    @pl.when(step == pl.num_programs(0) - 1)
    def _():
        gwo_ref[...] = acc_o[...].astype(bf16)
        gwt_ref[...] = acc_t[...].astype(bf16)


def middle_back(mid, mine, theirs, part_mine, part_theirs, cot, val, mod, vec, att_own, att_oth, wo_own, wo_oth):
    length, model = mid.shape
    width = att_own.shape[1]
    block = 256
    tall = row_spec(block, model)
    slim = row_spec(block, width)
    return pl.pallas_call(
        middle_back_kernel,
        grid=(length // block,),
        in_specs=[tall] * 6
        + [row_spec(block, LANES), whole((8, model)), whole((8, model)), slim, slim, whole((width, model)), whole((width, model))],
        out_specs=[tall, slim, slim, whole((model, width)), whole((model, width)), whole((8, model))],
        out_shape=[
            sds((length, model), f32),
            sds((length, width), bf16),
            sds((length, width), bf16),
            sds((model, width), bf16),
            sds((model, width), bf16),
            sds((8, model), f32),
        ],
        scratch_shapes=[pltpu.VMEM((model, width), f32)] * 2,
        compiler_params=params(),
        cost_estimate=cost(8),
        name="middle_back",
    )(mid, mine, theirs, part_mine, part_theirs, cot, val, mod, vec, att_own, att_oth, wo_own, wo_oth)


def out_kernel(mid_ref, mine_ref, theirs_ref, cot_ref, val_ref, mod_ref, vec_ref, out_ref, gs_ref):
    model = mid_ref.shape[1]

    @pl.when(pl.program_id(0) == 0)
    def _():
        gs_ref[...] = jnp.zeros_like(gs_ref)

    ffn_out = mine_ref[...].astype(f32) + theirs_ref[...].astype(f32) + vec_ref[1:2, :]
    grad_out = cot_ref[...].astype(f32) * wide_lanes(val_ref[...], model)
    out_ref[...] = (mid_ref[...] + mod_ref[5:6, :] * ffn_out).astype(bf16)
    gs_ref[0:1, :] += jnp.sum(grad_out * ffn_out, axis=0, keepdims=True)


def out_stage(mid, mine, theirs, cot, val, mod, vec):
    length, model = mid.shape
    block = 256
    tall = row_spec(block, model)
    return pl.pallas_call(
        out_kernel,
        grid=(length // block,),
        in_specs=[tall] * 4 + [row_spec(block, LANES), whole((8, model)), whole((8, model))],
        out_specs=[tall, whole((8, model))],
        out_shape=[sds((length, model), bf16), sds((8, model), f32)],
        compiler_params=params(),
        cost_estimate=cost(4),
        name="block_out",
    )(mid, mine, theirs, cot, val, mod, vec)


def tokens_back_kernel(x_ref, dmid_ref, mine_ref, theirs_ref, mod_ref, out_ref, gs_ref):
    @pl.when(pl.program_id(0) == 0)
    def _():
        gs_ref[...] = jnp.zeros_like(gs_ref)

    grad_n = mine_ref[...].astype(f32) + theirs_ref[...].astype(f32)
    plain, inv_std = norm(x_ref[...].astype(f32))
    gs_ref[0:1, :] += jnp.sum(grad_n, axis=0, keepdims=True)
    gs_ref[1:2, :] += jnp.sum(grad_n * plain, axis=0, keepdims=True)
    out_ref[...] = (dmid_ref[...] + norm_back(grad_n * (1.0 + mod_ref[1:2, :]), plain, inv_std)).astype(bf16)


def tokens_back(x, dmid, mine, theirs, mod):
    length, model = x.shape
    block = 256
    tall = row_spec(block, model)
    return pl.pallas_call(
        tokens_back_kernel,
        grid=(length // block,),
        in_specs=[tall] * 4 + [whole((8, model))],
        out_specs=[tall, whole((8, model))],
        out_shape=[sds((length, model), bf16), sds((8, model), f32)],
        compiler_params=params(),
        cost_estimate=cost(4),
        name="tokens_back",
    )(x, dmid, mine, theirs, mod)


def ffn_kernel(has_prev, *refs):
    nf_ref, nft_ref, df_ref, dft_ref, val_ref, wup_ref, wdn_ref, taps_ref, small_ref = refs[:9]
    refs = refs[9:]
    if has_prev:
        prev_ffn_ref, prev_dnf_ref = refs[:2]
        refs = refs[2:]
    ffn_ref, dnf_ref, gw_ref, gs_ref, acc_ffn, acc_dnf, hs, ds, act, gact, dh = refs
    step = pl.program_id(0)
    length = nf_ref.shape[0]
    chans = wup_ref.shape[1]
    parts = chans // LANES
    zero = jnp.zeros((GRID, chans), f32)
    for j in range(3):
        for buf in (hs, ds):
            buf[j, 0:GRID, :] = zero
            buf[j, length + GRID : length + 2 * GRID, :] = zero
    wup = wup_ref[...]
    wdn = wdn_ref[...]
    column = lax.broadcasted_iota(jnp.int32, (GRID, LANES), 0)
    first = column == 0
    last = column == GRID - 1

    def put(dst, r, lanes, x):
        rows = pl.ds(pl.multiple_of((r + 1) * GRID, GRID), GRID)
        dst[1, rows, lanes] = x
        dst[0, rows, lanes] = jnp.where(first, 0.0, pltpu.roll(x, 1, 0))
        dst[2, rows, lanes] = jnp.where(last, 0.0, pltpu.roll(x, GRID - 1, 0))

    group = 8

    def before(i, carry):
        rows = rows_of(i, group * GRID)
        h = dot(nf_ref[rows, :], wup) + small_ref[0:1, :]
        gact[rows, :] = dot_t(df_ref[rows, :], wdn)
        for r in range(group):
            valid = val_ref[rows_of(i * group + r, GRID), :]
            for part in range(parts):
                lanes = slice(part * LANES, (part + 1) * LANES)
                put(hs, i * group + r, lanes, h[r * GRID : (r + 1) * GRID, lanes] * valid)
        return carry

    lax.fori_loop(0, length // (group * GRID), before, 0)
    gs_ref[...] = jnp.zeros_like(gs_ref)
    tile = (GRID // 8, 8, LANES)

    def hidden_row(r):
        rows = rows_of(r, GRID)
        for part in range(parts):
            lanes = slice(part * LANES, (part + 1) * LANES)
            total = jnp.zeros(tile, f32)
            for i in range(3):
                for j in range(3):
                    x = ds[2 - j, pl.ds(pl.multiple_of((r + 2 - i) * GRID, GRID), GRID), lanes].reshape(tile)
                    total = total + taps_ref[3 * i + j, :, lanes] * x
            total = total * val_ref[rows, :].reshape(tile)
            rounded = total.reshape(GRID, LANES).astype(bf16)
            dh[rows, lanes] = rounded
            gs_ref[10, :, lanes] += jnp.sum(rounded.astype(f32).reshape(tile), axis=0)

    def grid_row(r, carry):
        rows = rows_of(r, GRID)
        for part in range(parts):
            lanes = slice(part * LANES, (part + 1) * LANES)
            near = [
                [hs[j, pl.ds(pl.multiple_of((r + i) * GRID, GRID), GRID), lanes].reshape(tile) for j in range(3)]
                for i in range(3)
            ]
            conv = jnp.broadcast_to(small_ref[1:2, lanes].reshape(1, 1, LANES), tile)
            for i in range(3):
                for j in range(3):
                    conv = conv + taps_ref[3 * i + j, :, lanes] * near[i][j]
            square = conv * conv
            th = jnp.tanh(conv * (GELU_A + (GELU_A * GELU_B) * square))
            half = 0.5 * conv
            act[rows, lanes] = (half + half * th).reshape(GRID, LANES).astype(bf16)
            slope = 0.5 + 0.5 * th + half * (1.0 - th * th) * (GELU_A + (3 * GELU_A * GELU_B) * square)
            dc = gact[rows, lanes].reshape(tile) * slope
            for i in range(3):
                for j in range(3):
                    gs_ref[3 * i + j, :, lanes] += jnp.sum(dc * near[i][j], axis=0)
            gs_ref[9, :, lanes] += jnp.sum(dc, axis=0)
            put(ds, r, lanes, dc.reshape(GRID, LANES))

        @pl.when(r > 0)
        def _():
            hidden_row(r - 1)

        return carry

    lax.fori_loop(0, GRID, grid_row, 0)
    hidden_row(GRID - 1)
    gw_ref[0] = dot(nft_ref[...], dh[...]).astype(bf16)
    gw_ref[1] = dot(dft_ref[...], act[...]).astype(bf16)
    block = 256

    def after(i, carry):
        rows = rows_of(i, block)
        part_ffn = dot(act[rows, :], wdn)
        part_dnf = dot_t(dh[rows, :], wup)

        @pl.when(step == 0)
        def _():
            if has_prev:
                acc_ffn[rows, :] = part_ffn + prev_ffn_ref[rows, :].astype(f32)
                acc_dnf[rows, :] = part_dnf + prev_dnf_ref[rows, :].astype(f32)
            else:
                acc_ffn[rows, :] = part_ffn
                acc_dnf[rows, :] = part_dnf

        @pl.when((step > 0) & (step < pl.num_programs(0) - 1))
        def _():
            acc_ffn[rows, :] += part_ffn
            acc_dnf[rows, :] += part_dnf

        @pl.when(step == pl.num_programs(0) - 1)
        def _():
            ffn_ref[rows, :] = (acc_ffn[rows, :] + part_ffn).astype(bf16)
            dnf_ref[rows, :] = (acc_dnf[rows, :] + part_dnf).astype(bf16)

        return carry

    lax.fori_loop(0, length // block, after, 0)


def ffn(nf, nft, df, dft, val, wup, wdn, taps, small, prev=()):
    length, model = nf.shape
    hidden = wup.shape[1]
    chans = 256
    return pl.pallas_call(
        functools.partial(ffn_kernel, bool(prev)),
        grid=(hidden // chans,),
        in_specs=[
            whole((length, model)),
            whole((model, length)),
            whole((length, model)),
            whole((model, length)),
            whole((length, LANES)),
            pl.BlockSpec((model, chans), lambda i: (0, i)),
            pl.BlockSpec((chans, model), lambda i: (i, 0)),
            pl.BlockSpec((9, 8, chans), lambda i: (0, 0, i)),
            pl.BlockSpec((8, chans), lambda i: (0, i)),
        ]
        + [whole((length, model))] * len(prev),
        out_specs=[
            whole((length, model)),
            whole((length, model)),
            pl.BlockSpec((2, model, chans), lambda i: (0, 0, i)),
            pl.BlockSpec((11, 8, chans), lambda i: (0, 0, i)),
        ],
        out_shape=[
            sds((length, model), bf16),
            sds((length, model), bf16),
            sds((2, model, hidden), bf16),
            sds((11, 8, hidden), f32),
        ],
        scratch_shapes=[pltpu.VMEM((length, model), f32)] * 2
        + [pltpu.VMEM((3, length + 2 * GRID, chans), f32)] * 2
        + [pltpu.VMEM((length, chans), bf16), pltpu.VMEM((length, chans), f32), pltpu.VMEM((length, chans), bf16)],
        compiler_params=params(),
        cost_estimate=cost(30),
        name="ffn",
    )(nf, nft, df, dft, val, wup, wdn, taps, small, *prev)


def after(value, *others):
    return lax.optimization_barrier((value,) + others)[0]


def on_device(
    n_wide, tokens, condition, validity, cotangent, w_ada, b_ada, w_qkv, b_qkv, w_out, b_out, w_up, b_up, conv_w, conv_b, w_down, b_down
):
    latents = condition.shape[0]
    length = tokens.shape[0] // latents
    model = tokens.shape[1]
    width = w_out.shape[0]
    hidden = w_up.shape[1]
    place = lax.axis_index("narrow")
    me_y, me_core = place // 2, place % 2
    me_wide = lax.axis_index("wide")
    core_pairs = [(0, 1), (1, 0), (2, 3), (3, 2)]
    chip_pairs = [(0, 2), (2, 0), (1, 3), (3, 1)]
    bits = [1 << b for b in range(n_wide.bit_length() - 1)]

    def to_core(value):
        return lax.ppermute(value, "narrow", core_pairs)

    def to_chip(value):
        return lax.ppermute(value, "narrow", chip_pairs)

    def across(value, bit):
        return lax.ppermute(value, "wide", [(i, i ^ bit) for i in range(n_wide)])

    pad = jnp.zeros((1, hidden - 2 * width), bf16)
    vectors = jnp.concatenate(
        (b_up[None], conv_b[None], conv_w, jnp.concatenate((b_qkv.reshape(1, 2 * width), pad), axis=1), jnp.zeros((4, hidden), bf16)),
        axis=0,
    )
    vectors_oth = to_chip(vectors)
    w_qkv_oth = to_chip(w_qkv)
    w_out_oth = to_chip(after(w_out, w_qkv_oth))
    w_up_oth = to_chip(after(w_up, w_out_oth))
    w_down_oth = to_chip(after(w_down, w_up_oth))

    start = me_y * length
    x = lax.dynamic_slice(tokens, (start, 0), (length, model))
    cot = lax.dynamic_slice(cotangent, (start, 0), (length, model))
    valid = lax.dynamic_slice(validity, (start,), (length,)).astype(f32)
    cond = lax.dynamic_slice(condition, (me_y, 0), (1, model)).astype(f32)
    val = jnp.broadcast_to(valid[:, None], (length, LANES))
    bias = jnp.where(valid[None, :] > 0, 0.0, neg_fill)
    silu = jax.nn.silu(cond).astype(bf16)
    modulation = dot(silu, w_ada) + b_ada.astype(f32)
    mod = jnp.concatenate((modulation.reshape(6, model), jnp.zeros((2, model), f32)), axis=0)
    vec = jnp.concatenate((b_out[None].astype(f32), b_down[None].astype(f32), jnp.zeros((6, model), f32)), axis=0)

    silu_all = silu
    silu_all = jnp.concatenate((silu_all, to_chip(silu_all)), axis=0)
    for bit in bits:
        silu_all = jnp.concatenate((silu_all, across(silu_all, bit)), axis=0)

    normed, q_own, k_own, v_own, att_own, lse_own = attn_own(x, mod, w_qkv, b_qkv, bias)
    b_qkv_oth = vectors_oth[11, : 2 * width].reshape(2, width)
    q_oth, k_oth, v_oth, att_oth, lse_oth, part = attn_other(normed, w_qkv_oth, b_qkv_oth, bias, att_own, w_out, w_out_oth)
    part_core = to_core(part)
    mid, nf, nft, df, dft, g_down = middle_stage(x, part, part_core, cot, val, mod, vec)

    def spread(rows):
        small = jnp.concatenate((rows[:2].astype(f32), jnp.zeros((6, hidden), f32)), axis=0)
        taps = jnp.broadcast_to(rows[2:11].astype(f32)[:, None, :], (9, 8, hidden))
        return taps, small

    ffn_1, dnf_1, gw_own, gs_own = ffn(nf, nft, df, dft, val, w_up, w_down, *spread(vectors))
    ffn_2, dnf_2, gw_oth, gs_oth = ffn(nf, nft, df, dft, val, w_up_oth, w_down_oth, *spread(vectors_oth), prev=(ffn_1, dnf_1))
    dnf_core = to_core(dnf_2)
    ffn_core = to_core(after(ffn_2, dnf_core))

    def scatter(own, oth):
        lead = own.shape[:-2]
        at = len(lead)
        columns = own.shape[-1]
        share = model // n_wide
        total = (own.astype(f32) + to_chip(oth).astype(f32)).astype(bf16)
        left = n_wide
        for bit in bits:
            total = total.reshape(lead + (left // 2, 2, share, columns))
            mine = (me_wide // bit) % 2
            keep = lax.dynamic_index_in_dim(total, mine, at + 1, keepdims=False)
            send = lax.dynamic_index_in_dim(total, 1 - mine, at + 1, keepdims=False)
            total = keep.astype(f32) + across(send, bit).astype(f32)
            left //= 2
            if left > 1:
                total = total.astype(bf16)
        return total.reshape(lead + (share, columns))

    def sum_wide(value):
        for bit in bits:
            value = value + across(value, bit)
        return value

    gw_ffn = scatter(gw_own, gw_oth)
    d_mid, do_own, do_oth, gwo_own, gwo_oth, gs_mid = middle_back(
        mid, dnf_2, dnf_core, part, part_core, cot, val, mod, vec, att_own, att_oth, w_out, w_out_oth
    )
    block_out, gs_out = out_stage(mid, ffn_2, ffn_core, cot, val, mod, vec)
    gq_oth, gb_oth, dn_1 = attn_back(q_oth, k_oth, v_oth, do_oth, lse_oth, bias, normed, w_qkv_oth)
    gq_own, gb_own, dn_2 = attn_back(q_own, k_own, v_own, do_own, lse_own, bias, normed, w_qkv, prev=dn_1)
    dn_core = to_core(dn_2)
    grad_x, gs_x = tokens_back(x, d_mid, dn_2, dn_core, mod)

    def other_latent(value):
        half = length // 2
        sent = lax.dynamic_slice(value, (me_core * half, 0), (half, model))
        direct = to_chip(sent)
        round_about = to_core(direct)
        low = jnp.where(me_core == 0, direct, round_about)
        high = jnp.where(me_core == 0, round_about, direct)
        return jnp.concatenate((low, high), axis=0)

    def both(mine, theirs, dtype):
        upper = jnp.where(me_y == 0, mine, theirs).astype(dtype)
        lower = jnp.where(me_y == 0, theirs, mine).astype(dtype)
        return jnp.concatenate((upper, lower), axis=0)

    block_out_all = both(block_out, other_latent(block_out), bf16)
    grad_x_all = both(grad_x, other_latent(grad_x), f32)

    def joined(gq, gwo):
        return jnp.concatenate((gq[0], gq[1], gq[2], gwo), axis=1)

    gw_att = scatter(joined(gq_own, gwo_own), joined(gq_oth, gwo_oth))

    ffn_small_own = jnp.sum(gs_own, axis=1)
    ffn_small_oth = jnp.sum(gs_oth, axis=1)
    small_ffn = sum_wide(ffn_small_own + to_chip(ffn_small_oth))
    gb_own_row = gb_own[:2].reshape(1, 2 * width)
    gb_oth_row = gb_oth[:2].reshape(1, 2 * width)
    small_att = sum_wide(gb_own_row + to_chip(gb_oth_row))
    rows_two = jnp.concatenate((gs_mid[3:4], g_down[0:1]), axis=0)
    rows_two = sum_wide(rows_two + to_chip(rows_two))

    d_mod = jnp.concatenate((gs_x[0:2], gs_mid[2:3], gs_mid[0:2], gs_out[0:1]), axis=0).reshape(1, 6 * model).astype(bf16)
    d_mod_chip = to_chip(d_mod)
    d_mod_all = jnp.concatenate((d_mod, d_mod_chip), axis=0)
    d_mod_pair = both(d_mod, d_mod_chip, bf16)
    for bit in bits:
        d_mod_all = jnp.concatenate((d_mod_all, across(d_mod_all, bit)), axis=0)

    share = model // n_wide
    silu_part = lax.dynamic_slice(silu_all, (0, me_wide * share), (silu_all.shape[0], share))
    grad_w_ada = lax.dot_general(silu_part, d_mod_all, (((0,), (0,)), ((), ())), preferred_element_type=f32)
    share_ada = 6 * model // n_wide
    grad_b_ada = jnp.sum(
        lax.dynamic_slice(d_mod_all, (0, me_wide * share_ada), (d_mod_all.shape[0], share_ada)).astype(f32), axis=0
    )
    cond_both = condition.astype(f32)
    sig = jax.nn.sigmoid(cond_both)
    grad_condition = dot_t(d_mod_pair, w_ada) * sig * (1.0 + cond_both * (1.0 - sig))

    grad_w_qkv = gw_att[:, : 3 * width].reshape(share, 3, width).transpose(1, 0, 2)
    grad_w_out = gw_att[:, 3 * width :].T
    grad_w_up = gw_ffn[0]
    grad_w_down = gw_ffn[1].T
    grad_b_out = lax.dynamic_slice(rows_two[0], (me_wide * share,), (share,))
    grad_b_down = lax.dynamic_slice(rows_two[1], (me_wide * share,), (share,))
    return (
        block_out_all,
        grad_x_all,
        grad_condition,
        grad_w_ada,
        grad_b_ada,
        grad_w_qkv,
        small_att.reshape(2, width),
        grad_w_out,
        grad_b_out,
        grad_w_up,
        small_ffn[10],
        small_ffn[:9],
        small_ffn[9],
        grad_w_down,
        grad_b_down,
    )


def solution(mesh):
    n_wide = mesh.shape["wide"]
    return jax.shard_map(
        functools.partial(on_device, n_wide),
        mesh=mesh,
        in_specs=(
            P("wide", None),
            P("wide", None),
            P("wide"),
            P("wide", None),
            P(),
            P(),
            P(None, None, "narrow"),
            P(None, "narrow"),
            P("narrow", None),
            P(),
            P(None, "narrow"),
            P("narrow"),
            P(None, "narrow"),
            P("narrow"),
            P("narrow", None),
            P(),
        ),
        out_specs=(
            P("wide", None),
            P("wide", None),
            P("wide", None),
            P("wide", None),
            P("wide"),
            P(None, "wide", "narrow"),
            P(None, "narrow"),
            P("narrow", "wide"),
            P("wide"),
            P("wide", "narrow"),
            P("narrow"),
            P(None, "narrow"),
            P("narrow"),
            P("narrow", "wide"),
            P("wide"),
        ),
        check_vma=False,
    )
```

```python
import functools

import jax
import jax.numpy as jnp
from jax import lax
from jax.experimental import pallas as pl
from jax.experimental.pallas import tpu as pltpu
from jax.sharding import PartitionSpec as P

HEAD_DIM = 64
GRID = 32
LANES = 128
MIB = 2**20

MESH = pl.DeviceIdType.MESH

bf16 = jnp.bfloat16
f32 = jnp.float32
epsilon = 1e-06
neg_fill = -1000000000.0

GELU_A = 0.7978845608
GELU_B = 0.044715


def dot(a, b):
    return jnp.dot(a, b, preferred_element_type=f32)


def dot_t(a, b):
    return lax.dot_general(a, b, (((1,), (1,)), ((), ())), preferred_element_type=f32)


def t_dot(a, b):
    return lax.dot_general(a, b, (((0,), (0,)), ((), ())), preferred_element_type=f32)


def norm(values):
    center = jnp.mean(values, axis=-1, keepdims=True)
    centered = values - center
    inv_std = lax.rsqrt(jnp.mean(centered * centered, axis=-1, keepdims=True) + epsilon)
    return centered * inv_std, inv_std


def norm_back(grad_plain, plain, inv_std):
    first_mean = jnp.mean(grad_plain, axis=-1, keepdims=True)
    second_mean = jnp.mean(grad_plain * plain, axis=-1, keepdims=True)
    return inv_std * (grad_plain - first_mean - plain * second_mean)


def wide_lanes(column, width):
    return jnp.concatenate([column] * (width // LANES), axis=1)


def of_head(values, head):
    lane = lax.broadcasted_iota(jnp.int32, values.shape, 1)
    inside = (lane >= head * HEAD_DIM) & (lane < (head + 1) * HEAD_DIM)
    return jnp.where(inside, values, jnp.zeros_like(values))


def cost(us):
    return pl.CostEstimate(flops=int(us * 1e9), bytes_accessed=0, transcendentals=0)


def params(limit):
    return pltpu.CompilerParams(vmem_limit_bytes=limit * MIB)


def sds(shape, dtype):
    return jax.ShapeDtypeStruct(shape, dtype)


def whole(shape):
    return pl.BlockSpec(shape, lambda i, y: tuple(0 for _ in shape))


def row_spec(block, width):
    return pl.BlockSpec((block, width), lambda i, y: (i, 0))


def latent_spec(block, width, steps):
    return pl.BlockSpec((block, width), lambda i, y: (y[0] * steps + i, 0))


def call(kernel, name, steps, in_specs, out_specs, out_shape, scratch, limit, us):
    return pl.pallas_call(
        kernel,
        out_shape=out_shape,
        grid_spec=pltpu.PrefetchScalarGridSpec(
            num_scalar_prefetch=1, grid=(steps,), in_specs=in_specs, out_specs=out_specs, scratch_shapes=scratch
        ),
        compiler_params=params(limit),
        cost_estimate=cost(us),
        name=name,
    )


def rows_of(i, size):
    return pl.ds(pl.multiple_of(i * size, size), size)


def prepare_kernel(y_ref, cond_ref, wada_ref, bada_ref, valid_ref, bup_ref, convb_ref, convw_ref, bqkv_ref, wout_ref, mod_ref, silu_ref, pack_ref, val_ref, bias_ref):
    step = pl.program_id(0)
    cond = jnp.where(y_ref[0] == 0, cond_ref[0:1, :], cond_ref[1:2, :]).astype(f32)
    silu = (cond / (1.0 + jnp.exp(-cond))).astype(bf16)
    row = dot(jnp.broadcast_to(silu, (8, silu.shape[1])), wada_ref[...])[0:1, :]
    mod_ref[pl.ds(step, 1), :] = row + bada_ref[...].astype(f32)

    @pl.when(step == 0)
    def _():
        silu_ref[...] = silu
        hidden = bup_ref.shape[1]
        pad = jnp.zeros((1, hidden - 2 * bqkv_ref.shape[1]), f32)
        rows = [bup_ref[...].astype(f32), convb_ref[...].astype(f32), convw_ref[...].astype(f32)]
        rows += [jnp.concatenate((bqkv_ref[0:1, :].astype(f32), bqkv_ref[1:2, :].astype(f32), pad), axis=1)]
        rows += [jnp.zeros((4, hidden), f32)]
        pack_ref[0:16, :] = jnp.concatenate(rows, axis=0).astype(bf16)
        pack_ref[16:, :] = wout_ref[...]
        for j in range(val_ref.shape[0] // LANES):
            valid = valid_ref[j : j + 1, :].astype(f32)
            val_ref[j * LANES : (j + 1) * LANES, :] = jnp.broadcast_to(valid, (LANES, LANES)).T
            bias_ref[:, j * LANES : (j + 1) * LANES] = jnp.where(valid > 0, 0.0, neg_fill)


def prepare(y, condition, w_ada, b_ada, validity, b_up, conv_b, conv_w, b_qkv, w_out, length):
    model = condition.shape[1]
    hidden = b_up.shape[0]
    tall = length // LANES
    return call(
        prepare_kernel,
        "prepare",
        6,
        [
            whole(condition.shape),
            pl.BlockSpec((model, model), lambda i, y: (0, i)),
            pl.BlockSpec((1, model), lambda i, y: (0, i)),
            pl.BlockSpec((tall, LANES), lambda i, y: (y[0], 0)),
            whole((1, hidden)),
            whole((1, hidden)),
            whole(conv_w.shape),
            whole(b_qkv.shape),
            whole(w_out.shape),
        ],
        [whole((8, model)), whole((1, model)), whole((16 + w_out.shape[0], model)), whole((length, LANES)), whole((1, length))],
        [
            sds((8, model), f32),
            sds((1, model), bf16),
            sds((16 + w_out.shape[0], model), bf16),
            sds((length, LANES), f32),
            sds((1, length), f32),
        ],
        [],
        16,
        5,
    )(y, condition, w_ada, b_ada[None], validity.reshape(-1, LANES), b_up[None], conv_b[None], conv_w, b_qkv, w_out)


def attend(normed, w_ref, b_rows, bias_ref, q_ref, k_ref, v_ref, lse_ref, vm, finish):
    length = normed.shape[0]
    width = w_ref.shape[1]
    heads = width // HEAD_DIM
    block = min(256, length)
    scale = HEAD_DIM ** (-0.5)
    queries = (dot_t(normed, w_ref[0]) + b_rows[0]).astype(bf16)
    q_ref[...] = (queries.astype(f32) * scale).astype(bf16)
    k_ref[...] = dot_t(normed, w_ref[1]).astype(bf16)
    values = (dot_t(normed, w_ref[2]) + b_rows[1]).astype(bf16)
    v_ref[...] = values
    for head in range(heads):
        vm[head] = of_head(values, head)
    for start in range(0, length, block):
        rows = pl.ds(start, block)
        q = q_ref[rows, :]
        k = k_ref[...]
        total = jnp.zeros((block, width), f32)
        for head in range(heads):
            s = dot_t(of_head(q, head), k) + bias_ref[...]
            top = jnp.max(s, axis=1, keepdims=True)
            raised = jnp.exp(s - top)
            mass = jnp.sum(raised, axis=1, keepdims=True)
            out = dot(raised.astype(bf16), vm[head])
            total = total + out * (1.0 / mass)
            lse_ref[rows, head : head + 1] = top + jnp.log(mass)
        finish(rows, total)


def attn_own_kernel(y_ref, x_ref, mod_ref, w_ref, b_ref, bias_ref, normed_ref, q_ref, k_ref, v_ref, att_ref, lse_ref, vm):
    length = x_ref.shape[0]

    def normalize(i, carry):
        rows = rows_of(i, 256)
        plain, _ = norm(x_ref[rows, :].astype(f32))
        normed_ref[rows, :] = (plain * (1.0 + mod_ref[1:2, :]) + mod_ref[0:1, :]).astype(bf16)
        return carry

    lax.fori_loop(0, length // 256, normalize, 0)

    def finish(rows, total):
        att_ref[rows, :] = total.astype(bf16)

    b_rows = (b_ref[0:1, :].astype(f32), b_ref[1:2, :].astype(f32))
    attend(normed_ref[...], w_ref, b_rows, bias_ref, q_ref, k_ref, v_ref, lse_ref, vm, finish)


def attn_own(y, tokens, mod, w_qkv, b_qkv, bias):
    length = bias.shape[1]
    model = tokens.shape[1]
    width = w_qkv.shape[1]
    slim = whole((length, width))
    return call(
        attn_own_kernel,
        "attn_own",
        1,
        [latent_spec(length, model, 1), whole(mod.shape), whole(w_qkv.shape), whole(b_qkv.shape), whole(bias.shape)],
        [whole((length, model)), slim, slim, slim, slim, whole((length, 8))],
        [sds((length, model), bf16)] + [sds((length, width), bf16)] * 4 + [sds((length, 8), f32)],
        [pltpu.VMEM((width // HEAD_DIM, length, width), bf16)],
        32,
        11,
    )(y, tokens, mod, w_qkv, b_qkv, bias)


def attn_other_kernel(
    y_ref, normed_ref, w_ref, pack_ref, bias_ref, att_own_ref, wo_own_ref, q_ref, k_ref, v_ref, att_ref, lse_ref, part_ref, vm
):
    width = w_ref.shape[1]

    def finish(rows, total):
        rounded = total.astype(bf16)
        att_ref[rows, :] = rounded
        part_ref[rows, :] = (dot(att_own_ref[rows, :], wo_own_ref[...]) + dot(rounded, pack_ref[16:, :])).astype(bf16)

    row = pack_ref[11:12, :].astype(f32)
    b_rows = (row[:, :width], row[:, width : 2 * width])
    attend(normed_ref[...], w_ref, b_rows, bias_ref, q_ref, k_ref, v_ref, lse_ref, vm, finish)


def attn_other(y, normed, w_qkv, pack, bias, att_own, wo_own):
    length, model = normed.shape
    width = w_qkv.shape[1]
    slim = whole((length, width))
    return call(
        attn_other_kernel,
        "attn_other",
        1,
        [whole(normed.shape), whole(w_qkv.shape), whole(pack.shape), whole(bias.shape), slim, whole(wo_own.shape)],
        [slim, slim, slim, slim, whole((length, 8)), whole((length, model))],
        [sds((length, width), bf16)] * 4 + [sds((length, 8), f32), sds((length, model), bf16)],
        [pltpu.VMEM((width // HEAD_DIM, length, width), bf16)],
        32,
        11,
    )(y, normed, w_qkv, pack, bias, att_own, wo_own)


def attn_back_kernel(has_prev, *refs):
    y_ref, q_ref, k_ref, v_ref, do_ref, lse_ref, bias_ref, normed_ref, w_ref, gwo_ref = refs[:10]
    refs = refs[10:]
    if has_prev:
        prev_ref = refs[0]
        refs = refs[1:]
    gw_ref, gb_ref, dn_ref, dq, dk, dv, qm, gm, km = refs
    length, width = q_ref.shape
    heads = width // HEAD_DIM
    block = min(512, length)
    scale = HEAD_DIM ** (-0.5)
    dk[...] = jnp.zeros_like(dk)
    dv[...] = jnp.zeros_like(dv)
    for head in range(heads):
        qm[head] = of_head(q_ref[...], head)
        gm[head] = of_head(do_ref[...], head)
        km[head] = of_head(k_ref[...], head)

    def body(i, carry):
        rows = rows_of(i, block)
        k = k_ref[...]
        v = v_ref[...]
        total = jnp.zeros((block, width), f32)
        for head in range(heads):
            qh = qm[head, rows, :]
            gh = gm[head, rows, :]
            weights = jnp.exp(dot_t(qh, k) + bias_ref[...] - lse_ref[rows, head : head + 1])
            grad_weights = dot_t(gh, v)
            inner = jnp.sum(weights * grad_weights, axis=1, keepdims=True)
            grad_scores = (weights * (grad_weights - inner)).astype(bf16)
            dv[...] += t_dot(weights.astype(bf16), gh)
            dk[...] += t_dot(grad_scores, qh)
            total = total + dot(grad_scores, km[head])
        dq[rows, :] = (total * scale).astype(bf16)
        return carry

    lax.fori_loop(0, length // block, body, 0)
    normed = normed_ref[...]
    dk16 = dk[...].astype(bf16)
    dv16 = dv[...].astype(bf16)
    dq16 = dq[...]
    places, share, _ = gw_ref.shape
    for part, grad in enumerate((dq16, dk16, dv16)):
        gw_ref[:, :, part * width : (part + 1) * width] = t_dot(normed, grad).astype(bf16).reshape(places, share, width)
    gw_ref[:, :, 3 * width :] = gwo_ref[...].reshape(places, share, width)
    gb_ref[...] = jnp.zeros_like(gb_ref)
    gb_ref[0:1, :width] = jnp.sum(dq16.astype(f32), axis=0, keepdims=True)
    gb_ref[0:1, width : 2 * width] = jnp.sum(dv16.astype(f32), axis=0, keepdims=True)
    back = dot(dq16, w_ref[0]) + dot(dk16, w_ref[1]) + dot(dv16, w_ref[2])
    if has_prev:
        back = back + prev_ref[...].astype(f32)
    dn_ref[...] = back.astype(bf16)


def attn_back(y, places, q, k, v, grad, lse, bias, normed, w_qkv, gwo, prev=()):
    length, width = q.shape
    model = normed.shape[1]
    slim = whole((length, width))
    out_gw = (places, model // places, 4 * width)
    return call(
        functools.partial(attn_back_kernel, bool(prev)),
        "attn_back",
        1,
        [slim, slim, slim, slim, whole(lse.shape), whole(bias.shape), whole(normed.shape), whole(w_qkv.shape), whole(gwo.shape)]
        + [whole((length, model))] * len(prev),
        [whole(out_gw), whole((8, model)), whole((length, model))],
        [sds(out_gw, bf16), sds((8, model), f32), sds((length, model), bf16)],
        [pltpu.VMEM((length, width), bf16), pltpu.VMEM((length, width), f32), pltpu.VMEM((length, width), f32)]
        + [pltpu.VMEM((width // HEAD_DIM, length, width), bf16)] * 3,
        40,
        16,
    )(y, q, k, v, grad, lse, bias, normed, w_qkv, gwo, *prev)


def middle_kernel(y_ref, x_ref, mine_ref, theirs_ref, cot_ref, val_ref, mod_ref, vec_ref, mid_ref, nf_ref, df_ref, gb_ref):
    model = x_ref.shape[1]
    attn_out = mine_ref[...].astype(f32) + theirs_ref[...].astype(f32) + vec_ref[0:1, :]
    middle = x_ref[...].astype(f32) + mod_ref[2:3, :] * attn_out
    mid_ref[...] = middle
    plain, _ = norm(middle)
    nf_ref[...] = (plain * (1.0 + mod_ref[4:5, :]) + mod_ref[3:4, :]).astype(bf16)
    grad_out = cot_ref[...].astype(f32) * wide_lanes(val_ref[...], model)
    df = (grad_out * mod_ref[5:6, :]).astype(bf16)
    df_ref[...] = df

    @pl.when(pl.program_id(0) == 0)
    def _():
        gb_ref[...] = jnp.zeros_like(gb_ref)

    gb_ref[0:1, :] += jnp.sum(df.astype(f32), axis=0, keepdims=True)


def middle_stage(y, tokens, mine, theirs, cotangent, val, mod, vec):
    length, model = mine.shape
    block = 256
    steps = length // block
    tall = row_spec(block, model)
    part = latent_spec(block, model, steps)
    return call(
        middle_kernel,
        "middle",
        steps,
        [part, tall, tall, part, row_spec(block, LANES), whole((8, model)), whole((8, model))],
        [tall, tall, tall, whole((8, model))],
        [sds((length, model), f32), sds((length, model), bf16), sds((length, model), bf16), sds((8, model), f32)],
        [],
        16,
        5,
    )(y, tokens, mine, theirs, cotangent, val, mod, vec)


def middle_back_kernel(
    y_ref, mid_ref, mine_ref, theirs_ref, pm_ref, pt_ref, cot_ref, val_ref, mod_ref, vec_ref, ao_ref, at_ref, wo_ref, pack_ref,
    dmid_ref, doo_ref, dot_ref, gwo_ref, gwt_ref, gs_ref, acc_o, acc_t,
):
    step = pl.program_id(0)
    model = mid_ref.shape[1]

    @pl.when(step == 0)
    def _():
        gs_ref[...] = jnp.zeros_like(gs_ref)
        acc_o[...] = jnp.zeros_like(acc_o)
        acc_t[...] = jnp.zeros_like(acc_t)

    grad_nf = mine_ref[...].astype(f32) + theirs_ref[...].astype(f32)
    plain, inv_std = norm(mid_ref[...])
    grad_out = cot_ref[...].astype(f32) * wide_lanes(val_ref[...], model)
    gs_ref[0:1, :] += jnp.sum(grad_nf, axis=0, keepdims=True)
    gs_ref[1:2, :] += jnp.sum(grad_nf * plain, axis=0, keepdims=True)
    d_middle = grad_out + norm_back(grad_nf * (1.0 + mod_ref[4:5, :]), plain, inv_std)
    dmid_ref[...] = d_middle
    attn_out = pm_ref[...].astype(f32) + pt_ref[...].astype(f32) + vec_ref[0:1, :]
    gs_ref[2:3, :] += jnp.sum(d_middle * attn_out, axis=0, keepdims=True)
    d_attn = (d_middle * mod_ref[2:3, :]).astype(bf16)
    gs_ref[3:4, :] += jnp.sum(d_attn.astype(f32), axis=0, keepdims=True)
    doo_ref[...] = dot_t(d_attn, wo_ref[...]).astype(bf16)
    dot_ref[...] = dot_t(d_attn, pack_ref[16:, :]).astype(bf16)
    acc_o[...] += t_dot(d_attn, ao_ref[...])
    acc_t[...] += t_dot(d_attn, at_ref[...])

    @pl.when(step == pl.num_programs(0) - 1)
    def _():
        gwo_ref[...] = acc_o[...].astype(bf16)
        gwt_ref[...] = acc_t[...].astype(bf16)


def middle_back(y, mid, mine, theirs, part_mine, part_theirs, cotangent, val, mod, vec, att_own, att_oth, wo_own, pack):
    length, model = mid.shape
    width = att_own.shape[1]
    block = 256
    steps = length // block
    tall = row_spec(block, model)
    slim = row_spec(block, width)
    return call(
        middle_back_kernel,
        "middle_back",
        steps,
        [tall] * 5
        + [latent_spec(block, model, steps), row_spec(block, LANES), whole((8, model)), whole((8, model)), slim, slim]
        + [whole(wo_own.shape), whole(pack.shape)],
        [tall, slim, slim, whole((model, width)), whole((model, width)), whole((8, model))],
        [
            sds((length, model), f32),
            sds((length, width), bf16),
            sds((length, width), bf16),
            sds((model, width), bf16),
            sds((model, width), bf16),
            sds((8, model), f32),
        ],
        [pltpu.VMEM((model, width), f32)] * 2,
        24,
        8,
    )(y, mid, mine, theirs, part_mine, part_theirs, cotangent, val, mod, vec, att_own, att_oth, wo_own, pack)


def out_kernel(y_ref, mid_ref, mine_ref, theirs_ref, cot_ref, val_ref, mod_ref, vec_ref, out_ref, gs_ref):
    model = mid_ref.shape[1]

    @pl.when(pl.program_id(0) == 0)
    def _():
        gs_ref[...] = jnp.zeros_like(gs_ref)

    ffn_out = mine_ref[...].astype(f32) + theirs_ref[...].astype(f32) + vec_ref[1:2, :]
    grad_out = cot_ref[...].astype(f32) * wide_lanes(val_ref[...], model)
    out_ref[...] = (mid_ref[...] + mod_ref[5:6, :] * ffn_out).astype(bf16)
    gs_ref[0:1, :] += jnp.sum(grad_out * ffn_out, axis=0, keepdims=True)


def out_stage(y, mid, mine, theirs, cotangent, val, mod, vec):
    length, model = mid.shape
    block = 256
    steps = length // block
    tall = row_spec(block, model)
    return call(
        out_kernel,
        "block_out",
        steps,
        [tall] * 3 + [latent_spec(block, model, steps), row_spec(block, LANES), whole((8, model)), whole((8, model))],
        [tall, whole((8, model))],
        [sds((length, model), bf16), sds((8, model), f32)],
        [],
        16,
        4,
    )(y, mid, mine, theirs, cotangent, val, mod, vec)


def tokens_back_kernel(y_ref, x_ref, dmid_ref, mine_ref, theirs_ref, mod_ref, out_ref, gs_ref):
    @pl.when(pl.program_id(0) == 0)
    def _():
        gs_ref[...] = jnp.zeros_like(gs_ref)

    grad_n = mine_ref[...].astype(f32) + theirs_ref[...].astype(f32)
    plain, inv_std = norm(x_ref[...].astype(f32))
    gs_ref[0:1, :] += jnp.sum(grad_n, axis=0, keepdims=True)
    gs_ref[1:2, :] += jnp.sum(grad_n * plain, axis=0, keepdims=True)
    out_ref[...] = (dmid_ref[...] + norm_back(grad_n * (1.0 + mod_ref[1:2, :]), plain, inv_std)).astype(bf16)


def tokens_back(y, tokens, dmid, mine, theirs, mod):
    length, model = dmid.shape
    block = 256
    steps = length // block
    tall = row_spec(block, model)
    return call(
        tokens_back_kernel,
        "tokens_back",
        steps,
        [latent_spec(block, model, steps)] + [tall] * 3 + [whole((8, model))],
        [tall, whole((8, model))],
        [sds((length, model), bf16), sds((8, model), f32)],
        [],
        16,
        4,
    )(y, tokens, dmid, mine, theirs, mod)


def ffn_kernel(has_prev, *refs):
    nf_ref, df_ref, val_ref, wup_ref, wdn_ref, pack_ref = refs[:6]
    refs = refs[6:]
    if has_prev:
        prev_ffn_ref, prev_dnf_ref = refs[:2]
        refs = refs[2:]
    if has_prev:
        ffn_ref, dnf_ref, gw_ref, gs_ref, got_dnf, got_ffn, taps, sums, center, hs, ds, act, gact, dh, sent, came = refs
        place = lax.axis_index("narrow")
        partner = {"narrow": place + 1 - 2 * lax.rem(place, 2)}
        barrier = pltpu.get_barrier_semaphore()
        pl.semaphore_signal(barrier, inc=1, device_id=partner, device_id_type=MESH)
    else:
        ffn_ref, dnf_ref, gw_ref, gs_ref, taps, sums, center, hs, ds, act, gact, dh = refs
    length = nf_ref.shape[0]
    chans = wup_ref.shape[1]
    tile = (GRID // 8, 8, LANES)
    zero = jnp.zeros((GRID, LANES), f32)
    for buf in (hs, ds):
        for j in range(3):
            buf[j, 0:GRID, :] = zero
            buf[j, length + GRID : length + 2 * GRID, :] = zero
    for t in range(11):
        taps[t] = jnp.broadcast_to(pack_ref[t : t + 1, :].astype(f32), (8, chans))
    sums[...] = jnp.zeros_like(sums)
    center[...] = dot(nf_ref[...], wup_ref[...])
    gact[...] = dot_t(df_ref[...], wdn_ref[...])
    column = lax.broadcasted_iota(jnp.int32, (GRID, LANES), 0)
    first = column == 0
    last = column == GRID - 1

    def put(dst, r, x):
        rows = pl.ds(pl.multiple_of((r + 1) * GRID, GRID), GRID)
        dst[1, rows, :] = x
        dst[0, rows, :] = jnp.where(first, 0.0, pltpu.roll(x, 1, 0))
        dst[2, rows, :] = jnp.where(last, 0.0, pltpu.roll(x, GRID - 1, 0))

    def near_row(buf, j, r):
        return buf[j, pl.ds(pl.multiple_of((r + 1) * GRID, GRID), GRID), :].reshape(tile)

    def channel_part(part, carry):
        lanes = pl.ds(pl.multiple_of(part * LANES, LANES), LANES)

        def spread(r):
            rows = rows_of(r, GRID)
            h = (center[rows, lanes].reshape(tile) + taps[0, :, lanes]).reshape(GRID, LANES)
            put(hs, r, h * val_ref[rows, :])

        def conv_row(r):
            rows = rows_of(r, GRID)
            near = [[near_row(hs, j, r + i - 1) for j in range(3)] for i in range(3)]
            conv = jnp.broadcast_to(taps[1, :, lanes], tile)
            for i in range(3):
                for j in range(3):
                    conv = conv + taps[2 + 3 * i + j, :, lanes] * near[i][j]
            square = conv * conv
            th = jnp.tanh(conv * (GELU_A + (GELU_A * GELU_B) * square))
            half = 0.5 * conv
            act[rows, lanes] = (half + half * th).reshape(GRID, LANES).astype(bf16)
            slope = 0.5 + 0.5 * th + half * (1.0 - th * th) * (GELU_A + (3 * GELU_A * GELU_B) * square)
            dc = gact[rows, lanes].reshape(tile) * slope
            for i in range(3):
                for j in range(3):
                    sums[3 * i + j, :, lanes] += jnp.sum(dc * near[i][j], axis=0)
            sums[9, :, lanes] += jnp.sum(dc, axis=0)
            put(ds, r, dc.reshape(GRID, LANES))

        def hidden_row(r):
            rows = rows_of(r, GRID)
            total = jnp.zeros(tile, f32)
            for i in range(3):
                for j in range(3):
                    total = total + taps[2 + 3 * i + j, :, lanes] * near_row(ds, 2 - j, r + 1 - i)
            total = total * val_ref[rows, :].reshape(tile)
            rounded = total.reshape(GRID, LANES).astype(bf16)
            dh[rows, lanes] = rounded
            sums[10, :, lanes] += jnp.sum(rounded.astype(f32).reshape(tile), axis=0)

        unroll = 4

        def loop(fun):
            def some(i, c):
                for u in range(unroll):
                    fun(i * unroll + u)
                return c

            lax.fori_loop(0, GRID // unroll, some, 0)

        loop(spread)
        loop(conv_row)
        loop(hidden_row)
        return carry

    lax.fori_loop(0, chans // LANES, channel_part, 0)
    for t in range(11):
        gs_ref[t : t + 1, :] = jnp.sum(sums[t], axis=0, keepdims=True)
    gs_ref[11:16, :] = jnp.zeros((5, chans), f32)
    places, _, share, _ = gw_ref.shape
    part_dnf = dot_t(dh[...], wup_ref[...])
    part_ffn = dot(act[...], wdn_ref[...])
    if has_prev:
        part_dnf = part_dnf + prev_dnf_ref[...].astype(f32)
        part_ffn = part_ffn + prev_ffn_ref[...].astype(f32)
    dnf_ref[...] = part_dnf.astype(bf16)
    ffn_ref[...] = part_ffn.astype(bf16)
    if has_prev:
        pl.semaphore_wait(barrier, 1)
        copies = [
            pltpu.make_async_remote_copy(src, dst, sent.at[k], came.at[k], device_id=partner, device_id_type=MESH)
            for k, (src, dst) in enumerate(((dnf_ref, got_dnf), (ffn_ref, got_ffn)))
        ]
        for copy in copies:
            copy.start()
    gw_ref[:, 0] = t_dot(nf_ref[...], dh[...]).astype(bf16).reshape(places, share, chans)
    gw_ref[:, 1] = t_dot(df_ref[...], act[...]).astype(bf16).reshape(places, share, chans)
    if has_prev:
        for copy in copies:
            copy.wait()


def ffn(places, nf, df, val, wup, wdn, pack, prev=()):
    length, model = nf.shape
    chans = wup.shape[1]
    out_gw = (places, 2, model // places, chans)
    tall = sds((length, model), bf16)
    vmem = pl.BlockSpec(memory_space=pltpu.VMEM)
    remote = dict(collective_id=1, has_side_effects=True) if prev else {}
    return pl.pallas_call(
        functools.partial(ffn_kernel, bool(prev)),
        in_specs=[vmem] * (6 + len(prev)),
        out_specs=[vmem] * 4 + [pl.BlockSpec(memory_space=pl.ANY)] * len(prev),
        out_shape=[tall, tall, sds(out_gw, bf16), sds((16, chans), f32)] + [tall] * len(prev),
        scratch_shapes=[pltpu.VMEM((11, 8, chans), f32)] * 2
        + [pltpu.VMEM((length, chans), f32)]
        + [pltpu.VMEM((3, length + 2 * GRID, LANES), f32)] * 2
        + [pltpu.VMEM((length, chans), bf16), pltpu.VMEM((length, chans), f32), pltpu.VMEM((length, chans), bf16)]
        + [pltpu.SemaphoreType.DMA((2,))] * len(prev),
        compiler_params=pltpu.CompilerParams(vmem_limit_bytes=44 * MIB, **remote),
        cost_estimate=cost(24),
        name="ffn",
    )(nf, df, val, wup, wdn, pack, *prev)


def ada_back_kernel(y_ref, rows_ref, silu_ref, pair_ref, wada_ref, cond_ref, gw_ref, gb_ref, gc_ref):
    step = pl.program_id(0)
    rows = rows_ref[0]
    gw_ref[...] = t_dot(silu_ref[...], rows)
    gb_ref[pl.ds(step, 1), :] = jnp.sum(rows.astype(f32), axis=0, keepdims=True)
    part = dot_t(pair_ref[0], wada_ref[...])

    @pl.when(step == 0)
    def _():
        gc_ref[...] = part

    @pl.when(step > 0)
    def _():
        gc_ref[...] += part

    @pl.when(step == pl.num_programs(0) - 1)
    def _():
        cond = cond_ref[...].astype(f32)
        sig = 1.0 / (1.0 + jnp.exp(-cond))
        gc_ref[...] = gc_ref[...] * (sig * (1.0 + cond * (1.0 - sig)))


def ada_back(y, rows, silu, pair, w_ada, condition):
    sections, latents, model = rows.shape
    share = silu.shape[1]
    pairs = condition.shape[0]
    return call(
        ada_back_kernel,
        "ada_back",
        6,
        [
            pl.BlockSpec((1, latents, model), lambda i, y: (i, 0, 0)),
            whole(silu.shape),
            pl.BlockSpec((1, pairs, model), lambda i, y: (i, 0, 0)),
            pl.BlockSpec((model, model), lambda i, y: (0, i)),
            whole(condition.shape),
        ],
        [pl.BlockSpec((share, model), lambda i, y: (0, i)), whole((8, model)), whole((pairs, model))],
        [sds((share, 6 * model), f32), sds((8, model), f32), sds((pairs, model), f32)],
        [],
        16,
        4,
    )(y, rows, silu, pair, w_ada, condition)


def after(value, *others):
    return lax.optimization_barrier((value,) + others)[0]


def on_device(
    n_wide, tokens, condition, validity, cotangent, w_ada, b_ada, w_qkv, b_qkv, w_out, b_out, w_up, b_up, conv_w, conv_b, w_down, b_down
):
    latents = condition.shape[0]
    length = tokens.shape[0] // latents
    model = tokens.shape[1]
    width = w_out.shape[0]
    place = lax.axis_index("narrow")
    me_y, me_core = place // 2, place % 2
    me_wide = lax.axis_index("wide")
    y = me_y.astype(jnp.int32).reshape(1)
    share = model // n_wide
    core_pairs = [(0, 1), (1, 0), (2, 3), (3, 2)]
    chip_pairs = [(0, 2), (2, 0), (1, 3), (3, 1)]
    bits = [1 << b for b in range(n_wide.bit_length() - 1)]

    def to_core(value):
        return lax.ppermute(value, "narrow", core_pairs)

    def to_chip(value):
        return lax.ppermute(value, "narrow", chip_pairs)

    def across(value, bit):
        return lax.ppermute(value, "wide", [(i, i ^ bit) for i in range(n_wide)])

    w_qkv = w_qkv.transpose(0, 2, 1)
    w_qkv_oth = to_chip(w_qkv)
    mod, silu, pack, val, bias = prepare(y, condition, w_ada, b_ada, validity, b_up, conv_b, conv_w, b_qkv, w_out, length)
    pack_oth = to_chip(pack)
    normed, q_own, k_own, v_own, att_own, lse_own = attn_own(y, tokens, mod, w_qkv, b_qkv, bias)
    w_up_oth = to_chip(after(w_up, att_own))
    w_down_oth = to_chip(after(w_down, att_own))
    vec = jnp.concatenate((b_out[None].astype(f32), b_down[None].astype(f32), jnp.zeros((6, model), f32)), axis=0)
    q_oth, k_oth, v_oth, att_oth, lse_oth, part = attn_other(y, normed, w_qkv_oth, pack_oth, bias, att_own, w_out)
    part_core = to_core(part)
    mid, nf, df, g_down = middle_stage(y, tokens, part, part_core, cotangent, val, mod, vec)

    def swap_wide(value):
        return lax.all_to_all(value, "wide", 0, 0)

    def total(value):
        return jnp.sum(value.astype(f32), axis=0)

    ffn_1, dnf_1, gw_own, gs_own = ffn(n_wide, nf, df, val, w_up, w_down, pack)
    got_own = swap_wide(gw_own)
    ffn_2, dnf_2, gw_oth, gs_oth, dnf_core, ffn_core = ffn(
        n_wide, nf, df, val, w_up_oth, w_down_oth, pack_oth, prev=(ffn_1, dnf_1)
    )
    d_mid, do_own, do_oth, gwo_own, gwo_oth, gs_mid = middle_back(
        y, mid, dnf_2, dnf_core, part, part_core, cotangent, val, mod, vec, att_own, att_oth, w_out, pack_oth
    )
    block_out, gs_out = out_stage(y, mid, ffn_2, ffn_core, cotangent, val, mod, vec)
    half = length // 2

    def my_half(value):
        return lax.dynamic_slice(value, (me_core * half, 0), (half, model))

    out_direct = to_chip(my_half(block_out))
    got_oth = swap_wide(after(gw_oth, got_own, out_direct))

    do_oth = after(do_oth, block_out)
    gw_att_oth, gb_oth, dn_1 = attn_back(y, n_wide, q_oth, k_oth, v_oth, do_oth, lse_oth, bias, normed, w_qkv_oth, gwo_oth)
    att_from_chip = to_chip(gw_att_oth)
    out_direct, sum_own, dn_1 = lax.optimization_barrier((out_direct, total(got_own), dn_1))
    out_around = to_core(out_direct)
    gw_att_own, gb_own, dn_2 = attn_back(
        y, n_wide, q_own, k_own, v_own, do_own, lse_own, bias, normed, w_qkv, gwo_own, prev=(dn_1,)
    )
    dn_core = to_core(dn_2)

    def both(mine, theirs, dtype):
        upper = jnp.where(me_y == 0, mine, theirs).astype(dtype)
        lower = jnp.where(me_y == 0, theirs, mine).astype(dtype)
        return jnp.concatenate((upper, lower), axis=0)

    def joined(direct, around):
        low = jnp.where(me_core == 0, direct, around)
        high = jnp.where(me_core == 0, around, direct)
        return jnp.concatenate((low, high), axis=0)

    grad_x, gs_x = tokens_back(y, tokens, d_mid, dn_2, dn_core, mod)
    x_direct = to_chip(my_half(grad_x))

    att = (gw_att_own.astype(f32) + att_from_chip.astype(f32)).astype(bf16)
    left = n_wide
    for bit in bits:
        att = att.reshape(left // 2, 2, share, 4 * width)
        mine = (me_wide // bit) % 2
        keep = lax.dynamic_index_in_dim(att, mine, 1, keepdims=False)
        send = lax.dynamic_index_in_dim(att, 1 - mine, 1, keepdims=False)
        att = keep.astype(f32) + across(send, bit).astype(f32)
        left //= 2
        if left > 1:
            att = att.astype(bf16)
    att = att.reshape(share, 4 * width)

    pad = jnp.zeros((2, model), f32)
    shared_rows = jnp.concatenate((gs_mid[3:4], g_down[0:1]), axis=0)
    sums_own = jnp.concatenate((gs_own[:11], gb_own[0:1], shared_rows, pad), axis=0)
    sums_oth = jnp.concatenate((gs_oth[:11], gb_oth[0:1], shared_rows, pad), axis=0)
    sums = sums_own + to_chip(sums_oth)
    rows = jnp.concatenate(
        (gs_x[0:2].astype(bf16), gs_mid[2:3].astype(bf16), gs_mid[0:2].astype(bf16), gs_out[0:1].astype(bf16), silu, jnp.zeros((1, model), bf16)),
        axis=0,
    )[None]
    rows_chip = to_chip(rows)
    pair = both(rows, rows_chip, bf16)
    rows = jnp.concatenate((rows, rows_chip), axis=0)
    for bit in bits:
        sums = sums + across(sums, bit)
        rows = jnp.concatenate((rows, across(rows, bit)), axis=0)
    silu_part = lax.dynamic_slice(rows[:, 6], (0, me_wide * share), (rows.shape[0], share))
    grad_w_ada, b_ada_rows, grad_condition = ada_back(
        y, rows.transpose(1, 0, 2), silu_part, pair.transpose(1, 0, 2), w_ada, condition
    )
    share_ada = 6 * model // n_wide
    grad_b_ada = lax.dynamic_slice(b_ada_rows[:6].reshape(-1), (me_wide * share_ada,), (share_ada,))

    sum_oth = total(got_oth).astype(bf16)
    ffn_grads = sum_own + to_chip(sum_oth).astype(f32)
    block_out_all = both(block_out, joined(out_direct, out_around), bf16)
    x_around = to_core(x_direct)
    grad_x_all = both(grad_x, joined(x_direct, x_around), f32)
    grad_w_qkv = att[:, : 3 * width].reshape(share, 3, width).transpose(1, 0, 2)
    return (
        block_out_all,
        grad_x_all,
        grad_condition,
        grad_w_ada,
        grad_b_ada,
        grad_w_qkv,
        sums[11, : 2 * width].reshape(2, width),
        att[:, 3 * width :].T,
        lax.dynamic_slice(sums[12], (me_wide * share,), (share,)),
        ffn_grads[0],
        sums[10],
        sums[:9],
        sums[9],
        ffn_grads[1].T,
        lax.dynamic_slice(sums[13], (me_wide * share,), (share,)),
    )


def solution(mesh):
    n_wide = mesh.shape["wide"]
    return jax.shard_map(
        functools.partial(on_device, n_wide),
        mesh=mesh,
        in_specs=(
            P("wide", None),
            P("wide", None),
            P("wide"),
            P("wide", None),
            P(),
            P(),
            P(None, None, "narrow"),
            P(None, "narrow"),
            P("narrow", None),
            P(),
            P(None, "narrow"),
            P("narrow"),
            P(None, "narrow"),
            P("narrow"),
            P("narrow", None),
            P(),
        ),
        out_specs=(
            P("wide", None),
            P("wide", None),
            P("wide", None),
            P("wide", None),
            P("wide"),
            P(None, "wide", "narrow"),
            P(None, "narrow"),
            P("narrow", "wide"),
            P("wide"),
            P("wide", "narrow"),
            P("narrow"),
            P(None, "narrow"),
            P("narrow"),
            P("narrow", "wide"),
            P("wide"),
        ),
        check_vma=False,
    )
```

```python
import functools

import jax
import jax.numpy as jnp
from jax import lax
from jax.experimental import pallas as pl
from jax.experimental.pallas import tpu as pltpu
from jax.sharding import PartitionSpec as P

HEAD_DIM = 64
GRID = 32
LANES = 128
MIB = 2**20

MESH = pl.DeviceIdType.MESH

bf16 = jnp.bfloat16
f32 = jnp.float32
epsilon = 1e-06
neg_fill = -1000000000.0

GELU_A = 0.7978845608
GELU_B = 0.044715


def dot(a, b):
    return jnp.dot(a, b, preferred_element_type=f32)


def dot_t(a, b):
    return lax.dot_general(a, b, (((1,), (1,)), ((), ())), preferred_element_type=f32)


def t_dot(a, b):
    return lax.dot_general(a, b, (((0,), (0,)), ((), ())), preferred_element_type=f32)


def norm(values):
    center = jnp.mean(values, axis=-1, keepdims=True)
    centered = values - center
    inv_std = lax.rsqrt(jnp.mean(centered * centered, axis=-1, keepdims=True) + epsilon)
    return centered * inv_std, inv_std


def norm_back(grad_plain, plain, inv_std):
    first_mean = jnp.mean(grad_plain, axis=-1, keepdims=True)
    second_mean = jnp.mean(grad_plain * plain, axis=-1, keepdims=True)
    return inv_std * (grad_plain - first_mean - plain * second_mean)


def wide_lanes(column, width):
    return jnp.concatenate([column] * (width // LANES), axis=1)


def of_head(values, head):
    lane = lax.broadcasted_iota(jnp.int32, values.shape, 1)
    inside = (lane >= head * HEAD_DIM) & (lane < (head + 1) * HEAD_DIM)
    return jnp.where(inside, values, jnp.zeros_like(values))


def cost(us):
    return pl.CostEstimate(flops=int(us * 1e9), bytes_accessed=0, transcendentals=0)


def params(limit):
    return pltpu.CompilerParams(vmem_limit_bytes=limit * MIB)


def sds(shape, dtype):
    return jax.ShapeDtypeStruct(shape, dtype)


def rows_of(i, size):
    return pl.ds(pl.multiple_of(i * size, size), size)


def flip(index, bit):
    return index + bit - 2 * bit * lax.rem(lax.div(index, bit), 2)


class Copies:
    def __init__(self, local_sems, send_sems, recv_sems):
        self.local_sems, self.send_sems, self.recv_sems = local_sems, send_sems, recv_sems
        self.locals, self.remotes = 0, 0
        self.pending = []

    def local(self, src, dst):
        copy = pltpu.make_async_copy(src, dst, self.local_sems.at[self.locals])
        self.locals += 1
        copy.start()
        return copy

    def save(self, src, dst):
        self.pending.append(self.local(src, dst).wait)

    def later(self, src, dst, device):
        k = self.remotes
        self.remotes += 1
        copy = pltpu.make_async_remote_copy(
            src, dst, self.send_sems.at[k], self.recv_sems.at[k], device_id=device, device_id_type=MESH
        )
        self.pending.append(copy.wait_send)
        return copy

    def settle(self, copy):
        self.pending.remove(copy.wait_send)
        copy.wait()

    def remote(self, src, dst, device):
        copy = self.later(src, dst, device)
        copy.start()
        return copy

    def finish(self):
        assert self.locals <= self.local_sems.shape[0] and self.remotes <= self.send_sems.shape[0]
        for wait in self.pending:
            wait()


def project(normed, w_ref, b_rows, q_ref, k_ref, v_ref):
    scale = HEAD_DIM ** (-0.5)
    queries = (dot_t(normed, w_ref[0]) + b_rows[0]).astype(bf16)
    q_ref[...] = (queries.astype(f32) * scale).astype(bf16)
    k_ref[...] = dot_t(normed, w_ref[1]).astype(bf16)
    v_ref[...] = (dot_t(normed, w_ref[2]) + b_rows[1]).astype(bf16)


def attend(bias_ref, q_ref, k_ref, v_ref, lse_ref, vm, finish):
    length, width = q_ref.shape
    heads = width // HEAD_DIM
    block = min(256, length)
    for head in range(heads):
        vm[head] = of_head(v_ref[...], head)
    for index in range(length // block):
        rows = pl.ds(index * block, block)
        q = q_ref[rows, :]
        k = k_ref[...]
        total = jnp.zeros((block, width), f32)
        for head in range(heads):
            s = dot_t(of_head(q, head), k) + bias_ref[...]
            top = jnp.max(s, axis=1, keepdims=True)
            raised = jnp.exp(s - top)
            mass = jnp.sum(raised, axis=1, keepdims=True)
            out = dot(raised.astype(bf16), vm[head])
            total = total + out * (1.0 / mass)
            lse_ref[rows, head : head + 1] = top + jnp.log(mass)
        finish(index, rows, total)


def ffn_half(nf, df, val_ref, wup_ref, wdn_ref, pack_ref, sums_ref, gw_ref, dnf_acc, ffn_acc, first_half, scratch, share_out, events=()):
    taps, sums, center, hs, ds, act, gact, dh = scratch
    length = nf.shape[0]
    chans = wup_ref.shape[1]
    tile = (GRID // 8, 8, LANES)
    zero = jnp.zeros((GRID, LANES), f32)
    for buf in (hs, ds):
        for j in range(3):
            buf[j, 0:GRID, :] = zero
            buf[j, length + GRID : length + 2 * GRID, :] = zero
    for t in range(11):
        taps[t] = jnp.broadcast_to(pack_ref[t : t + 1, :].astype(f32), (8, chans))
    sums[...] = jnp.zeros_like(sums)
    center[...] = dot(nf[...], wup_ref[...])
    gact[...] = dot_t(df[...], wdn_ref[...])
    column = lax.broadcasted_iota(jnp.int32, (GRID, LANES), 0)
    first = column == 0
    last = column == GRID - 1

    def put(dst, r, x):
        rows = pl.ds(pl.multiple_of((r + 1) * GRID, GRID), GRID)
        dst[1, rows, :] = x
        dst[0, rows, :] = jnp.where(first, 0.0, pltpu.roll(x, 1, 0))
        dst[2, rows, :] = jnp.where(last, 0.0, pltpu.roll(x, GRID - 1, 0))

    def near_row(buf, j, r):
        return buf[j, pl.ds(pl.multiple_of((r + 1) * GRID, GRID), GRID), :].reshape(tile)

    def channel_part(part, carry):
        for at, event in events:
            pl.when(part == at)(event)
        lanes = pl.ds(pl.multiple_of(part * LANES, LANES), LANES)

        def spread(r):
            rows = rows_of(r, GRID)
            h = (center[rows, lanes].reshape(tile) + taps[0, :, lanes]).reshape(GRID, LANES)
            put(hs, r, h * val_ref[rows, :])

        def conv_row(r):
            rows = rows_of(r, GRID)
            near = [[near_row(hs, j, r + i - 1) for j in range(3)] for i in range(3)]
            conv = jnp.broadcast_to(taps[1, :, lanes], tile)
            for i in range(3):
                for j in range(3):
                    conv = conv + taps[2 + 3 * i + j, :, lanes] * near[i][j]
            square = conv * conv
            th = jnp.tanh(conv * (GELU_A + (GELU_A * GELU_B) * square))
            half = 0.5 * conv
            act[rows, lanes] = (half + half * th).reshape(GRID, LANES).astype(bf16)
            slope = 0.5 + 0.5 * th + half * (1.0 - th * th) * (GELU_A + (3 * GELU_A * GELU_B) * square)
            dc = gact[rows, lanes].reshape(tile) * slope
            for i in range(3):
                for j in range(3):
                    sums[3 * i + j, :, lanes] += jnp.sum(dc * near[i][j], axis=0)
            sums[9, :, lanes] += jnp.sum(dc, axis=0)
            put(ds, r, dc.reshape(GRID, LANES))

        def hidden_row(r):
            rows = rows_of(r, GRID)
            total = jnp.zeros(tile, f32)
            for i in range(3):
                for j in range(3):
                    total = total + taps[2 + 3 * i + j, :, lanes] * near_row(ds, 2 - j, r + 1 - i)
            total = total * val_ref[rows, :].reshape(tile)
            rounded = total.reshape(GRID, LANES).astype(bf16)
            dh[rows, lanes] = rounded
            sums[10, :, lanes] += jnp.sum(rounded.astype(f32).reshape(tile), axis=0)

        unroll = 4

        def loop(fun):
            def some(i, c):
                for u in range(unroll):
                    fun(i * unroll + u)
                return c

            lax.fori_loop(0, GRID // unroll, some, 0)

        loop(spread)
        loop(conv_row)
        loop(hidden_row)
        return carry

    lax.fori_loop(0, chans // LANES, channel_part, 0)
    for t in range(11):
        sums_ref[t : t + 1, :] = jnp.sum(sums[t], axis=0, keepdims=True)
    sums_ref[11:16, :] = jnp.zeros((5, chans), f32)
    part_dnf = dot_t(dh[...], wup_ref[...])
    if not first_half:
        part_dnf = part_dnf + dnf_acc[...].astype(f32)
    dnf_acc[...] = part_dnf.astype(bf16)
    share_out(0)
    part_ffn = dot(act[...], wdn_ref[...])
    if not first_half:
        part_ffn = part_ffn + ffn_acc[...].astype(f32)
    ffn_acc[...] = part_ffn.astype(bf16)
    share_out(1)
    high = gw_ref.shape[0]
    share = gw_ref.shape[4]
    gw_ref[:, :, :, 0] = t_dot(nf[...], dh[...]).astype(bf16).reshape(high, 2, 2, share, chans)
    gw_ref[:, :, :, 1] = t_dot(df[...], act[...]).astype(bf16).reshape(high, 2, 2, share, chans)


FRONT_ANY_IN = 7
FRONT_VMEM_IN = 9
FRONT_ANY_OUT = 24
FRONT_VMEM_OUT = 7


def front_kernel(*refs):
    refs = list(refs)

    def take(count):
        head = refs[:count]
        del refs[:count]
        return head

    tokens, cotangent, w_ada, w_qkv, w_out, w_up, w_down = take(FRONT_ANY_IN)
    cond_ref, valid_ref, bada_ref, bqkv_ref, bout_ref, bup_ref, convw_ref, convb_ref, bdown_ref = take(FRONT_VMEM_IN)
    (
        o_normed, o_q1, o_k1, o_v1, o_a1, o_l1, o_q2, o_k2, o_v2, o_a2, o_l2, o_wqkv, o_pack, o_wout, o_part, o_theirs,
        o_dnf, o_dnf_theirs, o_ffn, o_ffn_theirs, o_gw, o_up1, o_dn1, o_val,
    ) = take(FRONT_ANY_OUT)
    mod_ref, silu_ref, bias_ref, sums1_ref, sums2_ref, gdown_ref, vec_ref = take(FRONT_VMEM_OUT)
    x, cot, normed, q1, k1, v1, a1, l1, q2, k2, v2, a2, l2, vm, val = take(15)
    wada_buf, wq1, wo1, wu1, wd1, wq2, wo2, wu2, wd2, pack1, pack2 = take(11)
    part, theirs, nf, df, dnf, ffn, gw1, gw2, got_up, got_dn = take(10)
    ffn_scratch = take(8)
    local_sems, send_sems, recv_sems = take(3)
    assert not refs

    length, model = x.shape
    width = wo1.shape[0]
    place = lax.axis_index("narrow")
    wide = lax.axis_index("wide")
    chip = lax.div(place, 2)
    x_bit = lax.rem(wide, 2)
    z_bit = lax.rem(lax.div(wide, 2), 2)
    core_dev = {"narrow": flip(place, 1)}
    chip_dev = {"narrow": flip(place, 2)}
    x_dev = {"wide": flip(wide, 1)}
    z_dev = {"wide": flip(wide, 2)}
    barrier = pltpu.get_barrier_semaphore()
    for device in (core_dev, chip_dev, x_dev, z_dev):
        pl.semaphore_signal(barrier, inc=1, device_id=device, device_id_type=MESH)
    copies = Copies(local_sems, send_sems, recv_sems)
    mine = pl.ds(pl.multiple_of(chip * length, length), length)
    ada = [
        copies.local(w_ada.at[:, pl.ds(i * model, model)], wada_buf.at[i]) for i in range(2)
    ]
    load_x = copies.local(tokens.at[mine, :], x)
    load_wq1 = copies.local(w_qkv, wq1)
    ada += [copies.local(w_ada.at[:, pl.ds(i * model, model)], wada_buf.at[i]) for i in range(2, 6)]
    load_cot = copies.local(cotangent.at[mine, :], cot)
    load_wo1 = copies.local(w_out, wo1)
    load_wu1 = copies.local(w_up, wu1)
    load_wd1 = copies.local(w_down, wd1)

    pad = jnp.zeros((1, model - 2 * width), f32)
    b_row = jnp.concatenate((bqkv_ref[0:1, :].astype(f32), bqkv_ref[1:2, :].astype(f32), pad), axis=1)
    pack1[...] = jnp.concatenate(
        (
            bup_ref[...].astype(f32).reshape(1, model),
            convb_ref[...].astype(f32).reshape(1, model),
            convw_ref[...].astype(f32),
            b_row,
            jnp.zeros((4, model), f32),
        ),
        axis=0,
    ).astype(bf16)
    vec_ref[...] = jnp.concatenate(
        (bout_ref[...].astype(f32).reshape(1, model), bdown_ref[...].astype(f32).reshape(1, model), jnp.zeros((6, model), f32)),
        axis=0,
    )
    pl.semaphore_wait(barrier, 4)

    def half_rows(size, piece):
        return pl.ds(pl.multiple_of(x_bit * (size // 2) + piece * (size // 4), size // 4), size // 4)

    def qkv_piece(ref, piece):
        return ref.at[piece, pl.ds(pl.multiple_of(x_bit * (width // 2), width // 2), width // 2), :]

    def ffn_piece(ref, piece):
        return ref.at[half_rows(model, piece), :]

    def down_piece(ref, piece):
        size = model // 8
        return ref.at[pl.ds(pl.multiple_of(x_bit * (model // 2) + piece * size, size), size), :]

    qkv_in = [copies.remote(qkv_piece(w_qkv, p), qkv_piece(wq2, p), chip_dev) for p in range(3)]
    pack_in = copies.remote(pack1, pack2, chip_dev)
    out_in = copies.remote(w_out, wo2, chip_dev)
    up_in = [copies.remote(ffn_piece(w_up, p), ffn_piece(wu2, p), chip_dev) for p in range(2)]
    down_in = [copies.remote(down_piece(w_down, p), down_piece(wd2, p), chip_dev) for p in range(4)]

    def pass_on(arrived, ref, piece, p):
        arrived.wait_recv()
        return copies.remote(piece(ref, p), piece(ref, p), x_dev)

    cond = jnp.where(chip == 0, cond_ref[0:1, :].astype(f32), cond_ref[1:2, :].astype(f32))
    silu = (cond / (1.0 + jnp.exp(-cond))).astype(bf16)
    silu_ref[...] = jnp.broadcast_to(silu, silu_ref.shape)
    tall = length // LANES
    for j in range(tall):
        valid = jnp.where(chip == 0, valid_ref[j : j + 1, :], valid_ref[tall + j : tall + j + 1, :]).astype(f32)
        val[j * LANES : (j + 1) * LANES, :] = jnp.broadcast_to(valid, (LANES, LANES)).T
        bias_ref[:, j * LANES : (j + 1) * LANES] = jnp.where(valid > 0, 0.0, neg_fill)
    copies.save(val, o_val)
    mod_ref[6:8, :] = jnp.zeros((2, model), f32)
    silu8 = silu_ref[...]
    for i in range(6):
        ada[i].wait()
        row = dot(silu8, wada_buf[i])[0:1, :]
        mod_ref[i : i + 1, :] = row + bada_ref[i * model : (i + 1) * model].astype(f32).reshape(1, model)

    load_x.wait()

    def normalize(i, carry):
        rows = rows_of(i, 256)
        plain, _ = norm(x[rows, :].astype(f32))
        normed[rows, :] = (plain * (1.0 + mod_ref[1:2, :]) + mod_ref[0:1, :]).astype(bf16)
        return carry

    lax.fori_loop(0, length // 256, normalize, 0)
    copies.save(normed, o_normed)
    load_wq1.wait()
    project(normed[...], wq1, (pack1[11:12, :width].astype(f32), b_row[:, width : 2 * width]), q1, k1, v1)
    for src, dst in ((q1, o_q1), (k1, o_k1), (v1, o_v1)):
        copies.save(src, dst)
    passed = {}

    def finish_own(index, rows, total):
        a1[rows, :] = total.astype(bf16)
        if index < 3:
            passed["qkv%d" % index] = pass_on(qkv_in[index], wq2, qkv_piece, index)

    attend(bias_ref, q1, k1, v1, l1, vm, finish_own)
    copies.save(a1, o_a1)
    copies.save(l1, o_l1)

    load_wo1.wait()
    pack_in.wait_recv()
    for p in range(3):
        passed["qkv%d" % p].wait_recv()
    row = pack2[11:12, :].astype(f32)
    project(normed[...], wq2, (row[:, :width], row[:, width : 2 * width]), q2, k2, v2)
    for src, dst in ((q2, o_q2), (k2, o_k2), (v2, o_v2), (wq2, o_wqkv), (pack2, o_pack)):
        copies.save(src, dst)
    part_in = []

    def finish_other(index, rows, total):
        if index == 0:
            out_in.wait_recv()
        rounded = total.astype(bf16)
        a2[rows, :] = rounded
        part[rows, :] = (dot(a1[rows, :], wo1[...]) + dot(rounded, wo2[...])).astype(bf16)
        part_in.append(copies.remote(part.at[rows, :], theirs.at[rows, :], core_dev))
        if index == 2:
            passed["up0"] = pass_on(up_in[0], wu2, ffn_piece, 0)

    attend(bias_ref, q2, k2, v2, l2, vm, finish_other)
    for src, dst in ((a2, o_a2), (l2, o_l2), (wo2, o_wout), (part, o_part)):
        copies.save(src, dst)

    load_cot.wait()
    block = 256
    gdown_ref[...] = jnp.zeros_like(gdown_ref)
    for index in range(length // block):
        rows = pl.ds(index * block, block)
        part_in[index].wait_recv()
        attn_out = part[rows, :].astype(f32) + theirs[rows, :].astype(f32) + vec_ref[0:1, :]
        middle = x[rows, :].astype(f32) + mod_ref[2:3, :] * attn_out
        plain, _ = norm(middle)
        nf[rows, :] = (plain * (1.0 + mod_ref[4:5, :]) + mod_ref[3:4, :]).astype(bf16)
        grad_out = cot[rows, :].astype(f32) * wide_lanes(val[rows, :], model)
        rounded = (grad_out * mod_ref[5:6, :]).astype(bf16)
        df[rows, :] = rounded
        gdown_ref[0:1, :] += jnp.sum(rounded.astype(f32), axis=0, keepdims=True)
    copies.save(theirs, o_theirs)

    passed["up1"] = pass_on(up_in[1], wu2, ffn_piece, 1)
    load_wu1.wait()
    load_wd1.wait()

    def pass_down(p):
        copy = copies.later(down_piece(wd2, p), down_piece(wd2, p), x_dev)
        passed["down%d" % p] = copy

        def event():
            down_in[p].wait_recv()
            copy.start()

        return event

    downs = [pass_down(p) for p in range(4)]
    ffn_half(
        nf, df, val, wu1, wd1, pack1, sums1_ref, gw1, dnf, ffn, True, ffn_scratch, lambda i: downs[2 + i](),
        events=((2, downs[0]), (4, downs[1])),
    )
    up_got = copies.remote(gw1.at[:, :, 1 - x_bit, 0], got_up, x_dev)
    down_got = copies.remote(gw1.at[:, 1 - z_bit, :, 1], got_dn, z_dev)

    for name in ("up0", "up1", "down0", "down1", "down2", "down3"):
        passed[name].wait_recv()
    arriving = []

    def exchange(i):
        src, saved, landing = ((dnf, o_dnf, o_dnf_theirs), (ffn, o_ffn, o_ffn_theirs))[i]
        arriving.append(copies.remote(src, landing, core_dev))
        copies.save(src, saved)

    ffn_half(nf, df, val, wu2, wd2, pack2, sums2_ref, gw2, dnf, ffn, False, ffn_scratch, exchange)
    copies.save(gw2, o_gw)
    up_got.wait_recv()
    got_up[...] = (gw1[:, :, x_bit, 0].astype(f32) + got_up[...].astype(f32)).astype(bf16)
    copies.save(got_up, o_up1)
    down_got.wait_recv()
    got_dn[...] = (gw1[:, z_bit, :, 1].astype(f32) + got_dn[...].astype(f32)).astype(bf16)
    copies.save(got_dn, o_dn1)
    for copy in arriving:
        copy.wait_recv()
    copies.finish()


def front(n_wide, tokens, condition, validity, cotangent, w_ada, b_ada, w_qkv, b_qkv, w_out, b_out, w_up, b_up, conv_w, conv_b, w_down, b_down):
    latents = condition.shape[0]
    length = tokens.shape[0] // latents
    model = tokens.shape[1]
    width = w_out.shape[0]
    chans = w_up.shape[1]
    share = model // n_wide
    high = n_wide // 4
    heads = width // HEAD_DIM
    tall = ((length, model), bf16)
    slim = ((length, width), bf16)
    lse = ((length, 8), f32)
    wq = (w_qkv.shape, bf16)
    pack = ((16, chans), bf16)
    wo = (w_out.shape, bf16)
    wf = (w_up.shape, bf16)
    gw = ((high, 2, 2, 2, share, chans), bf16)
    gw_half = ((high, 2, share, chans), bf16)
    val = ((length, LANES), f32)
    outs = [tall] + [slim] * 4 + [lse] + [slim] * 4 + [lse, wq, pack, wo] + [tall] * 6 + [gw, gw_half, gw_half, val]
    small_outs = [
        ((8, model), f32),
        ((8, model), bf16),
        ((1, length), f32),
        ((16, chans), f32),
        ((16, chans), f32),
        ((8, model), f32),
        ((8, model), f32),
    ]
    scratch = [tall] * 3 + [slim] * 4 + [lse] + [slim] * 4 + [lse, ((heads, length, width), bf16), val]
    scratch += [((6, model, model), bf16), wq, wo, wf, wf, wq, wo, wf, wf, pack, pack]
    scratch += [tall] * 6 + [gw, gw, gw_half, gw_half]
    scratch += [((11, 8, chans), f32)] * 2 + [((length, chans), f32)]
    scratch += [((3, length + 2 * GRID, LANES), f32)] * 2 + [((length, chans), bf16), ((length, chans), f32), ((length, chans), bf16)]
    any_spec = pl.BlockSpec(memory_space=pl.ANY)
    vmem = pl.BlockSpec(memory_space=pltpu.VMEM)
    assert len(outs) == FRONT_ANY_OUT and len(small_outs) == FRONT_VMEM_OUT
    return pl.pallas_call(
        front_kernel,
        in_specs=[any_spec] * FRONT_ANY_IN + [vmem] * FRONT_VMEM_IN,
        out_specs=[any_spec] * FRONT_ANY_OUT + [vmem] * FRONT_VMEM_OUT,
        out_shape=[sds(*o) for o in outs + small_outs],
        scratch_shapes=[pltpu.VMEM(*s) for s in scratch]
        + [pltpu.SemaphoreType.DMA((48,)), pltpu.SemaphoreType.DMA((32,)), pltpu.SemaphoreType.DMA((32,))],
        compiler_params=pltpu.CompilerParams(vmem_limit_bytes=62 * MIB, collective_id=1, has_side_effects=True),
        cost_estimate=cost(60),
        name="front",
    )(
        tokens, cotangent, w_ada, w_qkv, w_out, w_up, w_down,
        condition, validity.reshape(-1, LANES), b_ada, b_qkv, b_out, b_up, conv_w, conv_b, b_down,
    )


BACK_ANY_IN = 27
BACK_VMEM_IN = 7
BACK_ANY_OUT = 2
BACK_VMEM_OUT = 4


def attend_back(bias_ref, q_ref, k_ref, v_ref, grad_ref, lse_ref, masked, dq, dk, dv, between):
    qm, gm, km = masked
    length, width = q_ref.shape
    heads = width // HEAD_DIM
    block = min(512, length)
    scale = HEAD_DIM ** (-0.5)
    dk[...] = jnp.zeros_like(dk)
    dv[...] = jnp.zeros_like(dv)
    for head in range(heads):
        qm[head] = of_head(q_ref[...], head)
        gm[head] = of_head(grad_ref[...], head)
        km[head] = of_head(k_ref[...], head)
    for index in range(length // block):
        rows = pl.ds(index * block, block)
        k = k_ref[...]
        v = v_ref[...]
        total = jnp.zeros((block, width), f32)
        for head in range(heads):
            qh = qm[head, rows, :]
            gh = gm[head, rows, :]
            weights = jnp.exp(dot_t(qh, k) + bias_ref[...] - lse_ref[rows, head : head + 1])
            grad_weights = dot_t(gh, v)
            inner = jnp.sum(weights * grad_weights, axis=1, keepdims=True)
            grad_scores = (weights * (grad_weights - inner)).astype(bf16)
            dv[...] += t_dot(weights.astype(bf16), gh)
            dk[...] += t_dot(grad_scores, qh)
            total = total + dot(grad_scores, km[head])
        dq[rows, :] = (total * scale).astype(bf16)
        between(index)


def added(a, b):
    return (a.astype(f32) + b.astype(f32)).astype(bf16)


def back_kernel(n_wide, *refs):
    refs = list(refs)

    def take(count):
        head = refs[:count]
        del refs[:count]
        return head

    h_in = take(BACK_ANY_IN)
    (
        tokens, cotangent, h_dnf, h_dnf_t, h_ffn, h_ffn_t, h_part, h_theirs, h_normed, h_q1, h_k1, h_v1, h_a1, h_l1,
        h_q2, h_k2, h_v2, h_a2, h_l2, h_wq1, h_wq2, h_wo1, h_wo2, h_gw, h_up1, h_dn1, h_val,
    ) = h_in
    mod_ref, bias_ref, vec_ref, sums1_ref, sums2_ref, gdown_ref, silu_ref = take(BACK_VMEM_IN)
    out_all, grad_all = take(BACK_ANY_OUT)
    gffn_ref, gatt_ref, small_ref, rows_ref = take(BACK_VMEM_OUT)
    x, cot, dnf, dnf_t, ffn, ffn_t, part, theirs, normed, q1, k1, v1, a1, l1, q2, k2, v2, a2, l2, wq1, wq2, wo1, wo2, val = take(24)
    keep_up, keep_dn, got_up, got_dn, up, dn, got_up2, got_dn2, fw, got_fw, fw3, got_y = take(12)
    d_mid, d_attn, do1, do2, qm, gm, km, dq, dk, dv = take(10)
    att1, att2, got_att1, got_att2, got_att_y, at1, at2, got_z, atz, got_last, at_last = take(11)
    dn_t, sums, got_sums, gs = take(4)
    local_sems, send_sems, recv_sems = take(3)
    assert not refs

    length, model = x.shape
    width = wo1.shape[0]
    high = up.shape[1]
    share = up.shape[3]
    place = lax.axis_index("narrow")
    wide = lax.axis_index("wide")
    chip = lax.div(place, 2)
    core = lax.rem(place, 2)
    bits = [1 << b for b in range(n_wide.bit_length() - 1)]
    bit_of = {bit: lax.rem(lax.div(wide, bit), 2) for bit in bits}
    wide_dev = {bit: {"wide": flip(wide, bit)} for bit in bits}
    x_bit, z_bit = bit_of[1], bit_of[2]
    core_dev = {"narrow": flip(place, 1)}
    chip_dev = {"narrow": flip(place, 2)}
    barrier = pltpu.get_barrier_semaphore()
    for device in [core_dev, chip_dev] + [wide_dev[bit] for bit in bits]:
        pl.semaphore_signal(barrier, inc=1, device_id=device, device_id_type=MESH)
    copies = Copies(local_sems, send_sems, recv_sems)
    mine = pl.ds(pl.multiple_of(chip * length, length), length)
    first_loads = [
        copies.local(src, dst)
        for src, dst in (
            (tokens.at[mine, :], x), (h_part, part), (h_theirs, theirs), (cotangent.at[mine, :], cot), (h_val, val),
            (h_dnf, dnf), (h_dnf_t, dnf_t), (h_ffn, ffn), (h_ffn_t, ffn_t),
        )
    ]
    second_loads = [copies.local(src, dst) for src, dst in ((h_wo2, wo2), (h_wo1, wo1), (h_a2, a2), (h_a1, a1))]
    loads_2 = [
        copies.local(src, dst)
        for src, dst in ((h_q2, q2), (h_k2, k2), (h_v2, v2), (h_l2, l2), (h_normed, normed), (h_wq2, wq2))
    ]
    loads_up = [
        copies.local(src, dst)
        for src, dst in ((h_gw.at[:, :, x_bit, 0], keep_up), (h_gw.at[:, z_bit, :, 1], keep_dn), (h_up1, up.at[0]), (h_dn1, dn.at[0]))
    ]
    loads_1 = [copies.local(src, dst) for src, dst in ((h_q1, q1), (h_k1, k1), (h_v1, v1), (h_l1, l1), (h_wq1, wq1))]
    pl.semaphore_wait(barrier, 2 + len(bits))

    hop_up = copies.remote(h_gw.at[:, :, 1 - x_bit, 0], got_up, wide_dev[1])
    hop_dn = copies.remote(h_gw.at[:, 1 - z_bit, :, 1], got_dn, wide_dev[2])

    block = 256
    steps = length // block
    half_steps = steps // 2
    gs[...] = jnp.zeros_like(gs)
    for load in first_loads:
        load.wait()

    def rows_at(step):
        return pl.ds(pl.multiple_of(lax.rem(core * half_steps + step, steps) * block, block), block)

    def whole_rows(which, step):
        start = which * length + lax.rem(core * half_steps + step, steps) * block
        return pl.ds(pl.multiple_of(start, block), block)

    out_in = []
    for step in range(steps):
        rows = rows_at(step)
        attn_out = part[rows, :].astype(f32) + theirs[rows, :].astype(f32) + vec_ref[0:1, :]
        middle = x[rows, :].astype(f32) + mod_ref[2:3, :] * attn_out
        grad_out = cot[rows, :].astype(f32) * wide_lanes(val[rows, :], model)
        ffn_out = ffn[rows, :].astype(f32) + ffn_t[rows, :].astype(f32) + vec_ref[1:2, :]
        ffn[rows, :] = (middle + mod_ref[5:6, :] * ffn_out).astype(bf16)
        gs[5:6, :] += jnp.sum(grad_out * ffn_out, axis=0, keepdims=True)
        copies.save(ffn.at[rows, :], out_all.at[whole_rows(chip, step), :])
        if step < half_steps:
            out_in.append(copies.remote(ffn.at[rows, :], out_all.at[whole_rows(chip, step), :], chip_dev))
        grad_nf = dnf[rows, :].astype(f32) + dnf_t[rows, :].astype(f32)
        plain, inv_std = norm(middle)
        gs[3:4, :] += jnp.sum(grad_nf, axis=0, keepdims=True)
        gs[4:5, :] += jnp.sum(grad_nf * plain, axis=0, keepdims=True)
        d_middle = grad_out + norm_back(grad_nf * (1.0 + mod_ref[4:5, :]), plain, inv_std)
        d_mid[rows, :] = d_middle
        gs[2:3, :] += jnp.sum(d_middle * attn_out, axis=0, keepdims=True)
        rounded = (d_middle * mod_ref[2:3, :]).astype(bf16)
        d_attn[rows, :] = rounded
        gs[7:8, :] += jnp.sum(rounded.astype(f32), axis=0, keepdims=True)
    for load in second_loads:
        load.wait()
    do2[...] = dot_t(d_attn[...], wo2[...]).astype(bf16)
    do1[...] = dot_t(d_attn[...], wo1[...]).astype(bf16)
    tile = (high, 2, 2, share, width)
    att2[:, :, :, :, 3 * width :] = t_dot(d_attn[...], a2[...]).astype(bf16).reshape(tile)
    att1[:, :, :, :, 3 * width :] = t_dot(d_attn[...], a1[...]).astype(bf16).reshape(tile)

    def matrix_grads(att):
        for which, grad in enumerate((dq[...], dk[...].astype(bf16), dv[...].astype(bf16))):
            att[:, :, :, :, which * width : (which + 1) * width] = t_dot(normed[...], grad).astype(bf16).reshape(tile)

    def norm_grads(w_ref):
        return dot(dq[...], w_ref[0]) + dot(dk[...].astype(bf16), w_ref[1]) + dot(dv[...].astype(bf16), w_ref[2])

    def bias_grads(target):
        target[...] = jnp.zeros_like(target)
        target[11:12, :width] = jnp.sum(dq[...].astype(f32), axis=0, keepdims=True)
        target[11:12, width : 2 * width] = jnp.sum(dv[...].astype(bf16).astype(f32), axis=0, keepdims=True)

    for load in loads_2:
        load.wait()
    hops = {}

    def second_hop():
        for load in loads_up:
            load.wait()
        hop_up.wait_recv()
        up[1] = added(keep_up[...], got_up[...])
        hops["up"] = copies.remote(up.at[:, :, 1 - z_bit], got_up2, wide_dev[2])
        hop_dn.wait_recv()
        dn[1] = added(keep_dn[...], got_dn[...])
        hops["dn"] = copies.remote(dn.at[:, :, 1 - x_bit], got_dn2, wide_dev[1])

    def third_hop():
        hops["up"].wait_recv()
        hops["dn"].wait_recv()
        fw[:, 0] = added(up[:, :, z_bit], got_up2[...])
        fw[:, 1] = added(dn[:, :, x_bit], got_dn2[...])

    def high_hops(src, got, dst, lead):
        left = high
        at = 0
        cur = src
        for bit in bits[2:]:
            left //= 2
            mine_bit = bit_of[bit]
            started = [
                copies.remote(cur.at[lead + (2 * i + 1 - mine_bit,)], got.at[lead + (at + i,)], wide_dev[bit]) for i in range(left)
            ]
            yield
            for i in range(left):
                started[i].wait_recv()
                dst[lead + (at + i,)] = added(cur[lead + (2 * i + mine_bit,)], got[lead + (at + i,)])
            cur = dst.at[lead + (pl.ds(at, left),)]
            at += left
        yield cur

    every = slice(None)
    last = {}

    def between_other(index):
        if index == 0:
            second_hop()
        if index == 1:
            third_hop()
            last["fw"] = high_hops(fw, got_fw, fw3, (every, every))
            next(last["fw"])

    attend_back(bias_ref, q2, k2, v2, do2, l2, (qm, gm, km), dq, dk, dv, between_other)
    matrix_grads(att2)
    hop_att2 = copies.remote(att2.at[:, :, 1 - x_bit], got_att2, wide_dev[1])
    bias_grads(sums.at[1])
    dnf[...] = norm_grads(wq2).astype(bf16)

    def pass_on(arrived, array, step):
        arrived.wait_recv()
        rows = whole_rows(1 - chip, step)
        return copies.remote(array.at[rows, :], array.at[rows, :], core_dev)

    out_passed = [pass_on(out_in[step], out_all, step) for step in range(half_steps)]

    for load in loads_1:
        load.wait()

    def between_own(index):
        if index == 0:
            hop_att2.wait_recv()
            at2[...] = added(att2[:, :, x_bit], got_att2[...])
            last["att_y"] = copies.remote(at2, got_att_y, chip_dev)

    attend_back(bias_ref, q1, k1, v1, do1, l1, (qm, gm, km), dq, dk, dv, between_own)
    dnf[...] = added(dnf[...], norm_grads(wq1))
    dn_in = []
    for step in range(steps):
        rows = pl.ds(pl.multiple_of(lax.rem((1 - core) * half_steps + step, steps) * block, block), block)
        dn_in.append(copies.remote(dnf.at[rows, :], dn_t.at[rows, :], core_dev))
    matrix_grads(att1)
    hop_att1 = copies.remote(att1.at[:, :, 1 - x_bit], got_att1, wide_dev[1])
    bias_grads(sums.at[0])

    grad_in = []
    for step in range(steps):
        rows = rows_at(step)
        dn_in[step].wait_recv()
        grad_n = dnf[rows, :].astype(f32) + dn_t[rows, :].astype(f32)
        plain, inv_std = norm(x[rows, :].astype(f32))
        gs[0:1, :] += jnp.sum(grad_n, axis=0, keepdims=True)
        gs[1:2, :] += jnp.sum(grad_n * plain, axis=0, keepdims=True)
        part[rows, :] = (d_mid[rows, :] + norm_back(grad_n * (1.0 + mod_ref[1:2, :]), plain, inv_std)).astype(bf16)
        copies.save(part.at[rows, :], grad_all.at[whole_rows(chip, step), :])
        if step < half_steps:
            grad_in.append(copies.remote(part.at[rows, :], grad_all.at[whole_rows(chip, step), :], chip_dev))

    fw_left = None
    for fw_left in last["fw"]:
        pass
    hop_y = copies.remote(fw_left.at[1, :, 0], got_y, chip_dev)

    for which, ref in enumerate((sums1_ref, sums2_ref)):
        sums[which, 0:11, :] = ref[0:11, :]
        sums[which, 12:13, :] = gs[7:8, :]
        sums[which, 13:14, :] = gdown_ref[0:1, :]
    rows_ref[0, 0:6, :] = gs[0:6, :].astype(bf16)
    rows_ref[0, 6:8, :] = silu_ref[0:2, :]
    count = 1
    small_hops = []

    def small_start(device, level):
        small_hops.append(copies.remote(rows_ref.at[pl.ds(0, count)], rows_ref.at[pl.ds(count, count)], device))
        small_hops.append(copies.remote(sums, got_sums.at[level], device))

    def small_end(level):
        small_hops[-2].wait_recv()
        copies.settle(small_hops[-1])
        sums[...] = sums[...] + got_sums[level]

    small_start(wide_dev[1], 0)
    hop_att1.wait_recv()
    last["att_y"].wait_recv()
    at1[...] = (att1[:, :, x_bit].astype(f32) + got_att1[...].astype(f32) + got_att_y[...].astype(f32)).astype(bf16)
    hop_z = copies.remote(at1.at[:, 1 - z_bit], got_z, wide_dev[2])
    small_end(0)
    count *= 2
    small_start(wide_dev[2], 1)
    hop_z.wait_recv()
    atz[...] = added(at1[:, z_bit], got_z[...])
    last["att"] = high_hops(atz, got_last, at_last, ())
    next(last["att"])
    small_end(1)
    count *= 2
    for level, bit in enumerate(bits[2:]):
        small_start(wide_dev[bit], 2 + level)
        small_end(2 + level)
        count *= 2
    att_left = None
    for att_left in last["att"]:
        pass
    gatt_ref[...] = att_left[0].astype(f32)

    small_hops.append(copies.remote(rows_ref.at[pl.ds(0, count)], rows_ref.at[pl.ds(count, count)], chip_dev))
    small_hops.append(copies.remote(sums.at[1], got_sums.at[len(bits), 0], chip_dev))
    grad_passed = [pass_on(grad_in[step], grad_all, step) for step in range(half_steps)]
    hop_y.wait_recv()
    for which in range(2):
        gffn_ref[which] = fw_left[0, which, 0].astype(f32) + got_y[which].astype(f32)
    small_hops[-2].wait_recv()
    small_hops[-1].wait_recv()
    small_ref[...] = sums[0] + got_sums[len(bits), 0]
    for copy in out_passed + grad_passed:
        copy.wait_recv()
    copies.finish()


def back(n_wide, tokens, cotangent, arrays, vectors):
    length, model = arrays[0].shape
    width, chans = arrays[19].shape[0], model
    assert len(arrays) == BACK_ANY_IN - 2 and len(vectors) == BACK_VMEM_IN
    share = model // n_wide
    high = n_wide // 4
    heads = width // HEAD_DIM
    latents = 2 * n_wide
    levels = n_wide.bit_length()
    tall = ((length, model), bf16)
    slim = ((length, width), bf16)
    slim32 = ((length, width), f32)
    lse = ((length, 8), f32)
    wq = ((3, width, model), bf16)
    wo = ((width, model), bf16)
    half = ((high, 2, share, chans), bf16)
    left = max(high - 1, 1)
    masked = ((heads, length, width), bf16)
    att = ((high, 2, 2, share, 4 * width), bf16)
    att_half = ((high, 2, share, 4 * width), bf16)
    att_quarter = ((high, share, 4 * width), bf16)
    att_last = ((left, share, 4 * width), bf16)
    scratch = [tall] * 9 + [slim] * 4 + [lse] + [slim] * 4 + [lse, wq, wq, wo, wo, ((length, LANES), f32)]
    scratch += [half] * 4 + [((2,) + half[0], bf16)] * 2 + [((2, high, share, chans), bf16)] * 2
    scratch += [((2, 2, high, share, chans), bf16), ((2, 2, left, share, chans), bf16), ((2, 2, left, share, chans), bf16)]
    scratch += [((2, share, chans), bf16)]
    scratch += [((length, model), f32), tall, slim, slim, masked, masked, masked, slim, slim32, slim32]
    scratch += [att, att] + [att_half] * 5 + [att_quarter] * 2 + [att_last] * 2
    scratch += [tall, ((2, 16, model), f32), ((levels, 2, 16, model), f32), ((8, model), f32)]
    any_spec = pl.BlockSpec(memory_space=pl.ANY)
    vmem = pl.BlockSpec(memory_space=pltpu.VMEM)
    full = sds((2 * length, model), bf16)
    return pl.pallas_call(
        functools.partial(back_kernel, n_wide),
        in_specs=[any_spec] * BACK_ANY_IN + [vmem] * BACK_VMEM_IN,
        out_specs=[any_spec] * BACK_ANY_OUT + [vmem] * BACK_VMEM_OUT,
        out_shape=[full, full]
        + [sds((2, share, chans), f32), sds((share, 4 * width), f32), sds((16, model), f32), sds((latents, 8, model), bf16)],
        scratch_shapes=[pltpu.VMEM(*s) for s in scratch]
        + [pltpu.SemaphoreType.DMA((48,)), pltpu.SemaphoreType.DMA((64,)), pltpu.SemaphoreType.DMA((64,))],
        compiler_params=pltpu.CompilerParams(vmem_limit_bytes=63 * MIB, collective_id=2, has_side_effects=True),
        cost_estimate=cost(65),
        name="back",
    )(tokens, cotangent, *arrays, *vectors)


def finish_kernel(grad_ref, rows_ref, silu_ref, pair_ref, wada_ref, cond_ref, out_ref, gw_ref, gb_ref, gc_ref):
    step = pl.program_id(0)
    out_ref[...] = grad_ref[...].astype(f32)
    rows = rows_ref[0]
    gw_ref[...] = t_dot(silu_ref[...], rows)
    gb_ref[pl.ds(step, 1), :] = jnp.sum(rows.astype(f32), axis=0, keepdims=True)
    part = dot_t(pair_ref[0], wada_ref[...])

    @pl.when(step == 0)
    def _():
        gc_ref[...] = part

    @pl.when(step > 0)
    def _():
        gc_ref[...] += part

    @pl.when(step == pl.num_programs(0) - 1)
    def _():
        cond = cond_ref[...].astype(f32)
        sig = 1.0 / (1.0 + jnp.exp(-cond))
        gc_ref[...] = gc_ref[...] * (sig * (1.0 + cond * (1.0 - sig)))


def finish(grad, rows, silu, pair, w_ada, condition):
    sections, latents, model = rows.shape
    share = silu.shape[1]
    pairs = condition.shape[0]
    height = grad.shape[0]
    parts = 6
    block = -(-height // parts // 16) * 16

    def whole(shape):
        return pl.BlockSpec(shape, lambda i: tuple(0 for _ in shape))

    return pl.pallas_call(
        finish_kernel,
        grid=(parts,),
        in_specs=[
            pl.BlockSpec((block, model), lambda i: (i, 0)),
            pl.BlockSpec((1, latents, model), lambda i: (i, 0, 0)),
            whole(silu.shape),
            pl.BlockSpec((1, pairs, model), lambda i: (i, 0, 0)),
            pl.BlockSpec((model, model), lambda i: (0, i)),
            whole(condition.shape),
        ],
        out_specs=[
            pl.BlockSpec((block, model), lambda i: (i, 0)),
            pl.BlockSpec((share, model), lambda i: (0, i)),
            whole((8, model)),
            whole((pairs, model)),
        ],
        out_shape=[sds((height, model), f32), sds((share, 6 * model), f32), sds((8, model), f32), sds((pairs, model), f32)],
        compiler_params=params(24),
        cost_estimate=cost(5),
        name="finish",
    )(grad, rows, silu, pair, w_ada, condition)


def on_device(
    n_wide, tokens, condition, validity, cotangent, w_ada, b_ada, w_qkv, b_qkv, w_out, b_out, w_up, b_up, conv_w, conv_b, w_down, b_down
):
    model = tokens.shape[1]
    width = w_out.shape[0]
    place = lax.axis_index("narrow")
    me_y = place // 2
    me_wide = lax.axis_index("wide")
    share = model // n_wide
    w_qkv = w_qkv.transpose(0, 2, 1)
    (
        normed, q1, k1, v1, a1, l1, q2, k2, v2, a2, l2, wq2, pack2, wo2, part, theirs, dnf, dnf_t, ffn, ffn_t, gw, up1, dn1, val,
        mod, silu, bias, sums1, sums2, g_down, vec,
    ) = front(
        n_wide, tokens, condition, validity, cotangent, w_ada, b_ada, w_qkv, b_qkv, w_out, b_out, w_up, b_up, conv_w, conv_b, w_down, b_down
    )
    block_out, grad_x, g_ffn, g_att, small, rows = back(
        n_wide,
        tokens,
        cotangent,
        (dnf, dnf_t, ffn, ffn_t, part, theirs, normed, q1, k1, v1, a1, l1, q2, k2, v2, a2, l2, w_qkv, wq2, w_out, wo2, gw, up1, dn1, val),
        (mod, bias, vec, sums1, sums2, g_down, silu),
    )
    silu_part = lax.dynamic_slice(rows[:, 6], (0, me_wide * share), (rows.shape[0], share))
    pair = jnp.where(me_y == 0, jnp.stack((rows[0], rows[n_wide])), jnp.stack((rows[n_wide], rows[0])))
    grad_tokens, grad_w_ada, b_rows, grad_condition = finish(
        grad_x, rows.transpose(1, 0, 2), silu_part, pair.transpose(1, 0, 2), w_ada, condition
    )
    share_ada = 6 * model // n_wide
    return (
        block_out,
        grad_tokens,
        grad_condition,
        grad_w_ada,
        lax.dynamic_slice(b_rows[:6].reshape(-1), (me_wide * share_ada,), (share_ada,)),
        g_att[:, : 3 * width].reshape(share, 3, width).transpose(1, 0, 2),
        small[11, : 2 * width].reshape(2, width),
        g_att[:, 3 * width :].T,
        lax.dynamic_slice(small[12], (me_wide * share,), (share,)),
        g_ffn[0],
        small[10],
        small[:9],
        small[9],
        g_ffn[1].T,
        lax.dynamic_slice(small[13], (me_wide * share,), (share,)),
    )


def solution(mesh):
    n_wide = mesh.shape["wide"]
    return jax.shard_map(
        functools.partial(on_device, n_wide),
        mesh=mesh,
        in_specs=(
            P("wide", None),
            P("wide", None),
            P("wide"),
            P("wide", None),
            P(),
            P(),
            P(None, None, "narrow"),
            P(None, "narrow"),
            P("narrow", None),
            P(),
            P(None, "narrow"),
            P("narrow"),
            P(None, "narrow"),
            P("narrow"),
            P("narrow", None),
            P(),
        ),
        out_specs=(
            P("wide", None),
            P("wide", None),
            P("wide", None),
            P("wide", None),
            P("wide"),
            P(None, "wide", "narrow"),
            P(None, "narrow"),
            P("narrow", "wide"),
            P("wide"),
            P("wide", "narrow"),
            P("narrow"),
            P(None, "narrow"),
            P("narrow"),
            P("narrow", "wide"),
            P("wide"),
        ),
        check_vma=False,
    )
```

```python
import functools

import jax
import jax.numpy as jnp
from jax import lax
from jax.experimental import pallas as pl
from jax.experimental.pallas import tpu as pltpu
from jax.sharding import PartitionSpec as P

HEAD_DIM = 64
GRID = 32
LANES = 128
MIB = 2**20

MESH = pl.DeviceIdType.MESH

bf16 = jnp.bfloat16
f32 = jnp.float32
epsilon = 1e-06
neg_fill = -1000000000.0

GELU_A = 0.7978845608
GELU_B = 0.044715


def dot(a, b):
    return jnp.dot(a, b, preferred_element_type=f32)


def dot_t(a, b):
    return lax.dot_general(a, b, (((1,), (1,)), ((), ())), preferred_element_type=f32)


def t_dot(a, b):
    return lax.dot_general(a, b, (((0,), (0,)), ((), ())), preferred_element_type=f32)


def norm(values):
    center = jnp.mean(values, axis=-1, keepdims=True)
    centered = values - center
    inv_std = lax.rsqrt(jnp.mean(centered * centered, axis=-1, keepdims=True) + epsilon)
    return centered * inv_std, inv_std


def norm_back(grad_plain, plain, inv_std):
    first_mean = jnp.mean(grad_plain, axis=-1, keepdims=True)
    second_mean = jnp.mean(grad_plain * plain, axis=-1, keepdims=True)
    return inv_std * (grad_plain - first_mean - plain * second_mean)


def wide_lanes(column, width):
    return jnp.concatenate([column] * (width // LANES), axis=1)


def of_head(values, head):
    lane = lax.broadcasted_iota(jnp.int32, values.shape, 1)
    inside = (lane >= head * HEAD_DIM) & (lane < (head + 1) * HEAD_DIM)
    return jnp.where(inside, values, jnp.zeros_like(values))


def cost(us):
    return pl.CostEstimate(flops=int(us * 1e9), bytes_accessed=0, transcendentals=0)


def params(limit):
    return pltpu.CompilerParams(vmem_limit_bytes=limit * MIB)


def sds(shape, dtype):
    return jax.ShapeDtypeStruct(shape, dtype)


def rows_of(i, size):
    return pl.ds(pl.multiple_of(i * size, size), size)


def flip(index, bit):
    return index + bit - 2 * bit * lax.rem(lax.div(index, bit), 2)


class Copies:
    def __init__(self, local_sems, send_sems, recv_sems):
        self.local_sems, self.send_sems, self.recv_sems = local_sems, send_sems, recv_sems
        self.locals, self.remotes = 0, 0
        self.pending = []

    def local(self, src, dst):
        copy = pltpu.make_async_copy(src, dst, self.local_sems.at[self.locals])
        self.locals += 1
        copy.start()
        return copy

    def save(self, src, dst):
        self.pending.append(self.local(src, dst).wait)

    def later(self, src, dst, device):
        k = self.remotes
        self.remotes += 1
        copy = pltpu.make_async_remote_copy(
            src, dst, self.send_sems.at[k], self.recv_sems.at[k], device_id=device, device_id_type=MESH
        )
        self.pending.append(copy.wait_send)
        return copy

    def settle(self, copy):
        self.pending.remove(copy.wait_send)
        copy.wait()

    def remote(self, src, dst, device):
        copy = self.later(src, dst, device)
        copy.start()
        return copy

    def finish(self):
        assert self.locals <= self.local_sems.shape[0] and self.remotes <= self.send_sems.shape[0]
        for wait in self.pending:
            wait()


def project(normed, w_ref, b_rows, q_ref, k_ref, v_ref):
    scale = HEAD_DIM ** (-0.5)
    queries = (dot_t(normed, w_ref[0]) + b_rows[0]).astype(bf16)
    q_ref[...] = (queries.astype(f32) * scale).astype(bf16)
    k_ref[...] = dot_t(normed, w_ref[1]).astype(bf16)
    v_ref[...] = (dot_t(normed, w_ref[2]) + b_rows[1]).astype(bf16)


def attend(bias_ref, q_ref, k_ref, v_ref, lse_ref, vm, finish):
    length, width = q_ref.shape
    heads = width // HEAD_DIM
    block = min(512, length)
    for head in range(heads):
        vm[head] = of_head(v_ref[...], head)
    for index in range(length // block):
        rows = pl.ds(index * block, block)
        q = q_ref[rows, :]
        k = k_ref[...]
        total = jnp.zeros((block, width), f32)
        for head in range(heads):
            s = dot_t(of_head(q, head), k) + bias_ref[...]
            top = jnp.max(s, axis=1, keepdims=True)
            raised = jnp.exp(s - top)
            mass = jnp.sum(raised, axis=1, keepdims=True)
            out = dot(raised.astype(bf16), vm[head])
            total = total + out * (1.0 / mass)
            lse_ref[rows, head : head + 1] = top + jnp.log(mass)
        finish(index, rows, total)


def ffn_half(nf, df, val_ref, wup_ref, wdn_ref, pack_ref, sums_ref, gw_ref, dnf_acc, ffn_acc, first_half, scratch, share_out, events=()):
    taps, sums, center, hs, ds, act, gact, dh = scratch
    length = nf.shape[0]
    chans = wup_ref.shape[1]
    tile = (GRID // 8, 8, LANES)
    zero = jnp.zeros((GRID, LANES), f32)
    for buf in (hs, ds):
        for j in range(3):
            buf[j, 0:GRID, :] = zero
            buf[j, length + GRID : length + 2 * GRID, :] = zero
    for t in range(11):
        taps[t] = jnp.broadcast_to(pack_ref[t : t + 1, :].astype(f32), (8, chans))
    sums[...] = jnp.zeros_like(sums)
    center[...] = dot(nf[...], wup_ref[...])
    if not first_half:
        gact[...] = dot_t(df[...], wdn_ref[...])
    column = lax.broadcasted_iota(jnp.int32, (GRID, LANES), 0)
    first = column == 0
    last = column == GRID - 1

    def put(dst, r, x):
        rows = pl.ds(pl.multiple_of((r + 1) * GRID, GRID), GRID)
        dst[1, rows, :] = x
        dst[0, rows, :] = jnp.where(first, 0.0, pltpu.roll(x, 1, 0))
        dst[2, rows, :] = jnp.where(last, 0.0, pltpu.roll(x, GRID - 1, 0))

    def near_row(buf, j, r):
        return buf[j, pl.ds(pl.multiple_of((r + 1) * GRID, GRID), GRID), :].reshape(tile)

    def channel_part(part, carry):
        for at, event in events:
            pl.when(part == at)(event)
        lanes = pl.ds(pl.multiple_of(part * LANES, LANES), LANES)

        def spread(r):
            rows = rows_of(r, GRID)
            h = (center[rows, lanes].reshape(tile) + taps[0, :, lanes]).reshape(GRID, LANES)
            put(hs, r, h * val_ref[rows, :])

        def conv_row(r):
            rows = rows_of(r, GRID)
            near = [[near_row(hs, j, r + i - 1) for j in range(3)] for i in range(3)]
            conv = jnp.broadcast_to(taps[1, :, lanes], tile)
            for i in range(3):
                for j in range(3):
                    conv = conv + taps[2 + 3 * i + j, :, lanes] * near[i][j]
            square = conv * conv
            th = jnp.tanh(conv * (GELU_A + (GELU_A * GELU_B) * square))
            half = 0.5 * conv
            act[rows, lanes] = (half + half * th).reshape(GRID, LANES).astype(bf16)
            slope = 0.5 + 0.5 * th + half * (1.0 - th * th) * (GELU_A + (3 * GELU_A * GELU_B) * square)
            dc = gact[rows, lanes].reshape(tile) * slope
            for i in range(3):
                for j in range(3):
                    sums[3 * i + j, :, lanes] += jnp.sum(dc * near[i][j], axis=0)
            sums[9, :, lanes] += jnp.sum(dc, axis=0)
            put(ds, r, dc.reshape(GRID, LANES))

        def hidden_row(r):
            rows = rows_of(r, GRID)
            total = jnp.zeros(tile, f32)
            for i in range(3):
                for j in range(3):
                    total = total + taps[2 + 3 * i + j, :, lanes] * near_row(ds, 2 - j, r + 1 - i)
            total = total * val_ref[rows, :].reshape(tile)
            rounded = total.reshape(GRID, LANES).astype(bf16)
            dh[rows, lanes] = rounded
            sums[10, :, lanes] += jnp.sum(rounded.astype(f32).reshape(tile), axis=0)

        unroll = 4

        def loop(fun):
            def some(i, c):
                for u in range(unroll):
                    fun(i * unroll + u)
                return c

            lax.fori_loop(0, GRID // unroll, some, 0)

        loop(spread)
        loop(conv_row)
        loop(hidden_row)
        return carry

    lax.fori_loop(0, chans // LANES, channel_part, 0)
    for t in range(11):
        sums_ref[t : t + 1, :] = jnp.sum(sums[t], axis=0, keepdims=True)
    sums_ref[11:16, :] = jnp.zeros((5, chans), f32)
    part_dnf = dot_t(dh[...], wup_ref[...])
    if not first_half:
        part_dnf = part_dnf + dnf_acc[...].astype(f32)
    dnf_acc[...] = part_dnf.astype(bf16)
    share_out(0)
    part_ffn = dot(act[...], wdn_ref[...])
    if not first_half:
        part_ffn = part_ffn + ffn_acc[...].astype(f32)
    ffn_acc[...] = part_ffn.astype(bf16)
    share_out(1)
    high = gw_ref.shape[0]
    share = gw_ref.shape[4]
    gw_ref[:, :, :, 0] = t_dot(nf[...], dh[...]).astype(bf16).reshape(high, 2, 2, share, chans)
    gw_ref[:, :, :, 1] = t_dot(df[...], act[...]).astype(bf16).reshape(high, 2, 2, share, chans)


FRONT_ANY_IN = 7
FRONT_VMEM_IN = 9
FRONT_ANY_OUT = 24
FRONT_VMEM_OUT = 7


def front_kernel(*refs):
    refs = list(refs)

    def take(count):
        head = refs[:count]
        del refs[:count]
        return head

    tokens, cotangent, w_ada, w_qkv, w_out, w_up, w_down = take(FRONT_ANY_IN)
    cond_ref, valid_ref, bada_ref, bqkv_ref, bout_ref, bup_ref, convw_ref, convb_ref, bdown_ref = take(FRONT_VMEM_IN)
    (
        o_normed, o_q1, o_k1, o_v1, o_a1, o_l1, o_q2, o_k2, o_v2, o_a2, o_l2, o_wqkv, o_pack, o_wout, o_part, o_theirs,
        o_dnf, o_dnf_theirs, o_ffn, o_ffn_theirs, o_gw, o_up1, o_dn1, o_val,
    ) = take(FRONT_ANY_OUT)
    mod_ref, silu_ref, bias_ref, sums1_ref, sums2_ref, gdown_ref, vec_ref = take(FRONT_VMEM_OUT)
    x, cot, normed, q1, k1, v1, a1, l1, q2, k2, v2, a2, l2, vm, val = take(15)
    wada_buf, wq1, wo1, wu1, wd1, wq2, wo2, wu2, wd2, pack1, pack2 = take(11)
    part, theirs, nf, df, dnf, ffn, gw1, gw2, got_up, got_dn = take(10)
    ffn_scratch = take(8)
    local_sems, send_sems, recv_sems = take(3)
    assert not refs

    length, model = x.shape
    width = wo1.shape[0]
    place = lax.axis_index("narrow")
    wide = lax.axis_index("wide")
    chip = lax.div(place, 2)
    x_bit = lax.rem(wide, 2)
    z_bit = lax.rem(lax.div(wide, 2), 2)
    core_dev = {"narrow": flip(place, 1)}
    chip_dev = {"narrow": flip(place, 2)}
    x_dev = {"wide": flip(wide, 1)}
    z_dev = {"wide": flip(wide, 2)}
    barrier = pltpu.get_barrier_semaphore()
    for device in (core_dev, chip_dev, x_dev, z_dev):
        pl.semaphore_signal(barrier, inc=1, device_id=device, device_id_type=MESH)
    copies = Copies(local_sems, send_sems, recv_sems)
    mine = pl.ds(pl.multiple_of(chip * length, length), length)
    slots = wada_buf.shape[0]

    def load_ada(i):
        return copies.local(w_ada.at[:, pl.ds(i * model, model)], wada_buf.at[i % slots])

    ada = [load_ada(i) for i in range(slots)]
    load_x = copies.local(tokens.at[mine, :], x)
    load_wq1 = copies.local(w_qkv, wq1)
    load_cot = copies.local(cotangent.at[mine, :], cot)
    load_wo1 = copies.local(w_out, wo1)
    load_wu1 = copies.local(w_up, wu1)
    load_wd1 = copies.local(w_down, wd1)

    pad = jnp.zeros((1, model - 2 * width), f32)
    b_row = jnp.concatenate((bqkv_ref[0:1, :].astype(f32), bqkv_ref[1:2, :].astype(f32), pad), axis=1)
    pack1[...] = jnp.concatenate(
        (
            bup_ref[...].astype(f32).reshape(1, model),
            convb_ref[...].astype(f32).reshape(1, model),
            convw_ref[...].astype(f32),
            b_row,
            jnp.zeros((4, model), f32),
        ),
        axis=0,
    ).astype(bf16)
    vec_ref[...] = jnp.concatenate(
        (bout_ref[...].astype(f32).reshape(1, model), bdown_ref[...].astype(f32).reshape(1, model), jnp.zeros((6, model), f32)),
        axis=0,
    )
    pl.semaphore_wait(barrier, 4)

    def half_rows(size, piece):
        return pl.ds(pl.multiple_of(x_bit * (size // 2) + piece * (size // 4), size // 4), size // 4)

    def qkv_piece(ref, piece):
        return ref.at[piece, pl.ds(pl.multiple_of(x_bit * (width // 2), width // 2), width // 2), :]

    def ffn_piece(ref, piece):
        return ref.at[half_rows(model, piece), :]

    def down_piece(ref, piece):
        size = model // 8
        return ref.at[pl.ds(pl.multiple_of(x_bit * (model // 2) + piece * size, size), size), :]

    qkv_in = [copies.remote(qkv_piece(w_qkv, p), qkv_piece(wq2, p), chip_dev) for p in range(3)]
    pack_in = copies.remote(pack1, pack2, chip_dev)
    out_in = copies.remote(w_out, wo2, chip_dev)
    up_in = [copies.remote(ffn_piece(w_up, p), ffn_piece(wu2, p), chip_dev) for p in range(2)]
    down_in = [copies.remote(down_piece(w_down, p), down_piece(wd2, p), chip_dev) for p in range(4)]

    def pass_on(arrived, ref, piece, p):
        arrived.wait_recv()
        return copies.remote(piece(ref, p), piece(ref, p), x_dev)

    cond = jnp.where(chip == 0, cond_ref[0:1, :].astype(f32), cond_ref[1:2, :].astype(f32))
    silu = (cond / (1.0 + jnp.exp(-cond))).astype(bf16)
    silu_ref[...] = jnp.broadcast_to(silu, silu_ref.shape)
    tall = length // LANES
    for j in range(tall):
        valid = jnp.where(chip == 0, valid_ref[j : j + 1, :], valid_ref[tall + j : tall + j + 1, :]).astype(f32)
        val[j * LANES : (j + 1) * LANES, :] = jnp.broadcast_to(valid, (LANES, LANES)).T
        bias_ref[:, j * LANES : (j + 1) * LANES] = jnp.where(valid > 0, 0.0, neg_fill)
    copies.save(val, o_val)
    mod_ref[6:8, :] = jnp.zeros((2, model), f32)
    silu8 = silu_ref[...]
    for i in range(6):
        ada[i].wait()
        row = dot(silu8, wada_buf[i % slots])[0:1, :]
        mod_ref[i : i + 1, :] = row + bada_ref[i * model : (i + 1) * model].astype(f32).reshape(1, model)
        if i + slots < 6:
            ada.append(load_ada(i + slots))

    load_x.wait()

    def normalize(i, carry):
        rows = rows_of(i, 256)
        plain, _ = norm(x[rows, :].astype(f32))
        normed[rows, :] = (plain * (1.0 + mod_ref[1:2, :]) + mod_ref[0:1, :]).astype(bf16)
        return carry

    lax.fori_loop(0, length // 256, normalize, 0)
    copies.save(normed, o_normed)
    load_wq1.wait()
    project(normed[...], wq1, (pack1[11:12, :width].astype(f32), b_row[:, width : 2 * width]), q1, k1, v1)
    for src, dst in ((q1, o_q1), (k1, o_k1), (v1, o_v1)):
        copies.save(src, dst)
    passed = {}

    def finish_own(index, rows, total):
        a1[rows, :] = total.astype(bf16)
        for p in ((0, 1), (2,))[index]:
            passed["qkv%d" % p] = pass_on(qkv_in[p], wq2, qkv_piece, p)

    attend(bias_ref, q1, k1, v1, l1, vm, finish_own)
    copies.save(a1, o_a1)
    copies.save(l1, o_l1)

    block = 256
    load_cot.wait()
    gdown_ref[...] = jnp.zeros_like(gdown_ref)
    for index in range(length // block):
        rows = pl.ds(index * block, block)
        grad_out = cot[rows, :].astype(f32) * wide_lanes(val[rows, :], model)
        rounded = (grad_out * mod_ref[5:6, :]).astype(bf16)
        df[rows, :] = rounded
        gdown_ref[0:1, :] += jnp.sum(rounded.astype(f32), axis=0, keepdims=True)
    load_wd1.wait()
    ffn_scratch[6][...] = dot_t(df[...], wd1[...])

    load_wo1.wait()
    pack_in.wait_recv()
    for p in range(3):
        passed["qkv%d" % p].wait_recv()
    row = pack2[11:12, :].astype(f32)
    project(normed[...], wq2, (row[:, :width], row[:, width : 2 * width]), q2, k2, v2)
    for src, dst in ((q2, o_q2), (k2, o_k2), (v2, o_v2), (wq2, o_wqkv), (pack2, o_pack)):
        copies.save(src, dst)
    part_in = []

    def finish_other(index, rows, total):
        if index == 0:
            out_in.wait_recv()
        rounded = total.astype(bf16)
        a2[rows, :] = rounded
        part[rows, :] = (dot(a1[rows, :], wo1[...]) + dot(rounded, wo2[...])).astype(bf16)
        part_in.append(copies.remote(part.at[rows, :], theirs.at[rows, :], core_dev))
        if index == 1:
            passed["up0"] = pass_on(up_in[0], wu2, ffn_piece, 0)

    attend(bias_ref, q2, k2, v2, l2, vm, finish_other)
    for src, dst in ((a2, o_a2), (l2, o_l2), (wo2, o_wout), (part, o_part)):
        copies.save(src, dst)

    for index in range(length // block):
        rows = pl.ds(index * block, block)
        if index % 2 == 0:
            part_in[index // 2].wait_recv()
        attn_out = part[rows, :].astype(f32) + theirs[rows, :].astype(f32) + vec_ref[0:1, :]
        middle = x[rows, :].astype(f32) + mod_ref[2:3, :] * attn_out
        plain, _ = norm(middle)
        nf[rows, :] = (plain * (1.0 + mod_ref[4:5, :]) + mod_ref[3:4, :]).astype(bf16)
    copies.save(theirs, o_theirs)

    passed["up1"] = pass_on(up_in[1], wu2, ffn_piece, 1)
    load_wu1.wait()

    def pass_down(p):
        copy = copies.later(down_piece(wd2, p), down_piece(wd2, p), x_dev)
        passed["down%d" % p] = copy

        def event():
            down_in[p].wait_recv()
            copy.start()

        return event

    downs = [pass_down(p) for p in range(4)]
    ffn_half(
        nf, df, val, wu1, wd1, pack1, sums1_ref, gw1, dnf, ffn, True, ffn_scratch, lambda i: downs[2 + i](),
        events=((2, downs[0]), (4, downs[1])),
    )
    up_got = copies.remote(gw1.at[:, :, 1 - x_bit, 0], got_up, x_dev)
    down_got = copies.remote(gw1.at[:, 1 - z_bit, :, 1], got_dn, z_dev)

    for name in ("up0", "up1", "down0", "down1", "down2", "down3"):
        passed[name].wait_recv()
    arriving = []

    def exchange(i):
        src, saved, landing = ((dnf, o_dnf, o_dnf_theirs), (ffn, o_ffn, o_ffn_theirs))[i]
        arriving.append(copies.remote(src, landing, core_dev))
        copies.save(src, saved)

    ffn_half(nf, df, val, wu2, wd2, pack2, sums2_ref, gw2, dnf, ffn, False, ffn_scratch, exchange)
    copies.save(gw2, o_gw)
    up_got.wait_recv()
    got_up[...] = (gw1[:, :, x_bit, 0].astype(f32) + got_up[...].astype(f32)).astype(bf16)
    copies.save(got_up, o_up1)
    down_got.wait_recv()
    got_dn[...] = (gw1[:, z_bit, :, 1].astype(f32) + got_dn[...].astype(f32)).astype(bf16)
    copies.save(got_dn, o_dn1)
    for copy in arriving:
        copy.wait_recv()
    copies.finish()


def front(n_wide, tokens, condition, validity, cotangent, w_ada, b_ada, w_qkv, b_qkv, w_out, b_out, w_up, b_up, conv_w, conv_b, w_down, b_down):
    latents = condition.shape[0]
    length = tokens.shape[0] // latents
    model = tokens.shape[1]
    width = w_out.shape[0]
    chans = w_up.shape[1]
    share = model // n_wide
    high = n_wide // 4
    heads = width // HEAD_DIM
    tall = ((length, model), bf16)
    slim = ((length, width), bf16)
    lse = ((length, 8), f32)
    wq = (w_qkv.shape, bf16)
    pack = ((16, chans), bf16)
    wo = (w_out.shape, bf16)
    wf = (w_up.shape, bf16)
    gw = ((high, 2, 2, 2, share, chans), bf16)
    gw_half = ((high, 2, share, chans), bf16)
    val = ((length, LANES), f32)
    outs = [tall] + [slim] * 4 + [lse] + [slim] * 4 + [lse, wq, pack, wo] + [tall] * 6 + [gw, gw_half, gw_half, val]
    small_outs = [
        ((8, model), f32),
        ((8, model), bf16),
        ((1, length), f32),
        ((16, chans), f32),
        ((16, chans), f32),
        ((8, model), f32),
        ((8, model), f32),
    ]
    scratch = [tall] * 3 + [slim] * 4 + [lse] + [slim] * 4 + [lse, ((heads, length, width), bf16), val]
    scratch += [((6, model, model), bf16), wq, wo, wf, wf, wq, wo, wf, wf, pack, pack]
    scratch += [tall] * 6 + [gw, gw, gw_half, gw_half]
    scratch += [((11, 8, chans), f32)] * 2 + [((length, chans), f32)]
    scratch += [((3, length + 2 * GRID + 8, LANES), f32)] * 2 + [((length, chans), bf16), ((length, chans), f32), ((length, chans), bf16)]
    any_spec = pl.BlockSpec(memory_space=pl.ANY)
    vmem = pl.BlockSpec(memory_space=pltpu.VMEM)
    assert len(outs) == FRONT_ANY_OUT and len(small_outs) == FRONT_VMEM_OUT
    return pl.pallas_call(
        front_kernel,
        in_specs=[any_spec] * FRONT_ANY_IN + [vmem] * FRONT_VMEM_IN,
        out_specs=[any_spec] * FRONT_ANY_OUT + [vmem] * FRONT_VMEM_OUT,
        out_shape=[sds(*o) for o in outs + small_outs],
        scratch_shapes=[pltpu.VMEM(*s) for s in scratch]
        + [pltpu.SemaphoreType.DMA((48,)), pltpu.SemaphoreType.DMA((32,)), pltpu.SemaphoreType.DMA((32,))],
        compiler_params=pltpu.CompilerParams(vmem_limit_bytes=62 * MIB, collective_id=1, has_side_effects=True),
        cost_estimate=cost(60),
        name="front",
    )(
        tokens, cotangent, w_ada, w_qkv, w_out, w_up, w_down,
        condition, validity.reshape(-1, LANES), b_ada, b_qkv, b_out, b_up, conv_w, conv_b, b_down,
    )


BACK_ANY_IN = 28
BACK_VMEM_IN = 8
BACK_ANY_OUT = 2
BACK_VMEM_OUT = 6


def attend_back(bias_ref, q_ref, k_ref, v_ref, grad_ref, lse_ref, masked, dq, dk, dv, between):
    qm, gm, km = masked
    length, width = q_ref.shape
    heads = width // HEAD_DIM
    block = min(512, length)
    scale = HEAD_DIM ** (-0.5)
    dk[...] = jnp.zeros_like(dk)
    dv[...] = jnp.zeros_like(dv)
    for head in range(heads):
        qm[head] = of_head(q_ref[...], head)
        gm[head] = of_head(grad_ref[...], head)
        km[head] = of_head(k_ref[...], head)
    for index in range(length // block):
        rows = pl.ds(index * block, block)
        k = k_ref[...]
        v = v_ref[...]
        total = jnp.zeros((block, width), f32)
        for head in range(heads):
            qh = qm[head, rows, :]
            gh = gm[head, rows, :]
            weights = jnp.exp(dot_t(qh, k) + bias_ref[...] - lse_ref[rows, head : head + 1])
            grad_weights = dot_t(gh, v)
            inner = jnp.sum(weights * grad_weights, axis=1, keepdims=True)
            grad_scores = (weights * (grad_weights - inner)).astype(bf16)
            dv[...] += t_dot(weights.astype(bf16), gh)
            dk[...] += t_dot(grad_scores, qh)
            total = total + dot(grad_scores, km[head])
        dq[rows, :] = (total * scale).astype(bf16)
        between(index)


def added(a, b):
    return (a.astype(f32) + b.astype(f32)).astype(bf16)


def back_kernel(n_wide, *refs):
    refs = list(refs)

    def take(count):
        head = refs[:count]
        del refs[:count]
        return head

    h_in = take(BACK_ANY_IN)
    (
        tokens, cotangent, h_dnf, h_dnf_t, h_ffn, h_ffn_t, h_part, h_theirs, h_normed, h_q1, h_k1, h_v1, h_a1, h_l1,
        h_q2, h_k2, h_v2, h_a2, h_l2, h_wq1, h_wq2, h_wo1, h_wo2, h_gw, h_up1, h_dn1, h_val, w_ada,
    ) = h_in
    mod_ref, bias_ref, vec_ref, sums1_ref, sums2_ref, gdown_ref, silu_ref, cond_ref = take(BACK_VMEM_IN)
    out_all, grad_all = take(BACK_ANY_OUT)
    gffn_ref, gatt_ref, small_ref, rows_ref, rows_late_ref, gcond_ref = take(BACK_VMEM_OUT)
    x, cot, dnf, dnf_t, ffn, ffn_t, part, theirs, normed, q1, k1, v1, a1, l1, q2, k2, v2, a2, l2, wq1, wq2, wo1, wo2, val = take(24)
    own_up, own_dn, oth_up, oth_dn, got_up, got_dn, got_own = take(7)
    ffn_tails = [take(4) for _ in range(3)]
    d_mid, d_attn, do1, do2, qm, gm, km, dq, dk, dv = take(10)
    att1, att2 = take(2)
    att_heads = [take(2) for _ in range(4)]
    att_tails = [take(4) for _ in range(4)]
    got_y_ffn, got_y_att, gcond, got_cond, late, got_late = take(6)
    dn_t, sums, got_sums, gs = take(4)
    local_sems, send_sems, recv_sems = take(3)
    assert not refs

    length, model = x.shape
    width = wo1.shape[0]
    high = own_up.shape[0]
    share = own_up.shape[2]
    place = lax.axis_index("narrow")
    wide = lax.axis_index("wide")
    chip = lax.div(place, 2)
    core = lax.rem(place, 2)
    bits = [1 << b for b in range(n_wide.bit_length() - 1)]
    bit_of = {bit: lax.rem(lax.div(wide, bit), 2) for bit in bits}
    wide_dev = {bit: {"wide": flip(wide, bit)} for bit in bits}
    x_bit, z_bit = bit_of[1], bit_of[2]
    core_dev = {"narrow": flip(place, 1)}
    chip_dev = {"narrow": flip(place, 2)}
    barrier = pltpu.get_barrier_semaphore()
    for device in [core_dev, chip_dev] + [wide_dev[bit] for bit in bits]:
        pl.semaphore_signal(barrier, inc=1, device_id=device, device_id_type=MESH)
    copies = Copies(local_sems, send_sems, recv_sems)
    block = 256
    steps = length // block
    half_steps = steps // 2

    def rows_at(step):
        return pl.ds(pl.multiple_of(lax.rem(core * half_steps + step, steps) * block, block), block)

    def whole_rows(which, step):
        start = which * length + lax.rem(core * half_steps + step, steps) * block
        return pl.ds(pl.multiple_of(start, block), block)

    first_loads = []
    for step in range(steps):
        rows = rows_at(step)
        here = whole_rows(chip, step)
        pairs = [(tokens.at[here, :], x.at[rows, :]), (cotangent.at[here, :], cot.at[rows, :])]
        pairs += [
            (src.at[rows, :], dst.at[rows, :])
            for src, dst in ((h_part, part), (h_theirs, theirs), (h_val, val), (h_ffn, ffn), (h_ffn_t, ffn_t), (h_dnf, dnf), (h_dnf_t, dnf_t))
        ]
        first_loads.append([copies.local(src, dst) for src, dst in pairs])
    loads_own = [copies.local(h_up1, own_up), copies.local(h_dn1, own_dn)]
    second_loads = [copies.local(src, dst) for src, dst in ((h_wo2, wo2), (h_wo1, wo1), (h_a2, a2), (h_a1, a1))]
    loads_2 = [
        copies.local(src, dst)
        for src, dst in ((h_q2, q2), (h_k2, k2), (h_v2, v2), (h_l2, l2), (h_normed, normed), (h_wq2, wq2))
    ]
    loads_keep = [copies.local(h_gw.at[:, :, x_bit, 0], oth_up), copies.local(h_gw.at[:, z_bit, :, 1], oth_dn)]
    loads_1 = [copies.local(src, dst) for src, dst in ((h_q1, q1), (h_k1, k1), (h_v1, v1), (h_l1, l1), (h_wq1, wq1))]
    pl.semaphore_wait(barrier, 2 + len(bits))

    def high_hops(cur, got, dst):
        left = high
        at = 0
        for bit in bits[2:]:
            left //= 2
            mine_bit = bit_of[bit]
            started = [copies.remote(cur.at[2 * i + 1 - mine_bit], got.at[at + i], wide_dev[bit]) for i in range(left)]
            yield
            for i in range(left):
                started[i].wait_recv()
                dst[at + i] = added(cur[2 * i + mine_bit], got[at + i])
            cur = dst.at[pl.ds(at, left)]
            at += left
        yield cur

    def second_hop(cur, bit, tail):
        got, summed, got_high, summed_high = tail
        hop = copies.remote(cur.at[:, 1 - bit_of[bit]], got, wide_dev[bit])
        yield
        hop.wait_recv()
        summed[...] = added(cur[:, bit_of[bit]], got[...])
        yield from high_hops(summed, got_high, summed_high)

    def other_chain(which, first, cur, got, tail):
        if first == 1:
            hop = copies.remote(h_gw.at[:, :, 1 - x_bit, which], got, wide_dev[1])
        else:
            hop = copies.remote(h_gw.at[:, 1 - z_bit, :, which], got, wide_dev[2])
        yield
        hop.wait_recv()
        loads_keep[which].wait()
        cur[...] = added(cur[...], got[...])
        yield from second_hop(cur, 3 - first, tail)

    def att_chain(att, which, head, tail):
        got, cur = head
        first = 1 + which
        lanes = pl.ds(which * 2 * width, 2 * width)
        if first == 1:
            hop = copies.remote(att.at[:, :, 1 - x_bit, :, lanes], got, wide_dev[1])
            keep = att.at[:, :, x_bit, :, lanes]
        else:
            hop = copies.remote(att.at[:, 1 - z_bit, :, :, lanes], got, wide_dev[2])
            keep = att.at[:, z_bit, :, :, lanes]
        yield
        hop.wait_recv()
        cur[...] = added(keep[...], got[...])
        yield from second_hop(cur, 3 - first, tail)

    def step_on(*chains):
        for chain in chains:
            next(chain)

    def rest_of(chain):
        result = None
        for result in chain:
            pass
        return result

    def over_chip(cur, got):
        hop = copies.remote(h_gw.at[:, :, 1 - x_bit, 0], got_up, wide_dev[1])
        yield
        hop.wait_recv()
        loads_keep[0].wait()
        cur[...] = added(cur[...], got_up[...])
        hop = copies.remote(cur, got, chip_dev)
        yield
        hop.wait_recv()
        loads_own[0].wait()
        own_up[...] = added(own_up[...], got[...])
        yield from second_hop(own_up, 2, ffn_tails[0])

    up_chain = over_chip(oth_up, got_own)
    oth_dn_chain = other_chain(1, 2, oth_dn, got_dn, ffn_tails[2])
    step_on(up_chain, oth_dn_chain)
    own_dn_chain = second_hop(own_dn, 1, ffn_tails[1])

    gs[...] = jnp.zeros_like(gs)
    out_in = []
    for step in range(steps):
        rows = rows_at(step)
        for load in first_loads[step]:
            load.wait()
        attn_out = part[rows, :].astype(f32) + theirs[rows, :].astype(f32) + vec_ref[0:1, :]
        middle = x[rows, :].astype(f32) + mod_ref[2:3, :] * attn_out
        grad_out = cot[rows, :].astype(f32) * wide_lanes(val[rows, :], model)
        ffn_out = ffn[rows, :].astype(f32) + ffn_t[rows, :].astype(f32) + vec_ref[1:2, :]
        ffn[rows, :] = (middle + mod_ref[5:6, :] * ffn_out).astype(bf16)
        gs[5:6, :] += jnp.sum(grad_out * ffn_out, axis=0, keepdims=True)
        copies.save(ffn.at[rows, :], out_all.at[whole_rows(chip, step), :])
        if step < half_steps:
            out_in.append(copies.remote(ffn.at[rows, :], out_all.at[whole_rows(chip, step), :], chip_dev))
        grad_nf = dnf[rows, :].astype(f32) + dnf_t[rows, :].astype(f32)
        plain, inv_std = norm(middle)
        gs[3:4, :] += jnp.sum(grad_nf, axis=0, keepdims=True)
        gs[4:5, :] += jnp.sum(grad_nf * plain, axis=0, keepdims=True)
        d_middle = grad_out + norm_back(grad_nf * (1.0 + mod_ref[4:5, :]), plain, inv_std)
        d_mid[rows, :] = d_middle
        gs[2:3, :] += jnp.sum(d_middle * attn_out, axis=0, keepdims=True)
        rounded = (d_middle * mod_ref[2:3, :]).astype(bf16)
        d_attn[rows, :] = rounded
        gs[7:8, :] += jnp.sum(rounded.astype(f32), axis=0, keepdims=True)
    for load in second_loads:
        load.wait()
    do2[...] = dot_t(d_attn[...], wo2[...]).astype(bf16)
    do1[...] = dot_t(d_attn[...], wo1[...]).astype(bf16)
    tile = (high, 2, 2, share, width)
    att2[:, :, :, :, 3 * width :] = t_dot(d_attn[...], a2[...]).astype(bf16).reshape(tile)
    att1[:, :, :, :, 3 * width :] = t_dot(d_attn[...], a1[...]).astype(bf16).reshape(tile)

    def matrix_grads(att):
        for which, grad in enumerate((dq[...], dk[...].astype(bf16), dv[...].astype(bf16))):
            att[:, :, :, :, which * width : (which + 1) * width] = t_dot(normed[...], grad).astype(bf16).reshape(tile)

    def norm_grads(w_ref):
        return dot(dq[...], w_ref[0]) + dot(dk[...].astype(bf16), w_ref[1]) + dot(dv[...].astype(bf16), w_ref[2])

    def bias_grads(which):
        late[which] = jnp.zeros(late.shape[1:], f32)
        late[which, 0:1, :width] = jnp.sum(dq[...].astype(f32), axis=0, keepdims=True)
        late[which, 0:1, width : 2 * width] = jnp.sum(dv[...].astype(bf16).astype(f32), axis=0, keepdims=True)

    def load_ada(i, buf):
        return copies.local(w_ada.at[:, pl.ds(i * model, model)], buf.at[pl.ds(0, model), :])

    ada_bufs = [cot, theirs, dnf_t, ffn_t, d_attn, x]
    ada = [load_ada(i, ada_bufs[i]) for i in range(5)]

    for which, ref in enumerate((sums1_ref, sums2_ref)):
        sums[which] = ref[...]
        sums[which, 12:13, :] = gs[7:8, :]
        sums[which, 13:14, :] = gdown_ref[0:1, :]
    rows_ref[0, 0:6, :] = gs[0:6, :].astype(bf16)
    rows_ref[0, 6:8, :] = silu_ref[0:2, :]

    def small_chain(rows, total, got):
        count = 1
        for level, bit in enumerate(bits):
            hop = copies.remote(rows.at[pl.ds(0, count)], rows.at[pl.ds(count, count)], wide_dev[bit])
            other = copies.remote(total, got.at[level], wide_dev[bit])
            yield
            hop.wait_recv()
            copies.settle(other)
            total[...] = total[...] + got[level]
            count *= 2
        hop = copies.remote(rows.at[pl.ds(0, count)], rows.at[pl.ds(count, count)], chip_dev)
        other = copies.remote(total.at[1], got.at[len(bits), 0], chip_dev)
        yield
        hop.wait_recv()
        other.wait_recv()
        yield total[0] + got[len(bits), 0]

    small = small_chain(rows_ref, sums, got_sums)
    step_on(small)

    for load in loads_2:
        load.wait()

    def between_other(index):
        if index == 0:
            step_on(up_chain, oth_dn_chain, small)
        if index == 1:
            for load in loads_own[1:]:
                load.wait()
            step_on(own_dn_chain, small)

    attend_back(bias_ref, q2, k2, v2, do2, l2, (qm, gm, km), dq, dk, dv, between_other)
    matrix_grads(att2)
    att2_chains = [att_chain(att2, which, att_heads[which], att_tails[which]) for which in range(2)]
    step_on(*att2_chains)
    bias_grads(1)
    dnf[...] = norm_grads(wq2).astype(bf16)

    def pass_on(arrived, array, step):
        arrived.wait_recv()
        rows = whole_rows(1 - chip, step)
        return copies.remote(array.at[rows, :], array.at[rows, :], core_dev)

    out_passed = [pass_on(out_in[step], out_all, step) for step in range(half_steps)]

    for load in loads_1:
        load.wait()

    def between_own(index):
        if index == 0:
            step_on(oth_dn_chain, small)
        if index == 1:
            step_on(own_dn_chain)

    attend_back(bias_ref, q1, k1, v1, do1, l1, (qm, gm, km), dq, dk, dv, between_own)
    dnf[...] = added(dnf[...], norm_grads(wq1))
    dn_in = []
    for step in range(steps):
        rows = pl.ds(pl.multiple_of(lax.rem((1 - core) * half_steps + step, steps) * block, block), block)
        dn_in.append(copies.remote(dnf.at[rows, :], dn_t.at[rows, :], core_dev))
    step_on(up_chain, *att2_chains)
    matrix_grads(att1)
    att1_chains = [att_chain(att1, which, att_heads[2 + which], att_tails[2 + which]) for which in range(2)]
    step_on(*att1_chains)
    bias_grads(0)

    grad_in = []
    for step in range(steps):
        rows = rows_at(step)
        dn_in[step].wait_recv()
        grad_n = dnf[rows, :].astype(f32) + dn_t[rows, :].astype(f32)
        plain, inv_std = norm(x[rows, :].astype(f32))
        gs[0:1, :] += jnp.sum(grad_n, axis=0, keepdims=True)
        gs[1:2, :] += jnp.sum(grad_n * plain, axis=0, keepdims=True)
        part[rows, :] = (d_mid[rows, :] + norm_back(grad_n * (1.0 + mod_ref[1:2, :]), plain, inv_std)).astype(bf16)
        copies.save(part.at[rows, :], grad_all.at[whole_rows(chip, step), :])
        if step < half_steps:
            grad_in.append(copies.remote(part.at[rows, :], grad_all.at[whole_rows(chip, step), :], chip_dev))

    rows_late_ref[0] = gs[...].astype(bf16)
    last_small = small_chain(rows_late_ref, late, got_late)
    step_on(last_small)
    ada.append(load_ada(5, ada_bufs[5]))
    step_on(*att2_chains)
    oth_dn_left = rest_of(oth_dn_chain)
    hop_y_dn = copies.remote(oth_dn_left.at[0], got_y_ffn, chip_dev)
    step_on(last_small, *att1_chains)

    grads = jnp.concatenate((gs[0:6, :], jnp.zeros((2, model), f32)), axis=0).astype(bf16)
    total = jnp.zeros((8, model), f32)
    for i in range(6):
        ada[i].wait()
        row = jnp.broadcast_to(grads[i : i + 1, :], (8, model))
        total = total + dot_t(row, ada_bufs[i][0:model, :])
    step_on(last_small, up_chain)
    att2_left = [rest_of(chain) for chain in att2_chains]
    hops_y = [copies.remote(left.at[0], got_y_att.at[which], chip_dev) for which, left in enumerate(att2_left)]
    step_on(*att1_chains)
    gcond[...] = total
    hop_cond = copies.remote(gcond, got_cond, chip_dev)
    for _ in bits[2:]:
        step_on(last_small)
    own_up_left = rest_of(up_chain)
    own_dn_left = rest_of(own_dn_chain)
    grad_passed = [pass_on(grad_in[step], grad_all, step) for step in range(half_steps)]
    att1_left = [rest_of(chain) for chain in att1_chains]
    gffn_ref[0] = own_up_left[0].astype(f32)
    hop_y_dn.wait_recv()
    gffn_ref[1] = own_dn_left[0].astype(f32) + got_y_ffn[...].astype(f32)
    for which in range(2):
        hops_y[which].wait_recv()
        gatt_ref[:, which * 2 * width : (which + 1) * 2 * width] = att1_left[which][0].astype(f32) + got_y_att[which].astype(f32)
    small_ref[0:16, :] = rest_of(small)
    small_ref[16:24, :] = rest_of(last_small)
    hop_cond.wait_recv()
    cond = cond_ref[...].astype(f32)
    sig = 1.0 / (1.0 + jnp.exp(-cond))
    here, there = total[0:1, :], got_cond[0:1, :]
    both = jnp.concatenate((jnp.where(chip == 0, here, there), jnp.where(chip == 0, there, here)), axis=0)
    gcond_ref[...] = both * (sig * (1.0 + cond * (1.0 - sig)))
    for copy in out_passed + grad_passed:
        copy.wait_recv()
    copies.finish()


def back(n_wide, tokens, cotangent, arrays, vectors):
    length, model = arrays[0].shape
    width, chans = arrays[19].shape[0], model
    assert len(arrays) == BACK_ANY_IN - 2 and len(vectors) == BACK_VMEM_IN
    share = model // n_wide
    high = n_wide // 4
    heads = width // HEAD_DIM
    latents = 2 * n_wide
    levels = n_wide.bit_length()
    tall = ((length, model), bf16)
    slim = ((length, width), bf16)
    slim32 = ((length, width), f32)
    lse = ((length, 8), f32)
    wq = ((3, width, model), bf16)
    wo = ((width, model), bf16)
    half = ((high, 2, share, chans), bf16)
    left = max(high - 1, 1)
    masked = ((heads, length, width), bf16)
    att = ((high, 2, 2, share, 4 * width), bf16)
    att_half = ((high, 2, share, 2 * width), bf16)
    att_quarter = ((high, share, 2 * width), bf16)
    att_last = ((left, share, 2 * width), bf16)
    scratch = [tall] * 9 + [slim] * 4 + [lse] + [slim] * 4 + [lse, wq, wq, wo, wo, ((length, LANES), f32)]
    quarter = ((high, share, chans), bf16)
    last = ((left, share, chans), bf16)
    scratch += [half] * 7 + [quarter, quarter, last, last] * 3
    scratch += [((length, model), f32), tall, slim, slim, masked, masked, masked, slim, slim32, slim32]
    scratch += [att, att] + [att_half] * 8 + [att_quarter, att_quarter, att_last, att_last] * 4
    scratch += [((share, chans), bf16), ((2, share, 2 * width), bf16), ((8, model), f32), ((8, model), f32)]
    scratch += [((2, 8, model), f32), ((levels, 2, 8, model), f32)]
    scratch += [tall, ((2, 16, model), f32), ((levels, 2, 16, model), f32), ((8, model), f32)]
    any_spec = pl.BlockSpec(memory_space=pl.ANY)
    vmem = pl.BlockSpec(memory_space=pltpu.VMEM)
    full = sds((2 * length, model), bf16)
    return pl.pallas_call(
        functools.partial(back_kernel, n_wide),
        in_specs=[any_spec] * BACK_ANY_IN + [vmem] * BACK_VMEM_IN,
        out_specs=[any_spec] * BACK_ANY_OUT + [vmem] * BACK_VMEM_OUT,
        out_shape=[full, full]
        + [sds((2, share, chans), f32), sds((share, 4 * width), f32), sds((24, model), f32)] + [sds((latents, 8, model), bf16)] * 2
        + [sds((2, model), f32)],
        scratch_shapes=[pltpu.VMEM(*s) for s in scratch]
        + [pltpu.SemaphoreType.DMA((96,)), pltpu.SemaphoreType.DMA((160,)), pltpu.SemaphoreType.DMA((160,))],
        compiler_params=pltpu.CompilerParams(vmem_limit_bytes=63 * MIB, collective_id=2, has_side_effects=True),
        cost_estimate=cost(65),
        name="back",
    )(tokens, cotangent, *arrays, *vectors)


def finish_kernel(
    wide_ref, grad_ref, block_ref, rows_ref, late_ref, gffn_ref, gatt_ref, small_ref,
    out_ref, blockout_ref, gada_ref, gbada_ref, gqkv_ref, gbqkv_ref, gwo_ref, gbo_ref, gup_ref, gbup_ref, gcw_ref, gcb_ref, gdown_ref, gbdown_ref,
    flat, turned,
):
    out_ref[...] = grad_ref[...].astype(f32)
    blockout_ref[...] = block_ref[...]

    step = pl.program_id(0)
    model = rows_ref.shape[2]
    share, width = gqkv_ref.shape[1:]
    wide = wide_ref[0]

    @pl.when(step == 0)
    def _():
        turned[...] = rows_ref[:, 6, :].astype(f32).T

    for i in range(6):

        @pl.when(step == i)
        def _():
            silu = turned[pl.ds(pl.multiple_of(wide * share, 8), share), :].astype(bf16)
            rows = (late_ref if i < 2 else rows_ref)[:, i, :]
            gada_ref[:, i * model : (i + 1) * model] = dot(silu, rows)
            flat[0:1, i * model : (i + 1) * model] = jnp.sum(rows.astype(f32), axis=0, keepdims=True)

    @pl.when(step == 6)
    def _():
        total = 6 * model
        size = gbada_ref.shape[0]
        gbada_ref[...] = pltpu.roll(flat[...], lax.rem(total - wide * size, total), 1)[0, :size]
        shift = lax.rem(model - wide * share, model)
        rolled = pltpu.roll(small_ref[8:16, :], shift, 1)
        gbo_ref[...] = rolled[4, :share]
        gbdown_ref[...] = rolled[5, :share]
        gbqkv_ref[0:1, :] = small_ref[16:17, :width]
        gbqkv_ref[1:2, :] = small_ref[16:17, width : 2 * width]
        gcw_ref[...] = small_ref[0:9, :]
        gcb_ref[...] = small_ref[9, :]
        gbup_ref[...] = small_ref[10, :]

    @pl.when(step == 7)
    def _():
        for k in range(3):
            gqkv_ref[k] = gatt_ref[:, k * width : (k + 1) * width]
        gwo_ref[...] = gatt_ref[:, 3 * width :].T
        gup_ref[...] = gffn_ref[0]
        gdown_ref[...] = gffn_ref[1]


def finish(wide, grad, block_out, rows, rows_late, g_ffn, g_att, small, width):
    latents, _, model = rows.shape
    share = g_att.shape[0]
    chans = g_ffn.shape[2]
    height = grad.shape[0]
    parts = 8
    block = height // parts

    def whole(shape):
        return pl.BlockSpec(shape, lambda i, w: tuple(0 for _ in shape))

    tall = pl.BlockSpec((block, model), lambda i, w: (i, 0))
    outs = [
        (share, 6 * model), (6 * model * share // model,), (3, share, width), (2, width), (width, share), (share,),
        (share, chans), (chans,), (9, chans), (chans,), (share, chans), (share,),
    ]
    return pl.pallas_call(
        finish_kernel,
        grid_spec=pltpu.PrefetchScalarGridSpec(
            num_scalar_prefetch=1,
            grid=(parts,),
            in_specs=[tall, tall, whole(rows.shape), whole(rows.shape), whole(g_ffn.shape), whole(g_att.shape), whole(small.shape)],
            out_specs=[tall, tall] + [whole(o) for o in outs],
            scratch_shapes=[pltpu.VMEM((8, 6 * model), f32), pltpu.VMEM((model, latents), f32)],
        ),
        out_shape=[sds((height, model), f32), sds((height, model), bf16)] + [sds(o, f32) for o in outs],
        compiler_params=params(60),
        cost_estimate=cost(7),
        name="finish",
    )(wide, grad, block_out, rows, rows_late, g_ffn, g_att, small)


def on_device(
    n_wide, tokens, condition, validity, cotangent, w_ada, b_ada, w_qkv, b_qkv, w_out, b_out, w_up, b_up, conv_w, conv_b, w_down, b_down
):
    width = w_out.shape[0]
    w_qkv = w_qkv.transpose(0, 2, 1)
    (
        normed, q1, k1, v1, a1, l1, q2, k2, v2, a2, l2, wq2, pack2, wo2, part, theirs, dnf, dnf_t, ffn, ffn_t, gw, up1, dn1, val,
        mod, silu, bias, sums1, sums2, g_down, vec,
    ) = front(
        n_wide, tokens, condition, validity, cotangent, w_ada, b_ada, w_qkv, b_qkv, w_out, b_out, w_up, b_up, conv_w, conv_b, w_down, b_down
    )
    block_out, grad_x, g_ffn, g_att, small, rows, rows_late, grad_condition = back(
        n_wide,
        tokens,
        cotangent,
        (dnf, dnf_t, ffn, ffn_t, part, theirs, normed, q1, k1, v1, a1, l1, q2, k2, v2, a2, l2, w_qkv, wq2, w_out, wo2, gw, up1, dn1, val, w_ada),
        (mod, bias, vec, sums1, sums2, g_down, silu, condition),
    )
    wide = lax.axis_index("wide").astype(jnp.int32).reshape(1)
    (
        grad_tokens, block_out, grad_w_ada, grad_b_ada, grad_w_qkv, grad_b_qkv, grad_w_out, grad_b_out, grad_w_up, grad_b_up,
        grad_conv_w, grad_conv_b, grad_w_down, grad_b_down,
    ) = finish(wide, grad_x, block_out, rows, rows_late, g_ffn, g_att, small, width)
    return (
        block_out,
        grad_tokens,
        grad_condition,
        grad_w_ada,
        grad_b_ada,
        grad_w_qkv,
        grad_b_qkv,
        grad_w_out,
        grad_b_out,
        grad_w_up,
        grad_b_up,
        grad_conv_w,
        grad_conv_b,
        grad_w_down.T,
        grad_b_down,
    )


def solution(mesh):
    n_wide = mesh.shape["wide"]
    return jax.shard_map(
        functools.partial(on_device, n_wide),
        mesh=mesh,
        in_specs=(
            P("wide", None),
            P("wide", None),
            P("wide"),
            P("wide", None),
            P(),
            P(),
            P(None, None, "narrow"),
            P(None, "narrow"),
            P("narrow", None),
            P(),
            P(None, "narrow"),
            P("narrow"),
            P(None, "narrow"),
            P("narrow"),
            P("narrow", None),
            P(),
        ),
        out_specs=(
            P("wide", None),
            P("wide", None),
            P("wide", None),
            P("wide", None),
            P("wide"),
            P(None, "wide", "narrow"),
            P(None, "narrow"),
            P("narrow", "wide"),
            P("wide"),
            P("wide", "narrow"),
            P("narrow"),
            P(None, "narrow"),
            P("narrow"),
            P("narrow", "wide"),
            P("wide"),
        ),
        check_vma=False,
    )
```

```python
import functools

import jax
import jax.numpy as jnp
from jax import lax
from jax.experimental import pallas as pl
from jax.experimental.pallas import tpu as pltpu
from jax.sharding import PartitionSpec as P

HEAD_DIM = 64
GRID = 32
LANES = 128
MIB = 2**20

MESH = pl.DeviceIdType.MESH

bf16 = jnp.bfloat16
f32 = jnp.float32
epsilon = 1e-06
neg_fill = -1000000000.0

GELU_A = 0.7978845608
GELU_B = 0.044715


def dot(a, b):
    return jnp.dot(a, b, preferred_element_type=f32)


def dot_t(a, b):
    return lax.dot_general(a, b, (((1,), (1,)), ((), ())), preferred_element_type=f32)


def t_dot(a, b):
    return lax.dot_general(a, b, (((0,), (0,)), ((), ())), preferred_element_type=f32)


def norm(values):
    center = jnp.mean(values, axis=-1, keepdims=True)
    centered = values - center
    inv_std = lax.rsqrt(jnp.mean(centered * centered, axis=-1, keepdims=True) + epsilon)
    return centered * inv_std, inv_std


def norm_back(grad_plain, plain, inv_std):
    first_mean = jnp.mean(grad_plain, axis=-1, keepdims=True)
    second_mean = jnp.mean(grad_plain * plain, axis=-1, keepdims=True)
    return inv_std * (grad_plain - first_mean - plain * second_mean)


def wide_lanes(column, width):
    return jnp.concatenate([column] * (width // LANES), axis=1)


def of_head(values, head):
    lane = lax.broadcasted_iota(jnp.int32, values.shape, 1)
    inside = (lane >= head * HEAD_DIM) & (lane < (head + 1) * HEAD_DIM)
    return jnp.where(inside, values, jnp.zeros_like(values))


def cost(us):
    return pl.CostEstimate(flops=int(us * 1e9), bytes_accessed=0, transcendentals=0)


def params(limit):
    return pltpu.CompilerParams(vmem_limit_bytes=limit * MIB)


def sds(shape, dtype):
    return jax.ShapeDtypeStruct(shape, dtype)


def rows_of(i, size):
    return pl.ds(pl.multiple_of(i * size, size), size)


def flip(index, bit):
    return index + bit - 2 * bit * lax.rem(lax.div(index, bit), 2)


class Copies:
    def __init__(self, local_sems, send_sems, recv_sems):
        self.local_sems, self.send_sems, self.recv_sems = local_sems, send_sems, recv_sems
        self.locals, self.remotes = 0, 0
        self.pending = []

    def local(self, src, dst):
        copy = pltpu.make_async_copy(src, dst, self.local_sems.at[self.locals])
        self.locals += 1
        copy.start()
        return copy

    def save(self, src, dst):
        self.pending.append(self.local(src, dst).wait)

    def later(self, src, dst, device):
        k = self.remotes
        self.remotes += 1
        copy = pltpu.make_async_remote_copy(
            src, dst, self.send_sems.at[k], self.recv_sems.at[k], device_id=device, device_id_type=MESH
        )
        self.pending.append(copy.wait_send)
        return copy

    def settle(self, copy):
        self.pending.remove(copy.wait_send)
        copy.wait()

    def remote(self, src, dst, device):
        copy = self.later(src, dst, device)
        copy.start()
        return copy

    def finish(self):
        assert self.locals <= self.local_sems.shape[0] and self.remotes <= self.send_sems.shape[0]
        for wait in self.pending:
            wait()


def project(normed, w_ref, b_rows, q_ref, k_ref, v_ref):
    scale = HEAD_DIM ** (-0.5)
    queries = (dot_t(normed, w_ref[0]) + b_rows[0]).astype(bf16)
    q_ref[...] = (queries.astype(f32) * scale).astype(bf16)
    k_ref[...] = dot_t(normed, w_ref[1]).astype(bf16)
    v_ref[...] = (dot_t(normed, w_ref[2]) + b_rows[1]).astype(bf16)


def attend(bias_ref, q_ref, k_ref, v_ref, lse_ref, vm, finish):
    length, width = q_ref.shape
    heads = width // HEAD_DIM
    block = min(512, length)
    for head in range(heads):
        vm[head] = of_head(v_ref[...], head)
    for index in range(length // block):
        rows = pl.ds(index * block, block)
        q = q_ref[rows, :]
        k = k_ref[...]
        total = jnp.zeros((block, width), f32)
        for head in range(heads):
            s = dot_t(of_head(q, head), k) + bias_ref[...]
            top = jnp.max(s, axis=1, keepdims=True)
            raised = jnp.exp(s - top)
            mass = jnp.sum(raised, axis=1, keepdims=True)
            out = dot(raised.astype(bf16), vm[head])
            total = total + out * (1.0 / mass)
            lse_ref[rows, head : head + 1] = top + jnp.log(mass)
        finish(index, rows, total)


def ffn_half(nf, df, val_ref, wup_ref, wdn_ref, pack_ref, sums_ref, gw_ref, dnf_acc, ffn_acc, first_half, scratch, share_out, events=()):
    taps, sums, center, hs, ds, act, gact, dh = scratch
    length = nf.shape[0]
    chans = wup_ref.shape[1]
    tile = (GRID // 8, 8, LANES)
    zero = jnp.zeros((GRID, LANES), f32)
    for buf in (hs, ds):
        for j in range(3):
            buf[j, 0:GRID, :] = zero
            buf[j, length + GRID : length + 2 * GRID, :] = zero
    for t in range(11):
        taps[t] = jnp.broadcast_to(pack_ref[t : t + 1, :].astype(f32), (8, chans))
    sums[...] = jnp.zeros_like(sums)
    center[...] = dot(nf[...], wup_ref[...])
    if not first_half:
        gact[...] = dot_t(df[...], wdn_ref[...])
    column = lax.broadcasted_iota(jnp.int32, (GRID, LANES), 0)
    first = column == 0
    last = column == GRID - 1

    def put(dst, r, x):
        rows = pl.ds(pl.multiple_of((r + 1) * GRID, GRID), GRID)
        dst[1, rows, :] = x
        dst[0, rows, :] = jnp.where(first, 0.0, pltpu.roll(x, 1, 0))
        dst[2, rows, :] = jnp.where(last, 0.0, pltpu.roll(x, GRID - 1, 0))

    def near_row(buf, j, r):
        return buf[j, pl.ds(pl.multiple_of((r + 1) * GRID, GRID), GRID), :].reshape(tile)

    def channel_part(part, carry):
        for at, event in events:
            pl.when(part == at)(event)
        lanes = pl.ds(pl.multiple_of(part * LANES, LANES), LANES)

        def spread(r):
            rows = rows_of(r, GRID)
            h = (center[rows, lanes].reshape(tile) + taps[0, :, lanes]).reshape(GRID, LANES)
            put(hs, r, h * val_ref[rows, :])

        def conv_row(r):
            rows = rows_of(r, GRID)
            near = [[near_row(hs, j, r + i - 1) for j in range(3)] for i in range(3)]
            conv = jnp.broadcast_to(taps[1, :, lanes], tile)
            for i in range(3):
                for j in range(3):
                    conv = conv + taps[2 + 3 * i + j, :, lanes] * near[i][j]
            square = conv * conv
            th = jnp.tanh(conv * (GELU_A + (GELU_A * GELU_B) * square))
            half = 0.5 * conv
            act[rows, lanes] = (half + half * th).reshape(GRID, LANES).astype(bf16)
            slope = 0.5 + 0.5 * th + half * (1.0 - th * th) * (GELU_A + (3 * GELU_A * GELU_B) * square)
            dc = gact[rows, lanes].reshape(tile) * slope
            for i in range(3):
                for j in range(3):
                    sums[3 * i + j, :, lanes] += jnp.sum(dc * near[i][j], axis=0)
            sums[9, :, lanes] += jnp.sum(dc, axis=0)
            put(ds, r, dc.reshape(GRID, LANES))

        def hidden_row(r):
            rows = rows_of(r, GRID)
            total = jnp.zeros(tile, f32)
            for i in range(3):
                for j in range(3):
                    total = total + taps[2 + 3 * i + j, :, lanes] * near_row(ds, 2 - j, r + 1 - i)
            total = total * val_ref[rows, :].reshape(tile)
            rounded = total.reshape(GRID, LANES).astype(bf16)
            dh[rows, lanes] = rounded
            sums[10, :, lanes] += jnp.sum(rounded.astype(f32).reshape(tile), axis=0)

        unroll = 4

        def loop(fun):
            def some(i, c):
                for u in range(unroll):
                    fun(i * unroll + u)
                return c

            lax.fori_loop(0, GRID // unroll, some, 0)

        loop(spread)
        loop(conv_row)
        loop(hidden_row)
        return carry

    lax.fori_loop(0, chans // LANES, channel_part, 0)
    for t in range(11):
        sums_ref[t : t + 1, :] = jnp.sum(sums[t], axis=0, keepdims=True)
    sums_ref[11:16, :] = jnp.zeros((5, chans), f32)
    part_dnf = dot_t(dh[...], wup_ref[...])
    if not first_half:
        part_dnf = part_dnf + dnf_acc[...].astype(f32)
    dnf_acc[...] = part_dnf.astype(bf16)
    share_out(0)
    part_ffn = dot(act[...], wdn_ref[...])
    if not first_half:
        part_ffn = part_ffn + ffn_acc[...].astype(f32)
    ffn_acc[...] = part_ffn.astype(bf16)
    share_out(1)
    high = gw_ref.shape[0]
    share = gw_ref.shape[4]
    gw_ref[:, :, :, 0] = t_dot(nf[...], dh[...]).astype(bf16).reshape(high, 2, 2, share, chans)
    gw_ref[:, :, :, 1] = t_dot(df[...], act[...]).astype(bf16).reshape(high, 2, 2, share, chans)


FRONT_ANY_IN = 7
FRONT_VMEM_IN = 9
FRONT_ANY_OUT = 24
FRONT_VMEM_OUT = 7


def front_kernel(*refs):
    refs = list(refs)

    def take(count):
        head = refs[:count]
        del refs[:count]
        return head

    tokens, cotangent, w_ada, w_qkv, w_out, w_up, w_down = take(FRONT_ANY_IN)
    cond_ref, valid_ref, bada_ref, bqkv_ref, bout_ref, bup_ref, convw_ref, convb_ref, bdown_ref = take(FRONT_VMEM_IN)
    (
        o_normed, o_q1, o_k1, o_v1, o_a1, o_l1, o_q2, o_k2, o_v2, o_a2, o_l2, o_wqkv, o_pack, o_wout, o_part, o_theirs,
        o_dnf, o_dnf_theirs, o_ffn, o_ffn_theirs, o_gw, o_up1, o_dn1, o_val,
    ) = take(FRONT_ANY_OUT)
    mod_ref, silu_ref, bias_ref, sums1_ref, sums2_ref, gdown_ref, vec_ref = take(FRONT_VMEM_OUT)
    x, cot, normed, q1, k1, v1, a1, l1, q2, k2, v2, a2, l2, vm, val = take(15)
    wada_buf, wq1, wo1, wu1, wd1, wq2, wo2, wu2, wd2, pack1, pack2 = take(11)
    part, theirs, nf, df, dnf, ffn, gw1, gw2, got_up, got_dn = take(10)
    ffn_scratch = take(8)
    local_sems, send_sems, recv_sems = take(3)
    assert not refs

    length, model = x.shape
    width = wo1.shape[0]
    place = lax.axis_index("narrow")
    wide = lax.axis_index("wide")
    chip = lax.div(place, 2)
    x_bit = lax.rem(wide, 2)
    z_bit = lax.rem(lax.div(wide, 2), 2)
    core_dev = {"narrow": flip(place, 1)}
    chip_dev = {"narrow": flip(place, 2)}
    x_dev = {"wide": flip(wide, 1)}
    z_dev = {"wide": flip(wide, 2)}
    barrier = pltpu.get_barrier_semaphore()
    for device in (core_dev, chip_dev, x_dev, z_dev):
        pl.semaphore_signal(barrier, inc=1, device_id=device, device_id_type=MESH)
    copies = Copies(local_sems, send_sems, recv_sems)
    mine = pl.ds(pl.multiple_of(chip * length, length), length)
    slots = wada_buf.shape[0]

    def load_ada(i):
        return copies.local(w_ada.at[:, pl.ds(i * model, model)], wada_buf.at[i % slots])

    ada = [load_ada(i) for i in range(slots)]
    load_x = copies.local(tokens.at[mine, :], x)
    load_wq1 = copies.local(w_qkv, wq1)
    load_cot = copies.local(cotangent.at[mine, :], cot)
    load_wo1 = copies.local(w_out, wo1)
    load_wu1 = copies.local(w_up, wu1)
    load_wd1 = copies.local(w_down, wd1)

    pad = jnp.zeros((1, model - 2 * width), f32)
    b_row = jnp.concatenate((bqkv_ref[0:1, :].astype(f32), bqkv_ref[1:2, :].astype(f32), pad), axis=1)
    pack1[...] = jnp.concatenate(
        (
            bup_ref[...].astype(f32).reshape(1, model),
            convb_ref[...].astype(f32).reshape(1, model),
            convw_ref[...].astype(f32),
            b_row,
            jnp.zeros((4, model), f32),
        ),
        axis=0,
    ).astype(bf16)
    vec_ref[...] = jnp.concatenate(
        (bout_ref[...].astype(f32).reshape(1, model), bdown_ref[...].astype(f32).reshape(1, model), jnp.zeros((6, model), f32)),
        axis=0,
    )
    cond = jnp.where(chip == 0, cond_ref[0:1, :].astype(f32), cond_ref[1:2, :].astype(f32))
    silu = (cond / (1.0 + jnp.exp(-cond))).astype(bf16)
    silu_ref[...] = jnp.broadcast_to(silu, silu_ref.shape)
    tall = length // LANES
    for j in range(tall):
        valid = jnp.where(chip == 0, valid_ref[j : j + 1, :], valid_ref[tall + j : tall + j + 1, :]).astype(f32)
        val[j * LANES : (j + 1) * LANES, :] = jnp.broadcast_to(valid, (LANES, LANES)).T
        bias_ref[:, j * LANES : (j + 1) * LANES] = jnp.where(valid > 0, 0.0, neg_fill)
    copies.save(val, o_val)
    pl.semaphore_wait(barrier, 4)

    def half_rows(size, piece):
        return pl.ds(pl.multiple_of(x_bit * (size // 2) + piece * (size // 4), size // 4), size // 4)

    def qkv_piece(ref, piece):
        return ref.at[piece, pl.ds(pl.multiple_of(x_bit * (width // 2), width // 2), width // 2), :]

    def ffn_piece(ref, piece):
        return ref.at[half_rows(model, piece), :]

    def down_piece(ref, piece):
        size = model // 8
        return ref.at[pl.ds(pl.multiple_of(z_bit * (model // 2) + piece * size, size), size), :]

    qkv_in = [copies.remote(qkv_piece(w_qkv, p), qkv_piece(wq2, p), chip_dev) for p in range(3)]
    pack_in = copies.remote(pack1, pack2, chip_dev)
    out_in = copies.remote(w_out, wo2, chip_dev)
    up_in = [copies.remote(ffn_piece(w_up, p), ffn_piece(wu2, p), chip_dev) for p in range(2)]
    down_in = [copies.remote(down_piece(w_down, p), down_piece(wd2, p), chip_dev) for p in range(4)]

    def pass_on(arrived, ref, piece, p):
        arrived.wait_recv()
        return copies.remote(piece(ref, p), piece(ref, p), x_dev)

    mod_ref[6:8, :] = jnp.zeros((2, model), f32)
    silu8 = silu_ref[...]
    for i in range(6):
        ada[i].wait()
        row = dot(silu8, wada_buf[i % slots])[0:1, :]
        mod_ref[i : i + 1, :] = row + bada_ref[i * model : (i + 1) * model].astype(f32).reshape(1, model)
        if i + slots < 6:
            ada.append(load_ada(i + slots))

    load_x.wait()

    def normalize(i, carry):
        rows = rows_of(i, 256)
        plain, _ = norm(x[rows, :].astype(f32))
        normed[rows, :] = (plain * (1.0 + mod_ref[1:2, :]) + mod_ref[0:1, :]).astype(bf16)
        return carry

    lax.fori_loop(0, length // 256, normalize, 0)
    copies.save(normed, o_normed)
    load_wq1.wait()
    project(normed[...], wq1, (pack1[11:12, :width].astype(f32), b_row[:, width : 2 * width]), q1, k1, v1)
    for src, dst in ((q1, o_q1), (k1, o_k1), (v1, o_v1)):
        copies.save(src, dst)
    passed = {}

    def finish_own(index, rows, total):
        a1[rows, :] = total.astype(bf16)
        for p in ((0, 1), (2,))[index]:
            passed["qkv%d" % p] = pass_on(qkv_in[p], wq2, qkv_piece, p)

    attend(bias_ref, q1, k1, v1, l1, vm, finish_own)
    copies.save(a1, o_a1)
    copies.save(l1, o_l1)

    block = 256
    load_cot.wait()
    gdown_ref[...] = jnp.zeros_like(gdown_ref)
    for index in range(length // block):
        rows = pl.ds(index * block, block)
        grad_out = cot[rows, :].astype(f32) * wide_lanes(val[rows, :], model)
        rounded = (grad_out * mod_ref[5:6, :]).astype(bf16)
        df[rows, :] = rounded
        gdown_ref[0:1, :] += jnp.sum(rounded.astype(f32), axis=0, keepdims=True)
    load_wd1.wait()
    ffn_scratch[6][...] = dot_t(df[...], wd1[...])

    load_wo1.wait()
    pack_in.wait_recv()
    for p in range(3):
        passed["qkv%d" % p].wait_recv()
    row = pack2[11:12, :].astype(f32)
    project(normed[...], wq2, (row[:, :width], row[:, width : 2 * width]), q2, k2, v2)
    for src, dst in ((q2, o_q2), (k2, o_k2), (v2, o_v2), (wq2, o_wqkv), (pack2, o_pack)):
        copies.save(src, dst)
    part_in = []

    def finish_other(index, rows, total):
        if index == 0:
            out_in.wait_recv()
        rounded = total.astype(bf16)
        a2[rows, :] = rounded
        part[rows, :] = (dot(a1[rows, :], wo1[...]) + dot(rounded, wo2[...])).astype(bf16)
        part_in.append(copies.remote(part.at[rows, :], theirs.at[rows, :], core_dev))
        if index == 1:
            passed["up0"] = pass_on(up_in[0], wu2, ffn_piece, 0)

    attend(bias_ref, q2, k2, v2, l2, vm, finish_other)
    for src, dst in ((a2, o_a2), (l2, o_l2), (wo2, o_wout), (part, o_part)):
        copies.save(src, dst)

    for index in range(length // block):
        rows = pl.ds(index * block, block)
        if index % 2 == 0:
            part_in[index // 2].wait_recv()
        attn_out = part[rows, :].astype(f32) + theirs[rows, :].astype(f32) + vec_ref[0:1, :]
        middle = x[rows, :].astype(f32) + mod_ref[2:3, :] * attn_out
        plain, _ = norm(middle)
        nf[rows, :] = (plain * (1.0 + mod_ref[4:5, :]) + mod_ref[3:4, :]).astype(bf16)
    copies.save(theirs, o_theirs)

    passed["up1"] = pass_on(up_in[1], wu2, ffn_piece, 1)
    load_wu1.wait()

    def pass_down(p):
        copy = copies.later(down_piece(wd2, p), down_piece(wd2, p), z_dev)
        passed["down%d" % p] = copy

        def event():
            down_in[p].wait_recv()
            copy.start()

        return event

    downs = [pass_down(p) for p in range(4)]
    ffn_half(
        nf, df, val, wu1, wd1, pack1, sums1_ref, gw1, dnf, ffn, True, ffn_scratch, lambda i: downs[2 + i](),
        events=((2, downs[0]), (4, downs[1])),
    )
    up_got = copies.remote(gw1.at[:, :, 1 - x_bit, 0], got_up, x_dev)
    down_got = copies.remote(gw1.at[:, 1 - z_bit, :, 1], got_dn, z_dev)

    for name in ("up0", "up1", "down0", "down1", "down2", "down3"):
        passed[name].wait_recv()
    arriving = []

    def exchange(i):
        src, saved, landing = ((dnf, o_dnf, o_dnf_theirs), (ffn, o_ffn, o_ffn_theirs))[i]
        arriving.append(copies.remote(src, landing, core_dev))
        copies.save(src, saved)

    ffn_half(nf, df, val, wu2, wd2, pack2, sums2_ref, gw2, dnf, ffn, False, ffn_scratch, exchange)
    copies.save(gw2, o_gw)
    up_got.wait_recv()
    got_up[...] = (gw1[:, :, x_bit, 0].astype(f32) + got_up[...].astype(f32)).astype(bf16)
    copies.save(got_up, o_up1)
    down_got.wait_recv()
    got_dn[...] = (gw1[:, z_bit, :, 1].astype(f32) + got_dn[...].astype(f32)).astype(bf16)
    copies.save(got_dn, o_dn1)
    for copy in arriving:
        copy.wait_recv()
    copies.finish()


def front(n_wide, tokens, condition, validity, cotangent, w_ada, b_ada, w_qkv, b_qkv, w_out, b_out, w_up, b_up, conv_w, conv_b, w_down, b_down):
    latents = condition.shape[0]
    length = tokens.shape[0] // latents
    model = tokens.shape[1]
    width = w_out.shape[0]
    chans = w_up.shape[1]
    share = model // n_wide
    high = n_wide // 4
    heads = width // HEAD_DIM
    tall = ((length, model), bf16)
    slim = ((length, width), bf16)
    lse = ((length, 8), f32)
    wq = (w_qkv.shape, bf16)
    pack = ((16, chans), bf16)
    wo = (w_out.shape, bf16)
    wf = (w_up.shape, bf16)
    gw = ((high, 2, 2, 2, share, chans), bf16)
    gw_half = ((high, 2, share, chans), bf16)
    val = ((length, LANES), f32)
    outs = [tall] + [slim] * 4 + [lse] + [slim] * 4 + [lse, wq, pack, wo] + [tall] * 6 + [gw, gw_half, gw_half, val]
    small_outs = [
        ((8, model), f32),
        ((8, model), bf16),
        ((1, length), f32),
        ((16, chans), f32),
        ((16, chans), f32),
        ((8, model), f32),
        ((8, model), f32),
    ]
    scratch = [tall] * 3 + [slim] * 4 + [lse] + [slim] * 4 + [lse, ((heads, length, width), bf16), val]
    scratch += [((6, model, model), bf16), wq, wo, wf, wf, wq, wo, wf, wf, pack, pack]
    scratch += [tall] * 6 + [gw, gw, gw_half, gw_half]
    scratch += [((11, 8, chans), f32)] * 2 + [((length, chans), f32)]
    scratch += [((3, length + 2 * GRID + 8, LANES), f32)] * 2 + [((length, chans), bf16), ((length, chans), f32), ((length, chans), bf16)]
    any_spec = pl.BlockSpec(memory_space=pl.ANY)
    vmem = pl.BlockSpec(memory_space=pltpu.VMEM)
    assert len(outs) == FRONT_ANY_OUT and len(small_outs) == FRONT_VMEM_OUT
    return pl.pallas_call(
        front_kernel,
        in_specs=[any_spec] * FRONT_ANY_IN + [vmem] * FRONT_VMEM_IN,
        out_specs=[any_spec] * FRONT_ANY_OUT + [vmem] * FRONT_VMEM_OUT,
        out_shape=[sds(*o) for o in outs + small_outs],
        scratch_shapes=[pltpu.VMEM(*s) for s in scratch]
        + [pltpu.SemaphoreType.DMA((48,)), pltpu.SemaphoreType.DMA((32,)), pltpu.SemaphoreType.DMA((32,))],
        compiler_params=pltpu.CompilerParams(vmem_limit_bytes=62 * MIB, collective_id=1, has_side_effects=True),
        cost_estimate=cost(60),
        name="front",
    )(
        tokens, cotangent, w_ada, w_qkv, w_out, w_up, w_down,
        condition, validity.reshape(-1, LANES), b_ada, b_qkv, b_out, b_up, conv_w, conv_b, b_down,
    )


BACK_ANY_IN = 28
BACK_VMEM_IN = 8
BACK_ANY_OUT = 2
BACK_VMEM_OUT = 6


def attend_back(bias_ref, q_ref, k_ref, v_ref, grad_ref, lse_ref, masked, dq, dk, dv, between):
    qm, gm, km = masked
    length, width = q_ref.shape
    heads = width // HEAD_DIM
    block = min(512, length)
    scale = HEAD_DIM ** (-0.5)
    dk[...] = jnp.zeros_like(dk)
    dv[...] = jnp.zeros_like(dv)
    for head in range(heads):
        qm[head] = of_head(q_ref[...], head)
        gm[head] = of_head(grad_ref[...], head)
        km[head] = of_head(k_ref[...], head)
    for index in range(length // block):
        rows = pl.ds(index * block, block)
        k = k_ref[...]
        v = v_ref[...]
        total = jnp.zeros((block, width), f32)
        for head in range(heads):
            qh = qm[head, rows, :]
            gh = gm[head, rows, :]
            weights = jnp.exp(dot_t(qh, k) + bias_ref[...] - lse_ref[rows, head : head + 1])
            grad_weights = dot_t(gh, v)
            inner = jnp.sum(weights * grad_weights, axis=1, keepdims=True)
            grad_scores = (weights * (grad_weights - inner)).astype(bf16)
            dv[...] += t_dot(weights.astype(bf16), gh)
            dk[...] += t_dot(grad_scores, qh)
            total = total + dot(grad_scores, km[head])
        dq[rows, :] = (total * scale).astype(bf16)
        between(index)


def added(a, b):
    return (a.astype(f32) + b.astype(f32)).astype(bf16)


def back_kernel(n_wide, *refs):
    refs = list(refs)

    def take(count):
        head = refs[:count]
        del refs[:count]
        return head

    h_in = take(BACK_ANY_IN)
    (
        tokens, cotangent, h_dnf, h_dnf_t, h_ffn, h_ffn_t, h_part, h_theirs, h_normed, h_q1, h_k1, h_v1, h_a1, h_l1,
        h_q2, h_k2, h_v2, h_a2, h_l2, h_wq1, h_wq2, h_wo1, h_wo2, h_gw, h_up1, h_dn1, h_val, w_ada,
    ) = h_in
    mod_ref, bias_ref, vec_ref, sums1_ref, sums2_ref, gdown_ref, silu_ref, cond_ref = take(BACK_VMEM_IN)
    out_all, grad_all = take(BACK_ANY_OUT)
    gffn_ref, gatt_ref, small_ref, rows_ref, rows_late_ref, gcond_ref = take(BACK_VMEM_OUT)
    x, cot, dnf, dnf_t, ffn, ffn_t, part, theirs, normed, q1, k1, v1, a1, l1, q2, k2, v2, a2, l2, wq1, wq2, wo1, wo2, val = take(24)
    own_up, own_dn, oth_up, oth_dn, got_up, got_dn = take(6)
    up_more = take(3)
    ffn_tails = [take(4) for _ in range(3)]
    d_mid, d_attn, do1, do2, qm, gm, km, dq, dk, dv = take(10)
    att1, att2 = take(2)
    att_heads = [take(2) for _ in range(4)]
    att_tails = [take(4) for _ in range(4)]
    got_y_ffn, got_y_att, gcond, got_cond, late, got_late = take(6)
    dn_t, sums, got_sums, gs = take(4)
    local_sems, send_sems, recv_sems = take(3)
    assert not refs

    length, model = x.shape
    width = wo1.shape[0]
    high = own_up.shape[0]
    share = own_up.shape[2]
    place = lax.axis_index("narrow")
    wide = lax.axis_index("wide")
    chip = lax.div(place, 2)
    core = lax.rem(place, 2)
    bits = [1 << b for b in range(n_wide.bit_length() - 1)]
    bit_of = {bit: lax.rem(lax.div(wide, bit), 2) for bit in bits}
    wide_dev = {bit: {"wide": flip(wide, bit)} for bit in bits}
    x_bit, z_bit = bit_of[1], bit_of[2]
    core_dev = {"narrow": flip(place, 1)}
    chip_dev = {"narrow": flip(place, 2)}
    barrier = pltpu.get_barrier_semaphore()
    for device in [core_dev, chip_dev] + [wide_dev[bit] for bit in bits]:
        pl.semaphore_signal(barrier, inc=1, device_id=device, device_id_type=MESH)
    copies = Copies(local_sems, send_sems, recv_sems)
    block = 256
    steps = length // block
    half_steps = steps // 2

    def rows_at(step):
        return pl.ds(pl.multiple_of(lax.rem(core * half_steps + step, steps) * block, block), block)

    def whole_rows(which, step):
        start = which * length + lax.rem(core * half_steps + step, steps) * block
        return pl.ds(pl.multiple_of(start, block), block)

    first_loads = []
    for step in range(steps):
        rows = rows_at(step)
        here = whole_rows(chip, step)
        pairs = [(tokens.at[here, :], x.at[rows, :]), (cotangent.at[here, :], cot.at[rows, :])]
        pairs += [
            (src.at[rows, :], dst.at[rows, :])
            for src, dst in ((h_part, part), (h_theirs, theirs), (h_val, val), (h_ffn, ffn), (h_ffn_t, ffn_t), (h_dnf, dnf), (h_dnf_t, dnf_t))
        ]
        first_loads.append([copies.local(src, dst) for src, dst in pairs])
    loads_own = [copies.local(h_up1, own_up), copies.local(h_dn1, own_dn)]
    second_loads = [copies.local(src, dst) for src, dst in ((h_wo2, wo2), (h_wo1, wo1), (h_a2, a2), (h_a1, a1))]
    loads_2 = [
        copies.local(src, dst)
        for src, dst in ((h_q2, q2), (h_k2, k2), (h_v2, v2), (h_l2, l2), (h_normed, normed), (h_wq2, wq2))
    ]
    loads_keep = [copies.local(h_gw.at[:, :, x_bit, 0], oth_up), copies.local(h_gw.at[:, z_bit, :, 1], oth_dn)]
    loads_1 = [copies.local(src, dst) for src, dst in ((h_q1, q1), (h_k1, k1), (h_v1, v1), (h_l1, l1), (h_wq1, wq1))]
    pl.semaphore_wait(barrier, 2 + len(bits))

    def high_hops(cur, got, dst):
        left = high
        at = 0
        for bit in bits[2:]:
            left //= 2
            mine_bit = bit_of[bit]
            started = [copies.remote(cur.at[2 * i + 1 - mine_bit], got.at[at + i], wide_dev[bit]) for i in range(left)]
            yield
            for i in range(left):
                started[i].wait_recv()
                dst[at + i] = added(cur[2 * i + mine_bit], got[at + i])
            cur = dst.at[pl.ds(at, left)]
            at += left
        yield cur

    def second_hop(cur, bit, tail):
        got, summed, got_high, summed_high = tail
        hop = copies.remote(cur.at[:, 1 - bit_of[bit]], got, wide_dev[bit])
        yield
        hop.wait_recv()
        summed[...] = added(cur[:, bit_of[bit]], got[...])
        yield from high_hops(summed, got_high, summed_high)

    def other_chain(which, first, cur, got, tail):
        if first == 1:
            hop = copies.remote(h_gw.at[:, :, 1 - x_bit, which], got, wide_dev[1])
        else:
            hop = copies.remote(h_gw.at[:, 1 - z_bit, :, which], got, wide_dev[2])
        yield
        hop.wait_recv()
        loads_keep[which].wait()
        cur[...] = added(cur[...], got[...])
        yield from second_hop(cur, 3 - first, tail)

    def att_chain(att, which, head, tail):
        got, cur = head
        first = 1 + which
        lanes = pl.ds(which * 2 * width, 2 * width)
        if first == 1:
            hop = copies.remote(att.at[:, :, 1 - x_bit, :, lanes], got, wide_dev[1])
            keep = att.at[:, :, x_bit, :, lanes]
        else:
            hop = copies.remote(att.at[:, 1 - z_bit, :, :, lanes], got, wide_dev[2])
            keep = att.at[:, z_bit, :, :, lanes]
        yield
        hop.wait_recv()
        cur[...] = added(keep[...], got[...])
        yield from second_hop(cur, 3 - first, tail)

    def step_on(*chains):
        for chain in chains:
            next(chain)

    def rest_of(chain):
        result = None
        for result in chain:
            pass
        return result

    def up_parts(cur, tail):
        got_oth, oth, got_y = up_more
        got, summed, got_high, summed_high = tail
        hop_oth = copies.remote(h_gw.at[:, :, 1 - x_bit, 0], got_up, wide_dev[1])
        yield
        loads_own[0].wait()
        hop_own = copies.remote(own_up.at[:, 1 - z_bit], got, wide_dev[2])
        yield
        hop_oth.wait_recv()
        loads_keep[0].wait()
        cur[...] = added(cur[...], got_up[...])
        hop_oth = copies.remote(cur.at[:, 1 - z_bit], got_oth, wide_dev[2])
        yield
        hop_oth.wait_recv()
        oth[...] = added(cur[:, z_bit], got_oth[...])
        hop_y = copies.remote(oth, got_y, chip_dev)
        yield
        hop_own.wait_recv()
        hop_y.wait_recv()
        summed[...] = (own_up[:, z_bit].astype(f32) + got[...].astype(f32) + got_y[...].astype(f32)).astype(bf16)
        yield from high_hops(summed, got_high, summed_high)

    up_chain = up_parts(oth_up, ffn_tails[0])
    oth_dn_chain = other_chain(1, 2, oth_dn, got_dn, ffn_tails[2])
    step_on(up_chain, oth_dn_chain)
    own_dn_chain = second_hop(own_dn, 1, ffn_tails[1])

    gs[...] = jnp.zeros_like(gs)
    out_in = []
    for step in range(steps):
        rows = rows_at(step)
        for load in first_loads[step]:
            load.wait()
        attn_out = part[rows, :].astype(f32) + theirs[rows, :].astype(f32) + vec_ref[0:1, :]
        middle = x[rows, :].astype(f32) + mod_ref[2:3, :] * attn_out
        grad_out = cot[rows, :].astype(f32) * wide_lanes(val[rows, :], model)
        ffn_out = ffn[rows, :].astype(f32) + ffn_t[rows, :].astype(f32) + vec_ref[1:2, :]
        ffn[rows, :] = (middle + mod_ref[5:6, :] * ffn_out).astype(bf16)
        gs[5:6, :] += jnp.sum(grad_out * ffn_out, axis=0, keepdims=True)
        copies.save(ffn.at[rows, :], out_all.at[whole_rows(chip, step), :])
        if step < half_steps:
            out_in.append(copies.remote(ffn.at[rows, :], out_all.at[whole_rows(chip, step), :], chip_dev))
        grad_nf = dnf[rows, :].astype(f32) + dnf_t[rows, :].astype(f32)
        plain, inv_std = norm(middle)
        gs[3:4, :] += jnp.sum(grad_nf, axis=0, keepdims=True)
        gs[4:5, :] += jnp.sum(grad_nf * plain, axis=0, keepdims=True)
        d_middle = grad_out + norm_back(grad_nf * (1.0 + mod_ref[4:5, :]), plain, inv_std)
        d_mid[rows, :] = d_middle
        gs[2:3, :] += jnp.sum(d_middle * attn_out, axis=0, keepdims=True)
        rounded = (d_middle * mod_ref[2:3, :]).astype(bf16)
        d_attn[rows, :] = rounded
        gs[7:8, :] += jnp.sum(rounded.astype(f32), axis=0, keepdims=True)
    for load in second_loads:
        load.wait()
    do2[...] = dot_t(d_attn[...], wo2[...]).astype(bf16)
    do1[...] = dot_t(d_attn[...], wo1[...]).astype(bf16)
    tile = (high, 2, 2, share, width)
    att2[:, :, :, :, 3 * width :] = t_dot(d_attn[...], a2[...]).astype(bf16).reshape(tile)
    att1[:, :, :, :, 3 * width :] = t_dot(d_attn[...], a1[...]).astype(bf16).reshape(tile)

    def matrix_grads(att):
        for which, grad in enumerate((dq[...], dk[...].astype(bf16), dv[...].astype(bf16))):
            att[:, :, :, :, which * width : (which + 1) * width] = t_dot(normed[...], grad).astype(bf16).reshape(tile)

    def norm_grads(w_ref):
        return dot(dq[...], w_ref[0]) + dot(dk[...].astype(bf16), w_ref[1]) + dot(dv[...].astype(bf16), w_ref[2])

    def bias_grads(which):
        late[which] = jnp.zeros(late.shape[1:], f32)
        late[which, 0:1, :width] = jnp.sum(dq[...].astype(f32), axis=0, keepdims=True)
        late[which, 0:1, width : 2 * width] = jnp.sum(dv[...].astype(bf16).astype(f32), axis=0, keepdims=True)

    def load_ada(i, buf):
        return copies.local(w_ada.at[:, pl.ds(i * model, model)], buf.at[pl.ds(0, model), :])

    ada_bufs = [cot, theirs, dnf_t, ffn_t, d_attn, x]
    ada = [load_ada(i, ada_bufs[i]) for i in range(5)]

    for which, ref in enumerate((sums1_ref, sums2_ref)):
        sums[which] = ref[...]
        sums[which, 12:13, :] = gs[7:8, :]
        sums[which, 13:14, :] = gdown_ref[0:1, :]
    rows_ref[0, 0:6, :] = gs[0:6, :].astype(bf16)
    rows_ref[0, 6:8, :] = silu_ref[0:2, :]

    def small_chain(rows, total, got):
        count = 1
        for level, bit in enumerate(bits):
            hop = copies.remote(rows.at[pl.ds(0, count)], rows.at[pl.ds(count, count)], wide_dev[bit])
            other = copies.remote(total, got.at[level], wide_dev[bit])
            yield
            hop.wait_recv()
            copies.settle(other)
            total[...] = total[...] + got[level]
            count *= 2
        hop = copies.remote(rows.at[pl.ds(0, count)], rows.at[pl.ds(count, count)], chip_dev)
        other = copies.remote(total.at[1], got.at[len(bits), 0], chip_dev)
        yield
        hop.wait_recv()
        other.wait_recv()
        yield total[0] + got[len(bits), 0]

    small = small_chain(rows_ref, sums, got_sums)
    step_on(small, up_chain)

    for load in loads_2:
        load.wait()

    def between_other(index):
        if index == 0:
            step_on(oth_dn_chain, small)
        if index == 1:
            for load in loads_own[1:]:
                load.wait()
            step_on(up_chain, own_dn_chain, small)

    attend_back(bias_ref, q2, k2, v2, do2, l2, (qm, gm, km), dq, dk, dv, between_other)
    matrix_grads(att2)
    att2_chains = [att_chain(att2, which, att_heads[which], att_tails[which]) for which in range(2)]
    step_on(*att2_chains)
    bias_grads(1)
    dnf[...] = norm_grads(wq2).astype(bf16)

    def pass_on(arrived, array, step):
        arrived.wait_recv()
        rows = whole_rows(1 - chip, step)
        return copies.remote(array.at[rows, :], array.at[rows, :], core_dev)

    out_passed = [pass_on(out_in[step], out_all, step) for step in range(half_steps)]

    for load in loads_1:
        load.wait()

    def between_own(index):
        if index == 0:
            step_on(up_chain, oth_dn_chain, small)
        if index == 1:
            step_on(own_dn_chain)

    attend_back(bias_ref, q1, k1, v1, do1, l1, (qm, gm, km), dq, dk, dv, between_own)
    dnf[...] = added(dnf[...], norm_grads(wq1))
    dn_in = []
    for step in range(steps):
        rows = pl.ds(pl.multiple_of(lax.rem((1 - core) * half_steps + step, steps) * block, block), block)
        dn_in.append(copies.remote(dnf.at[rows, :], dn_t.at[rows, :], core_dev))
    step_on(up_chain, *att2_chains)
    matrix_grads(att1)
    att1_chains = [att_chain(att1, which, att_heads[2 + which], att_tails[2 + which]) for which in range(2)]
    step_on(*att1_chains)
    bias_grads(0)

    grad_in = []
    for step in range(steps):
        rows = rows_at(step)
        dn_in[step].wait_recv()
        grad_n = dnf[rows, :].astype(f32) + dn_t[rows, :].astype(f32)
        plain, inv_std = norm(x[rows, :].astype(f32))
        gs[0:1, :] += jnp.sum(grad_n, axis=0, keepdims=True)
        gs[1:2, :] += jnp.sum(grad_n * plain, axis=0, keepdims=True)
        part[rows, :] = (d_mid[rows, :] + norm_back(grad_n * (1.0 + mod_ref[1:2, :]), plain, inv_std)).astype(bf16)
        copies.save(part.at[rows, :], grad_all.at[whole_rows(chip, step), :])
        if step < half_steps:
            grad_in.append(copies.remote(part.at[rows, :], grad_all.at[whole_rows(chip, step), :], chip_dev))

    rows_late_ref[0] = gs[...].astype(bf16)
    last_small = small_chain(rows_late_ref, late, got_late)
    step_on(last_small)
    ada.append(load_ada(5, ada_bufs[5]))
    step_on(*att2_chains)
    oth_dn_left = rest_of(oth_dn_chain)
    hop_y_dn = copies.remote(oth_dn_left.at[0], got_y_ffn, chip_dev)
    step_on(last_small, *att1_chains)

    grads = jnp.concatenate((gs[0:6, :], jnp.zeros((2, model), f32)), axis=0).astype(bf16)
    total = jnp.zeros((8, model), f32)
    for i in range(6):
        ada[i].wait()
        row = jnp.broadcast_to(grads[i : i + 1, :], (8, model))
        total = total + dot_t(row, ada_bufs[i][0:model, :])
    step_on(last_small)
    att2_left = [rest_of(chain) for chain in att2_chains]
    hops_y = [copies.remote(left.at[0], got_y_att.at[which], chip_dev) for which, left in enumerate(att2_left)]
    step_on(*att1_chains)
    gcond[...] = total
    hop_cond = copies.remote(gcond, got_cond, chip_dev)
    for _ in bits[2:]:
        step_on(last_small)
    own_up_left = rest_of(up_chain)
    own_dn_left = rest_of(own_dn_chain)
    grad_passed = [pass_on(grad_in[step], grad_all, step) for step in range(half_steps)]
    att1_left = [rest_of(chain) for chain in att1_chains]
    gffn_ref[0] = own_up_left[0].astype(f32)
    hop_y_dn.wait_recv()
    gffn_ref[1] = own_dn_left[0].astype(f32) + got_y_ffn[...].astype(f32)
    for which in range(2):
        hops_y[which].wait_recv()
        gatt_ref[:, which * 2 * width : (which + 1) * 2 * width] = att1_left[which][0].astype(f32) + got_y_att[which].astype(f32)
    small_ref[0:16, :] = rest_of(small)
    small_ref[16:24, :] = rest_of(last_small)
    hop_cond.wait_recv()
    cond = cond_ref[...].astype(f32)
    sig = 1.0 / (1.0 + jnp.exp(-cond))
    here, there = total[0:1, :], got_cond[0:1, :]
    both = jnp.concatenate((jnp.where(chip == 0, here, there), jnp.where(chip == 0, there, here)), axis=0)
    gcond_ref[...] = both * (sig * (1.0 + cond * (1.0 - sig)))
    for copy in out_passed + grad_passed:
        copy.wait_recv()
    copies.finish()


def back(n_wide, tokens, cotangent, arrays, vectors):
    length, model = arrays[0].shape
    width, chans = arrays[19].shape[0], model
    assert len(arrays) == BACK_ANY_IN - 2 and len(vectors) == BACK_VMEM_IN
    share = model // n_wide
    high = n_wide // 4
    heads = width // HEAD_DIM
    latents = 2 * n_wide
    levels = n_wide.bit_length()
    tall = ((length, model), bf16)
    slim = ((length, width), bf16)
    slim32 = ((length, width), f32)
    lse = ((length, 8), f32)
    wq = ((3, width, model), bf16)
    wo = ((width, model), bf16)
    half = ((high, 2, share, chans), bf16)
    left = max(high - 1, 1)
    masked = ((heads, length, width), bf16)
    att = ((high, 2, 2, share, 4 * width), bf16)
    att_half = ((high, 2, share, 2 * width), bf16)
    att_quarter = ((high, share, 2 * width), bf16)
    att_last = ((left, share, 2 * width), bf16)
    scratch = [tall] * 9 + [slim] * 4 + [lse] + [slim] * 4 + [lse, wq, wq, wo, wo, ((length, LANES), f32)]
    quarter = ((high, share, chans), bf16)
    last = ((left, share, chans), bf16)
    scratch += [half] * 6 + [quarter] * 3 + [quarter, quarter, last, last] * 3
    scratch += [((length, model), f32), tall, slim, slim, masked, masked, masked, slim, slim32, slim32]
    scratch += [att, att] + [att_half] * 8 + [att_quarter, att_quarter, att_last, att_last] * 4
    scratch += [((share, chans), bf16), ((2, share, 2 * width), bf16), ((8, model), f32), ((8, model), f32)]
    scratch += [((2, 8, model), f32), ((levels, 2, 8, model), f32)]
    scratch += [tall, ((2, 16, model), f32), ((levels, 2, 16, model), f32), ((8, model), f32)]
    any_spec = pl.BlockSpec(memory_space=pl.ANY)
    vmem = pl.BlockSpec(memory_space=pltpu.VMEM)
    full = sds((2 * length, model), bf16)
    return pl.pallas_call(
        functools.partial(back_kernel, n_wide),
        in_specs=[any_spec] * BACK_ANY_IN + [vmem] * BACK_VMEM_IN,
        out_specs=[any_spec] * BACK_ANY_OUT + [vmem] * BACK_VMEM_OUT,
        out_shape=[full, full]
        + [sds((2, share, chans), f32), sds((share, 4 * width), f32), sds((24, model), f32)] + [sds((latents, 8, model), bf16)] * 2
        + [sds((2, model), f32)],
        scratch_shapes=[pltpu.VMEM(*s) for s in scratch]
        + [pltpu.SemaphoreType.DMA((96,)), pltpu.SemaphoreType.DMA((160,)), pltpu.SemaphoreType.DMA((160,))],
        compiler_params=pltpu.CompilerParams(vmem_limit_bytes=63 * MIB, collective_id=2, has_side_effects=True),
        cost_estimate=cost(65),
        name="back",
    )(tokens, cotangent, *arrays, *vectors)


def finish_kernel(
    wide_ref, grad_ref, block_ref, rows_ref, late_ref, gffn_ref, gatt_ref, small_ref,
    out_ref, blockout_ref, gada_ref, gbada_ref, gqkv_ref, gbqkv_ref, gwo_ref, gbo_ref, gup_ref, gbup_ref, gcw_ref, gcb_ref, gdown_ref, gbdown_ref,
    flat, turned,
):
    out_ref[...] = grad_ref[...].astype(f32)
    blockout_ref[...] = block_ref[...]

    step = pl.program_id(0)
    model = rows_ref.shape[2]
    share, width = gqkv_ref.shape[1:]
    wide = wide_ref[0]

    @pl.when(step == 0)
    def _():
        turned[...] = rows_ref[:, 6, :].astype(f32).T

    for i in range(3):

        @pl.when(step == i)
        def _():
            silu = turned[pl.ds(pl.multiple_of(wide * share, 8), share), :].astype(bf16)
            for part in range(2):
                at = 2 * i + part
                rows = (late_ref if at < 2 else rows_ref)[:, at, :]
                gada_ref[:, part * model : (part + 1) * model] = dot(silu, rows)
                flat[0:1, at * model : (at + 1) * model] = jnp.sum(rows.astype(f32), axis=0, keepdims=True)

    @pl.when(step == 3)
    def _():
        total = 6 * model
        size = gbada_ref.shape[0]
        gbada_ref[...] = pltpu.roll(flat[...], lax.rem(total - wide * size, total), 1)[0, :size]
        shift = lax.rem(model - wide * share, model)
        rolled = pltpu.roll(small_ref[8:16, :], shift, 1)
        gbo_ref[...] = rolled[4, :share]
        gbdown_ref[...] = rolled[5, :share]
        gbqkv_ref[0:1, :] = small_ref[16:17, :width]
        gbqkv_ref[1:2, :] = small_ref[16:17, width : 2 * width]
        gcw_ref[...] = small_ref[0:9, :]
        gcb_ref[...] = small_ref[9, :]
        gbup_ref[...] = small_ref[10, :]

    @pl.when(step == 1)
    def _():
        for k in range(3):
            gqkv_ref[k] = gatt_ref[:, k * width : (k + 1) * width]
        gwo_ref[...] = gatt_ref[:, 3 * width :].T
        gup_ref[...] = gffn_ref[0]
        gdown_ref[...] = gffn_ref[1]


def finish(wide, grad, block_out, rows, rows_late, g_ffn, g_att, small, width):
    latents, _, model = rows.shape
    share = g_att.shape[0]
    chans = g_ffn.shape[2]
    height = grad.shape[0]
    parts = 4
    block = height // parts

    def whole(shape):
        return pl.BlockSpec(shape, lambda i, w: tuple(0 for _ in shape))

    tall = pl.BlockSpec((block, model), lambda i, w: (i, 0))
    outs = [
        (share, 6 * model), (6 * model * share // model,), (3, share, width), (2, width), (width, share), (share,),
        (share, chans), (chans,), (9, chans), (chans,), (share, chans), (share,),
    ]
    return pl.pallas_call(
        finish_kernel,
        grid_spec=pltpu.PrefetchScalarGridSpec(
            num_scalar_prefetch=1,
            grid=(parts,),
            in_specs=[tall, tall, whole(rows.shape), whole(rows.shape), whole(g_ffn.shape), whole(g_att.shape), whole(small.shape)],
            out_specs=[tall, tall, pl.BlockSpec((share, 2 * model), lambda i, w: (0, jnp.minimum(i, 2)))] + [whole(o) for o in outs[1:]],
            scratch_shapes=[pltpu.VMEM((8, 6 * model), f32), pltpu.VMEM((model, latents), f32)],
        ),
        out_shape=[sds((height, model), f32), sds((height, model), bf16)] + [sds(o, f32) for o in outs],
        compiler_params=params(60),
        cost_estimate=cost(7),
        name="finish",
    )(wide, grad, block_out, rows, rows_late, g_ffn, g_att, small)


def on_device(
    n_wide, tokens, condition, validity, cotangent, w_ada, b_ada, w_qkv, b_qkv, w_out, b_out, w_up, b_up, conv_w, conv_b, w_down, b_down
):
    width = w_out.shape[0]
    w_qkv = w_qkv.transpose(0, 2, 1)
    (
        normed, q1, k1, v1, a1, l1, q2, k2, v2, a2, l2, wq2, pack2, wo2, part, theirs, dnf, dnf_t, ffn, ffn_t, gw, up1, dn1, val,
        mod, silu, bias, sums1, sums2, g_down, vec,
    ) = front(
        n_wide, tokens, condition, validity, cotangent, w_ada, b_ada, w_qkv, b_qkv, w_out, b_out, w_up, b_up, conv_w, conv_b, w_down, b_down
    )
    block_out, grad_x, g_ffn, g_att, small, rows, rows_late, grad_condition = back(
        n_wide,
        tokens,
        cotangent,
        (dnf, dnf_t, ffn, ffn_t, part, theirs, normed, q1, k1, v1, a1, l1, q2, k2, v2, a2, l2, w_qkv, wq2, w_out, wo2, gw, up1, dn1, val, w_ada),
        (mod, bias, vec, sums1, sums2, g_down, silu, condition),
    )
    wide = lax.axis_index("wide").astype(jnp.int32).reshape(1)
    (
        grad_tokens, block_out, grad_w_ada, grad_b_ada, grad_w_qkv, grad_b_qkv, grad_w_out, grad_b_out, grad_w_up, grad_b_up,
        grad_conv_w, grad_conv_b, grad_w_down, grad_b_down,
    ) = finish(wide, grad_x, block_out, rows, rows_late, g_ffn, g_att, small, width)
    return (
        block_out,
        grad_tokens,
        grad_condition,
        grad_w_ada,
        grad_b_ada,
        grad_w_qkv,
        grad_b_qkv,
        grad_w_out,
        grad_b_out,
        grad_w_up,
        grad_b_up,
        grad_conv_w,
        grad_conv_b,
        grad_w_down.T,
        grad_b_down,
    )


def solution(mesh):
    n_wide = mesh.shape["wide"]
    return jax.shard_map(
        functools.partial(on_device, n_wide),
        mesh=mesh,
        in_specs=(
            P("wide", None),
            P("wide", None),
            P("wide"),
            P("wide", None),
            P(),
            P(),
            P(None, None, "narrow"),
            P(None, "narrow"),
            P("narrow", None),
            P(),
            P(None, "narrow"),
            P("narrow"),
            P(None, "narrow"),
            P("narrow"),
            P("narrow", None),
            P(),
        ),
        out_specs=(
            P("wide", None),
            P("wide", None),
            P("wide", None),
            P("wide", None),
            P("wide"),
            P(None, "wide", "narrow"),
            P(None, "narrow"),
            P("narrow", "wide"),
            P("wide"),
            P("wide", "narrow"),
            P("narrow"),
            P(None, "narrow"),
            P("narrow"),
            P("narrow", "wide"),
            P("wide"),
        ),
        check_vma=False,
    )
```

```python
import functools

import jax
import jax.numpy as jnp
from jax import lax
from jax.experimental import pallas as pl
from jax.experimental.pallas import tpu as pltpu
from jax.sharding import PartitionSpec as P

HEAD_DIM = 64
GRID = 32
LANES = 128
MIB = 2**20

MESH = pl.DeviceIdType.MESH

bf16 = jnp.bfloat16
f32 = jnp.float32
epsilon = 1e-06
neg_fill = -1000000000.0

GELU_A = 0.7978845608
GELU_B = 0.044715


def dot(a, b):
    return jnp.dot(a, b, preferred_element_type=f32)


def dot_t(a, b):
    return lax.dot_general(a, b, (((1,), (1,)), ((), ())), preferred_element_type=f32)


def t_dot(a, b):
    return lax.dot_general(a, b, (((0,), (0,)), ((), ())), preferred_element_type=f32)


def norm(values):
    center = jnp.mean(values, axis=-1, keepdims=True)
    centered = values - center
    inv_std = lax.rsqrt(jnp.mean(centered * centered, axis=-1, keepdims=True) + epsilon)
    return centered * inv_std, inv_std


def norm_back(grad_plain, plain, inv_std):
    first_mean = jnp.mean(grad_plain, axis=-1, keepdims=True)
    second_mean = jnp.mean(grad_plain * plain, axis=-1, keepdims=True)
    return inv_std * (grad_plain - first_mean - plain * second_mean)


def wide_lanes(column, width):
    return jnp.concatenate([column] * (width // LANES), axis=1)


def of_head(values, head):
    lane = lax.broadcasted_iota(jnp.int32, values.shape, 1)
    inside = (lane >= head * HEAD_DIM) & (lane < (head + 1) * HEAD_DIM)
    return jnp.where(inside, values, jnp.zeros_like(values))


def cost(us):
    return pl.CostEstimate(flops=int(us * 1e9), bytes_accessed=0, transcendentals=0)


def params(limit):
    return pltpu.CompilerParams(vmem_limit_bytes=limit * MIB)


def sds(shape, dtype):
    return jax.ShapeDtypeStruct(shape, dtype)


def rows_of(i, size):
    return pl.ds(pl.multiple_of(i * size, size), size)


def flip(index, bit):
    return index + bit - 2 * bit * lax.rem(lax.div(index, bit), 2)


class Copies:
    def __init__(self, local_sems, send_sems, recv_sems):
        self.local_sems, self.send_sems, self.recv_sems = local_sems, send_sems, recv_sems
        self.locals, self.remotes = 0, 0
        self.pending = []

    def local(self, src, dst):
        copy = pltpu.make_async_copy(src, dst, self.local_sems.at[self.locals])
        self.locals += 1
        copy.start()
        return copy

    def save(self, src, dst):
        self.pending.append(self.local(src, dst).wait)

    def later(self, src, dst, device):
        k = self.remotes
        self.remotes += 1
        copy = pltpu.make_async_remote_copy(
            src, dst, self.send_sems.at[k], self.recv_sems.at[k], device_id=device, device_id_type=MESH
        )
        self.pending.append(copy.wait_send)
        return copy

    def settle(self, copy):
        self.pending.remove(copy.wait_send)
        copy.wait()

    def remote(self, src, dst, device):
        copy = self.later(src, dst, device)
        copy.start()
        return copy

    def finish(self):
        assert self.locals <= self.local_sems.shape[0] and self.remotes <= self.send_sems.shape[0]
        for wait in self.pending:
            wait()


def project(normed, w_ref, b_rows, q_ref, k_ref, v_ref):
    scale = HEAD_DIM ** (-0.5)
    queries = (dot_t(normed, w_ref[0]) + b_rows[0]).astype(bf16)
    q_ref[...] = (queries.astype(f32) * scale).astype(bf16)
    k_ref[...] = dot_t(normed, w_ref[1]).astype(bf16)
    v_ref[...] = (dot_t(normed, w_ref[2]) + b_rows[1]).astype(bf16)


def attend(bias_ref, q_ref, k_ref, v_ref, lse_ref, vm, finish):
    length, width = q_ref.shape
    heads = width // HEAD_DIM
    block = min(512, length)
    for head in range(heads):
        vm[head] = of_head(v_ref[...], head)
    for index in range(length // block):
        rows = pl.ds(index * block, block)
        q = q_ref[rows, :]
        k = k_ref[...]
        total = jnp.zeros((block, width), f32)
        for head in range(heads):
            s = dot_t(of_head(q, head), k) + bias_ref[...]
            top = jnp.max(s, axis=1, keepdims=True)
            raised = jnp.exp(s - top)
            mass = jnp.sum(raised, axis=1, keepdims=True)
            out = dot(raised.astype(bf16), vm[head])
            total = total + out * (1.0 / mass)
            lse_ref[rows, head : head + 1] = top + jnp.log(mass)
        finish(index, rows, total)


def ffn_half(nf, df, val_ref, wup_ref, wdn_ref, pack_ref, sums_ref, gw_ref, dnf_acc, ffn_acc, first_half, scratch, share_out, events=()):
    taps, sums, center, hs, ds, act, gact, dh = scratch
    length = nf.shape[0]
    chans = wup_ref.shape[1]
    tile = (GRID // 8, 8, LANES)
    zero = jnp.zeros((GRID, LANES), f32)
    for buf in (hs, ds):
        for j in range(3):
            buf[j, 0:GRID, :] = zero
            buf[j, length + GRID : length + 2 * GRID, :] = zero
    for t in range(11):
        taps[t] = jnp.broadcast_to(pack_ref[t : t + 1, :].astype(f32), (8, chans))
    sums[...] = jnp.zeros_like(sums)
    center[...] = dot(nf[...], wup_ref[...])
    if not first_half:
        gact[...] = dot_t(df[...], wdn_ref[...])
    column = lax.broadcasted_iota(jnp.int32, (GRID, LANES), 0)
    first = column == 0
    last = column == GRID - 1

    def put(dst, r, x):
        rows = pl.ds(pl.multiple_of((r + 1) * GRID, GRID), GRID)
        dst[1, rows, :] = x
        dst[0, rows, :] = jnp.where(first, 0.0, pltpu.roll(x, 1, 0))
        dst[2, rows, :] = jnp.where(last, 0.0, pltpu.roll(x, GRID - 1, 0))

    def near_row(buf, j, r):
        return buf[j, pl.ds(pl.multiple_of((r + 1) * GRID, GRID), GRID), :].reshape(tile)

    def channel_part(part, carry):
        for at, event in events:
            pl.when(part == at)(event)
        lanes = pl.ds(pl.multiple_of(part * LANES, LANES), LANES)

        def spread(r):
            rows = rows_of(r, GRID)
            h = (center[rows, lanes].reshape(tile) + taps[0, :, lanes]).reshape(GRID, LANES)
            put(hs, r, h * val_ref[rows, :])

        def conv_row(r):
            rows = rows_of(r, GRID)
            near = [[near_row(hs, j, r + i - 1) for j in range(3)] for i in range(3)]
            conv = jnp.broadcast_to(taps[1, :, lanes], tile)
            for i in range(3):
                for j in range(3):
                    conv = conv + taps[2 + 3 * i + j, :, lanes] * near[i][j]
            square = conv * conv
            th = jnp.tanh(conv * (GELU_A + (GELU_A * GELU_B) * square))
            half = 0.5 * conv
            act[rows, lanes] = (half + half * th).reshape(GRID, LANES).astype(bf16)
            slope = 0.5 + 0.5 * th + half * (1.0 - th * th) * (GELU_A + (3 * GELU_A * GELU_B) * square)
            dc = gact[rows, lanes].reshape(tile) * slope
            for i in range(3):
                for j in range(3):
                    sums[3 * i + j, :, lanes] += jnp.sum(dc * near[i][j], axis=0)
            sums[9, :, lanes] += jnp.sum(dc, axis=0)
            put(ds, r, dc.reshape(GRID, LANES))

        def hidden_row(r):
            rows = rows_of(r, GRID)
            total = jnp.zeros(tile, f32)
            for i in range(3):
                for j in range(3):
                    total = total + taps[2 + 3 * i + j, :, lanes] * near_row(ds, 2 - j, r + 1 - i)
            total = total * val_ref[rows, :].reshape(tile)
            rounded = total.reshape(GRID, LANES).astype(bf16)
            dh[rows, lanes] = rounded
            sums[10, :, lanes] += jnp.sum(rounded.astype(f32).reshape(tile), axis=0)

        unroll = 4

        def loop(fun):
            def some(i, c):
                for u in range(unroll):
                    fun(i * unroll + u)
                return c

            lax.fori_loop(0, GRID // unroll, some, 0)

        loop(spread)
        loop(conv_row)
        loop(hidden_row)
        return carry

    lax.fori_loop(0, chans // LANES, channel_part, 0)
    for t in range(11):
        sums_ref[t : t + 1, :] = jnp.sum(sums[t], axis=0, keepdims=True)
    sums_ref[11:16, :] = jnp.zeros((5, chans), f32)
    part_dnf = dot_t(dh[...], wup_ref[...])
    if not first_half:
        part_dnf = part_dnf + dnf_acc[...].astype(f32)
    dnf_acc[...] = part_dnf.astype(bf16)
    share_out(0)
    part_ffn = dot(act[...], wdn_ref[...])
    if not first_half:
        part_ffn = part_ffn + ffn_acc[...].astype(f32)
    ffn_acc[...] = part_ffn.astype(bf16)
    share_out(1)
    high = gw_ref.shape[0]
    share = gw_ref.shape[4]
    gw_ref[:, :, :, 0] = t_dot(nf[...], dh[...]).astype(bf16).reshape(high, 2, 2, share, chans)
    gw_ref[:, :, :, 1] = t_dot(df[...], act[...]).astype(bf16).reshape(high, 2, 2, share, chans)


FRONT_ANY_IN = 7
FRONT_VMEM_IN = 9
FRONT_ANY_OUT = 24
FRONT_VMEM_OUT = 7


def front_kernel(*refs):
    refs = list(refs)

    def take(count):
        head = refs[:count]
        del refs[:count]
        return head

    tokens, cotangent, w_ada, w_qkv, w_out, w_up, w_down = take(FRONT_ANY_IN)
    cond_ref, valid_ref, bada_ref, bqkv_ref, bout_ref, bup_ref, convw_ref, convb_ref, bdown_ref = take(FRONT_VMEM_IN)
    (
        o_normed, o_q1, o_k1, o_v1, o_a1, o_l1, o_q2, o_k2, o_v2, o_a2, o_l2, o_wqkv, o_pack, o_wout, o_part, o_theirs,
        o_dnf, o_dnf_theirs, o_ffn, o_ffn_theirs, o_gw, o_up1, o_dn1, o_val,
    ) = take(FRONT_ANY_OUT)
    mod_ref, silu_ref, bias_ref, sums1_ref, sums2_ref, gdown_ref, vec_ref = take(FRONT_VMEM_OUT)
    x, cot, normed, q1, k1, v1, a1, l1, q2, k2, v2, a2, l2, vm, val = take(15)
    wada_buf, wq1, wo1, wu1, wd1, wq2, wo2, wu2, wd2, pack1, pack2 = take(11)
    part, theirs, nf, df, dnf, ffn, gw1, gw2, got_up, got_dn = take(10)
    ffn_scratch = take(8)
    local_sems, send_sems, recv_sems = take(3)
    assert not refs

    length, model = x.shape
    width = wo1.shape[0]
    place = lax.axis_index("narrow")
    wide = lax.axis_index("wide")
    chip = lax.div(place, 2)
    x_bit = lax.rem(wide, 2)
    z_bit = lax.rem(lax.div(wide, 2), 2)
    core_dev = {"narrow": flip(place, 1)}
    chip_dev = {"narrow": flip(place, 2)}
    x_dev = {"wide": flip(wide, 1)}
    z_dev = {"wide": flip(wide, 2)}
    barrier = pltpu.get_barrier_semaphore()
    for device in (core_dev, chip_dev, x_dev, z_dev):
        pl.semaphore_signal(barrier, inc=1, device_id=device, device_id_type=MESH)
    copies = Copies(local_sems, send_sems, recv_sems)
    mine = pl.ds(pl.multiple_of(chip * length, length), length)
    slots = wada_buf.shape[0]

    def load_ada(i):
        return copies.local(w_ada.at[:, pl.ds(i * model, model)], wada_buf.at[i % slots])

    ada = [load_ada(i) for i in range(slots)]
    load_x = copies.local(tokens.at[mine, :], x)
    load_wq1 = copies.local(w_qkv, wq1)
    load_cot = copies.local(cotangent.at[mine, :], cot)
    load_wo1 = copies.local(w_out, wo1)
    load_wu1 = copies.local(w_up, wu1)
    load_wd1 = copies.local(w_down, wd1)

    pad = jnp.zeros((1, model - 2 * width), f32)
    b_row = jnp.concatenate((bqkv_ref[0:1, :].astype(f32), bqkv_ref[1:2, :].astype(f32), pad), axis=1)
    pack1[...] = jnp.concatenate(
        (
            bup_ref[...].astype(f32).reshape(1, model),
            convb_ref[...].astype(f32).reshape(1, model),
            convw_ref[...].astype(f32),
            b_row,
            jnp.zeros((4, model), f32),
        ),
        axis=0,
    ).astype(bf16)
    vec_ref[...] = jnp.concatenate(
        (bout_ref[...].astype(f32).reshape(1, model), bdown_ref[...].astype(f32).reshape(1, model), jnp.zeros((6, model), f32)),
        axis=0,
    )
    cond = jnp.where(chip == 0, cond_ref[0:1, :].astype(f32), cond_ref[1:2, :].astype(f32))
    silu = (cond / (1.0 + jnp.exp(-cond))).astype(bf16)
    silu_ref[...] = jnp.broadcast_to(silu, silu_ref.shape)
    tall = length // LANES
    for j in range(tall):
        valid = jnp.where(chip == 0, valid_ref[j : j + 1, :], valid_ref[tall + j : tall + j + 1, :]).astype(f32)
        val[j * LANES : (j + 1) * LANES, :] = jnp.broadcast_to(valid, (LANES, LANES)).T
        bias_ref[:, j * LANES : (j + 1) * LANES] = jnp.where(valid > 0, 0.0, neg_fill)
    copies.save(val, o_val)
    pl.semaphore_wait(barrier, 4)

    def half_rows(size, piece):
        return pl.ds(pl.multiple_of(x_bit * (size // 2) + piece * (size // 4), size // 4), size // 4)

    def qkv_piece(ref, piece):
        return ref.at[piece, pl.ds(pl.multiple_of(x_bit * (width // 2), width // 2), width // 2), :]

    def ffn_piece(ref, piece):
        return ref.at[half_rows(model, piece), :]

    def down_piece(ref, piece):
        size = model // 8
        return ref.at[pl.ds(pl.multiple_of(z_bit * (model // 2) + piece * size, size), size), :]

    qkv_in = [copies.remote(qkv_piece(w_qkv, p), qkv_piece(wq2, p), chip_dev) for p in range(3)]
    pack_in = copies.remote(pack1, pack2, chip_dev)
    out_in = copies.remote(w_out, wo2, chip_dev)
    up_in = [copies.remote(ffn_piece(w_up, p), ffn_piece(wu2, p), chip_dev) for p in range(2)]
    down_in = [copies.remote(down_piece(w_down, p), down_piece(wd2, p), chip_dev) for p in range(4)]

    def pass_on(arrived, ref, piece, p):
        arrived.wait_recv()
        return copies.remote(piece(ref, p), piece(ref, p), x_dev)

    mod_ref[6:8, :] = jnp.zeros((2, model), f32)
    silu8 = silu_ref[...]
    for i in range(6):
        ada[i].wait()
        row = dot(silu8, wada_buf[i % slots])[0:1, :]
        mod_ref[i : i + 1, :] = row + bada_ref[i * model : (i + 1) * model].astype(f32).reshape(1, model)
        if i + slots < 6:
            ada.append(load_ada(i + slots))

    load_x.wait()

    def normalize(i, carry):
        rows = rows_of(i, 256)
        plain, _ = norm(x[rows, :].astype(f32))
        normed[rows, :] = (plain * (1.0 + mod_ref[1:2, :]) + mod_ref[0:1, :]).astype(bf16)
        return carry

    lax.fori_loop(0, length // 256, normalize, 0)
    copies.save(normed, o_normed)
    load_wq1.wait()
    project(normed[...], wq1, (pack1[11:12, :width].astype(f32), b_row[:, width : 2 * width]), q1, k1, v1)
    for src, dst in ((q1, o_q1), (k1, o_k1), (v1, o_v1)):
        copies.save(src, dst)
    passed = {}

    def finish_own(index, rows, total):
        a1[rows, :] = total.astype(bf16)
        for p in ((0, 1), (2,))[index]:
            passed["qkv%d" % p] = pass_on(qkv_in[p], wq2, qkv_piece, p)

    attend(bias_ref, q1, k1, v1, l1, vm, finish_own)
    copies.save(a1, o_a1)
    copies.save(l1, o_l1)

    block = 256
    load_cot.wait()
    gdown_ref[...] = jnp.zeros_like(gdown_ref)
    for index in range(length // block):
        rows = pl.ds(index * block, block)
        grad_out = cot[rows, :].astype(f32) * wide_lanes(val[rows, :], model)
        rounded = (grad_out * mod_ref[5:6, :]).astype(bf16)
        df[rows, :] = rounded
        gdown_ref[0:1, :] += jnp.sum(rounded.astype(f32), axis=0, keepdims=True)
    load_wd1.wait()
    ffn_scratch[6][...] = dot_t(df[...], wd1[...])

    load_wo1.wait()
    pack_in.wait_recv()
    for p in range(3):
        passed["qkv%d" % p].wait_recv()
    row = pack2[11:12, :].astype(f32)
    project(normed[...], wq2, (row[:, :width], row[:, width : 2 * width]), q2, k2, v2)
    for src, dst in ((q2, o_q2), (k2, o_k2), (v2, o_v2), (wq2, o_wqkv), (pack2, o_pack)):
        copies.save(src, dst)
    part_in = []

    def finish_other(index, rows, total):
        if index == 0:
            out_in.wait_recv()
        rounded = total.astype(bf16)
        a2[rows, :] = rounded
        part[rows, :] = (dot(a1[rows, :], wo1[...]) + dot(rounded, wo2[...])).astype(bf16)
        part_in.append(copies.remote(part.at[rows, :], theirs.at[rows, :], core_dev))
        if index == 1:
            passed["up0"] = pass_on(up_in[0], wu2, ffn_piece, 0)

    attend(bias_ref, q2, k2, v2, l2, vm, finish_other)
    for src, dst in ((a2, o_a2), (l2, o_l2), (wo2, o_wout), (part, o_part)):
        copies.save(src, dst)

    for index in range(length // block):
        rows = pl.ds(index * block, block)
        if index % 2 == 0:
            part_in[index // 2].wait_recv()
        attn_out = part[rows, :].astype(f32) + theirs[rows, :].astype(f32) + vec_ref[0:1, :]
        middle = x[rows, :].astype(f32) + mod_ref[2:3, :] * attn_out
        plain, _ = norm(middle)
        nf[rows, :] = (plain * (1.0 + mod_ref[4:5, :]) + mod_ref[3:4, :]).astype(bf16)
    copies.save(theirs, o_theirs)

    passed["up1"] = pass_on(up_in[1], wu2, ffn_piece, 1)
    load_wu1.wait()

    def pass_down(p):
        copy = copies.later(down_piece(wd2, p), down_piece(wd2, p), z_dev)
        passed["down%d" % p] = copy

        def event():
            down_in[p].wait_recv()
            copy.start()

        return event

    downs = [pass_down(p) for p in range(4)]
    ffn_half(
        nf, df, val, wu1, wd1, pack1, sums1_ref, gw1, dnf, ffn, True, ffn_scratch, lambda i: downs[2 + i](),
        events=((2, downs[0]), (4, downs[1])),
    )
    up_got = copies.remote(gw1.at[:, :, 1 - x_bit, 0], got_up, x_dev)
    down_got = copies.remote(gw1.at[:, 1 - z_bit, :, 1], got_dn, z_dev)

    for name in ("up0", "up1", "down0", "down1", "down2", "down3"):
        passed[name].wait_recv()
    arriving = []

    def exchange(i):
        src, saved, landing = ((dnf, o_dnf, o_dnf_theirs), (ffn, o_ffn, o_ffn_theirs))[i]
        arriving.append(copies.remote(src, landing, core_dev))
        copies.save(src, saved)

    ffn_half(nf, df, val, wu2, wd2, pack2, sums2_ref, gw2, dnf, ffn, False, ffn_scratch, exchange)
    copies.save(gw2, o_gw)
    up_got.wait_recv()
    got_up[...] = (gw1[:, :, x_bit, 0].astype(f32) + got_up[...].astype(f32)).astype(bf16)
    copies.save(got_up, o_up1)
    down_got.wait_recv()
    got_dn[...] = (gw1[:, z_bit, :, 1].astype(f32) + got_dn[...].astype(f32)).astype(bf16)
    copies.save(got_dn, o_dn1)
    for copy in arriving:
        copy.wait_recv()
    copies.finish()


def front(n_wide, tokens, condition, validity, cotangent, w_ada, b_ada, w_qkv, b_qkv, w_out, b_out, w_up, b_up, conv_w, conv_b, w_down, b_down):
    latents = condition.shape[0]
    length = tokens.shape[0] // latents
    model = tokens.shape[1]
    width = w_out.shape[0]
    chans = w_up.shape[1]
    share = model // n_wide
    high = n_wide // 4
    heads = width // HEAD_DIM
    tall = ((length, model), bf16)
    slim = ((length, width), bf16)
    lse = ((length, 8), f32)
    wq = (w_qkv.shape, bf16)
    pack = ((16, chans), bf16)
    wo = (w_out.shape, bf16)
    wf = (w_up.shape, bf16)
    gw = ((high, 2, 2, 2, share, chans), bf16)
    gw_half = ((high, 2, share, chans), bf16)
    val = ((length, LANES), f32)
    outs = [tall] + [slim] * 4 + [lse] + [slim] * 4 + [lse, wq, pack, wo] + [tall] * 6 + [gw, gw_half, gw_half, val]
    small_outs = [
        ((8, model), f32),
        ((8, model), bf16),
        ((1, length), f32),
        ((16, chans), f32),
        ((16, chans), f32),
        ((8, model), f32),
        ((8, model), f32),
    ]
    scratch = [tall] * 3 + [slim] * 4 + [lse] + [slim] * 4 + [lse, ((heads, length, width), bf16), val]
    scratch += [((6, model, model), bf16), wq, wo, wf, wf, wq, wo, wf, wf, pack, pack]
    scratch += [tall] * 6 + [gw, gw, gw_half, gw_half]
    scratch += [((11, 8, chans), f32)] * 2 + [((length, chans), f32)]
    scratch += [((3, length + 2 * GRID + 8, LANES), f32)] * 2 + [((length, chans), bf16), ((length, chans), f32), ((length, chans), bf16)]
    any_spec = pl.BlockSpec(memory_space=pl.ANY)
    vmem = pl.BlockSpec(memory_space=pltpu.VMEM)
    assert len(outs) == FRONT_ANY_OUT and len(small_outs) == FRONT_VMEM_OUT
    return pl.pallas_call(
        front_kernel,
        in_specs=[any_spec] * FRONT_ANY_IN + [vmem] * FRONT_VMEM_IN,
        out_specs=[any_spec] * FRONT_ANY_OUT + [vmem] * FRONT_VMEM_OUT,
        out_shape=[sds(*o) for o in outs + small_outs],
        scratch_shapes=[pltpu.VMEM(*s) for s in scratch]
        + [pltpu.SemaphoreType.DMA((48,)), pltpu.SemaphoreType.DMA((32,)), pltpu.SemaphoreType.DMA((32,))],
        compiler_params=pltpu.CompilerParams(vmem_limit_bytes=62 * MIB, collective_id=1, has_side_effects=True),
        cost_estimate=cost(60),
        name="front",
    )(
        tokens, cotangent, w_ada, w_qkv, w_out, w_up, w_down,
        condition, validity.reshape(-1, LANES), b_ada, b_qkv, b_out, b_up, conv_w, conv_b, b_down,
    )


BACK_ANY_IN = 28
BACK_VMEM_IN = 8
BACK_ANY_OUT = 2
BACK_VMEM_OUT = 6


def attend_back(bias_ref, q_ref, k_ref, v_ref, grad_ref, lse_ref, masked, dq, dk, dv, between):
    qm, gm, km = masked
    length, width = q_ref.shape
    heads = width // HEAD_DIM
    block = min(512, length)
    scale = HEAD_DIM ** (-0.5)
    dk[...] = jnp.zeros_like(dk)
    dv[...] = jnp.zeros_like(dv)
    for head in range(heads):
        qm[head] = of_head(q_ref[...], head)
        gm[head] = of_head(grad_ref[...], head)
        km[head] = of_head(k_ref[...], head)
    for index in range(length // block):
        rows = pl.ds(index * block, block)
        k = k_ref[...]
        v = v_ref[...]
        total = jnp.zeros((block, width), f32)
        for head in range(heads):
            qh = qm[head, rows, :]
            gh = gm[head, rows, :]
            weights = jnp.exp(dot_t(qh, k) + bias_ref[...] - lse_ref[rows, head : head + 1])
            grad_weights = dot_t(gh, v)
            inner = jnp.sum(weights * grad_weights, axis=1, keepdims=True)
            grad_scores = (weights * (grad_weights - inner)).astype(bf16)
            dv[...] += t_dot(weights.astype(bf16), gh)
            dk[...] += t_dot(grad_scores, qh)
            total = total + dot(grad_scores, km[head])
        dq[rows, :] = (total * scale).astype(bf16)
        between(index)


def added(a, b):
    return (a.astype(f32) + b.astype(f32)).astype(bf16)


def back_kernel(n_wide, *refs):
    refs = list(refs)

    def take(count):
        head = refs[:count]
        del refs[:count]
        return head

    h_in = take(BACK_ANY_IN)
    (
        tokens, cotangent, h_dnf, h_dnf_t, h_ffn, h_ffn_t, h_part, h_theirs, h_normed, h_q1, h_k1, h_v1, h_a1, h_l1,
        h_q2, h_k2, h_v2, h_a2, h_l2, h_wq1, h_wq2, h_wo1, h_wo2, h_gw, h_up1, h_dn1, h_val, w_ada,
    ) = h_in
    mod_ref, bias_ref, vec_ref, sums1_ref, sums2_ref, gdown_ref, silu_ref, cond_ref = take(BACK_VMEM_IN)
    out_all, grad_all = take(BACK_ANY_OUT)
    gffn_ref, gatt_ref, small_ref, rows_ref, rows_late_ref, gcond_ref = take(BACK_VMEM_OUT)
    x, cot, dnf, dnf_t, ffn, ffn_t, part, theirs, normed, q1, k1, v1, a1, l1, q2, k2, v2, a2, l2, wq1, wq2, wo1, wo2, val = take(24)
    own_up, own_dn, oth_up, oth_dn, got_up, got_dn = take(6)
    up_more = take(3)
    ffn_tails = [take(4) for _ in range(3)]
    d_mid, d_attn, do1, do2, qm, gm, km, dq, dk, dv = take(10)
    att1, att2 = take(2)
    att_heads = [take(2) for _ in range(4)]
    att_tails = [take(4) for _ in range(4)]
    got_y_ffn, got_y_att, gcond, got_cond, late, got_late = take(6)
    dn_t, sums, got_sums, gs = take(4)
    local_sems, send_sems, recv_sems = take(3)
    assert not refs

    length, model = x.shape
    width = wo1.shape[0]
    high = own_up.shape[0]
    share = own_up.shape[2]
    place = lax.axis_index("narrow")
    wide = lax.axis_index("wide")
    chip = lax.div(place, 2)
    core = lax.rem(place, 2)
    bits = [1 << b for b in range(n_wide.bit_length() - 1)]
    bit_of = {bit: lax.rem(lax.div(wide, bit), 2) for bit in bits}
    wide_dev = {bit: {"wide": flip(wide, bit)} for bit in bits}
    x_bit, z_bit = bit_of[1], bit_of[2]
    core_dev = {"narrow": flip(place, 1)}
    chip_dev = {"narrow": flip(place, 2)}
    barrier = pltpu.get_barrier_semaphore()
    for device in [core_dev, chip_dev] + [wide_dev[bit] for bit in bits]:
        pl.semaphore_signal(barrier, inc=1, device_id=device, device_id_type=MESH)
    copies = Copies(local_sems, send_sems, recv_sems)
    block = 256
    steps = length // block
    half_steps = steps // 2

    def rows_at(step):
        return pl.ds(pl.multiple_of(lax.rem(core * half_steps + step, steps) * block, block), block)

    def whole_rows(which, step):
        start = which * length + lax.rem(core * half_steps + step, steps) * block
        return pl.ds(pl.multiple_of(start, block), block)

    first_loads = []
    for step in range(steps):
        rows = rows_at(step)
        here = whole_rows(chip, step)
        pairs = [(tokens.at[here, :], x.at[rows, :]), (cotangent.at[here, :], cot.at[rows, :])]
        pairs += [
            (src.at[rows, :], dst.at[rows, :])
            for src, dst in ((h_part, part), (h_theirs, theirs), (h_val, val), (h_ffn, ffn), (h_ffn_t, ffn_t), (h_dnf, dnf), (h_dnf_t, dnf_t))
        ]
        first_loads.append([copies.local(src, dst) for src, dst in pairs])
    loads_own = [copies.local(h_up1, own_up), copies.local(h_dn1, own_dn)]
    second_loads = [copies.local(src, dst) for src, dst in ((h_wo2, wo2), (h_wo1, wo1), (h_a2, a2), (h_a1, a1))]
    loads_2 = [
        copies.local(src, dst)
        for src, dst in ((h_q2, q2), (h_k2, k2), (h_v2, v2), (h_l2, l2), (h_normed, normed), (h_wq2, wq2))
    ]
    loads_keep = [copies.local(h_gw.at[:, :, x_bit, 0], oth_up), copies.local(h_gw.at[:, z_bit, :, 1], oth_dn)]
    loads_1 = [copies.local(src, dst) for src, dst in ((h_q1, q1), (h_k1, k1), (h_v1, v1), (h_l1, l1), (h_wq1, wq1))]
    pl.semaphore_wait(barrier, 2 + len(bits))

    def high_hops(cur, got, dst):
        left = high
        at = 0
        for bit in bits[2:]:
            left //= 2
            mine_bit = bit_of[bit]
            started = [copies.remote(cur.at[2 * i + 1 - mine_bit], got.at[at + i], wide_dev[bit]) for i in range(left)]
            yield
            for i in range(left):
                started[i].wait_recv()
                dst[at + i] = added(cur[2 * i + mine_bit], got[at + i])
            cur = dst.at[pl.ds(at, left)]
            at += left
        yield cur

    def second_hop(cur, bit, tail):
        got, summed, got_high, summed_high = tail
        hop = copies.remote(cur.at[:, 1 - bit_of[bit]], got, wide_dev[bit])
        yield
        hop.wait_recv()
        summed[...] = added(cur[:, bit_of[bit]], got[...])
        yield from high_hops(summed, got_high, summed_high)

    def other_chain(which, first, cur, got, tail):
        if first == 1:
            hop = copies.remote(h_gw.at[:, :, 1 - x_bit, which], got, wide_dev[1])
        else:
            hop = copies.remote(h_gw.at[:, 1 - z_bit, :, which], got, wide_dev[2])
        yield
        hop.wait_recv()
        loads_keep[which].wait()
        cur[...] = added(cur[...], got[...])
        yield from second_hop(cur, 3 - first, tail)

    def att_chain(att, which, head, tail):
        got, cur = head
        first = 1 + which
        lanes = pl.ds(which * 2 * width, 2 * width)
        if first == 1:
            hop = copies.remote(att.at[:, :, 1 - x_bit, :, lanes], got, wide_dev[1])
            keep = att.at[:, :, x_bit, :, lanes]
        else:
            hop = copies.remote(att.at[:, 1 - z_bit, :, :, lanes], got, wide_dev[2])
            keep = att.at[:, z_bit, :, :, lanes]
        yield
        hop.wait_recv()
        cur[...] = added(keep[...], got[...])
        yield from second_hop(cur, 3 - first, tail)

    def step_on(*chains):
        for chain in chains:
            next(chain)

    def rest_of(chain):
        result = None
        for result in chain:
            pass
        return result

    def up_parts(cur, tail):
        got_oth, oth, got_y = up_more
        got, summed, got_high, summed_high = tail
        hop_oth = copies.remote(h_gw.at[:, :, 1 - x_bit, 0], got_up, wide_dev[1])
        yield
        loads_own[0].wait()
        hop_own = copies.remote(own_up.at[:, 1 - z_bit], got, wide_dev[2])
        yield
        hop_oth.wait_recv()
        loads_keep[0].wait()
        cur[...] = added(cur[...], got_up[...])
        hop_oth = copies.remote(cur.at[:, 1 - z_bit], got_oth, wide_dev[2])
        yield
        hop_oth.wait_recv()
        oth[...] = added(cur[:, z_bit], got_oth[...])
        hop_y = copies.remote(oth, got_y, chip_dev)
        yield
        hop_own.wait_recv()
        hop_y.wait_recv()
        summed[...] = (own_up[:, z_bit].astype(f32) + got[...].astype(f32) + got_y[...].astype(f32)).astype(bf16)
        yield from high_hops(summed, got_high, summed_high)

    up_chain = up_parts(oth_up, ffn_tails[0])
    oth_dn_chain = other_chain(1, 2, oth_dn, got_dn, ffn_tails[2])
    step_on(up_chain, oth_dn_chain)
    own_dn_chain = second_hop(own_dn, 1, ffn_tails[1])

    gs[...] = jnp.zeros_like(gs)
    out_in = []
    for step in range(steps):
        rows = rows_at(step)
        for load in first_loads[step]:
            load.wait()
        attn_out = part[rows, :].astype(f32) + theirs[rows, :].astype(f32) + vec_ref[0:1, :]
        middle = x[rows, :].astype(f32) + mod_ref[2:3, :] * attn_out
        grad_out = cot[rows, :].astype(f32) * wide_lanes(val[rows, :], model)
        ffn_out = ffn[rows, :].astype(f32) + ffn_t[rows, :].astype(f32) + vec_ref[1:2, :]
        ffn[rows, :] = (middle + mod_ref[5:6, :] * ffn_out).astype(bf16)
        gs[5:6, :] += jnp.sum(grad_out * ffn_out, axis=0, keepdims=True)
        copies.save(ffn.at[rows, :], out_all.at[whole_rows(chip, step), :])
        if step < half_steps:
            out_in.append(copies.remote(ffn.at[rows, :], out_all.at[whole_rows(chip, step), :], chip_dev))
        grad_nf = dnf[rows, :].astype(f32) + dnf_t[rows, :].astype(f32)
        plain, inv_std = norm(middle)
        gs[3:4, :] += jnp.sum(grad_nf, axis=0, keepdims=True)
        gs[4:5, :] += jnp.sum(grad_nf * plain, axis=0, keepdims=True)
        d_middle = grad_out + norm_back(grad_nf * (1.0 + mod_ref[4:5, :]), plain, inv_std)
        d_mid[rows, :] = d_middle
        gs[2:3, :] += jnp.sum(d_middle * attn_out, axis=0, keepdims=True)
        rounded = (d_middle * mod_ref[2:3, :]).astype(bf16)
        d_attn[rows, :] = rounded
        gs[7:8, :] += jnp.sum(rounded.astype(f32), axis=0, keepdims=True)
    for load in second_loads:
        load.wait()
    do2[...] = dot_t(d_attn[...], wo2[...]).astype(bf16)
    do1[...] = dot_t(d_attn[...], wo1[...]).astype(bf16)
    tile = (high, 2, 2, share, width)
    att2[:, :, :, :, 3 * width :] = t_dot(d_attn[...], a2[...]).astype(bf16).reshape(tile)
    att1[:, :, :, :, 3 * width :] = t_dot(d_attn[...], a1[...]).astype(bf16).reshape(tile)

    def matrix_grads(att):
        for which, grad in enumerate((dq[...], dk[...].astype(bf16), dv[...].astype(bf16))):
            att[:, :, :, :, which * width : (which + 1) * width] = t_dot(normed[...], grad).astype(bf16).reshape(tile)

    def norm_grads(w_ref):
        return dot(dq[...], w_ref[0]) + dot(dk[...].astype(bf16), w_ref[1]) + dot(dv[...].astype(bf16), w_ref[2])

    def bias_grads(which):
        late[which] = jnp.zeros(late.shape[1:], f32)
        late[which, 0:1, :width] = jnp.sum(dq[...].astype(f32), axis=0, keepdims=True)
        late[which, 0:1, width : 2 * width] = jnp.sum(dv[...].astype(bf16).astype(f32), axis=0, keepdims=True)

    def load_ada(i, buf):
        return copies.local(w_ada.at[:, pl.ds(i * model, model)], buf.at[pl.ds(0, model), :])

    ada_bufs = [cot, theirs, dnf_t, ffn_t, d_attn, x]
    ada = [load_ada(i, ada_bufs[i]) for i in range(5)]

    for which, ref in enumerate((sums1_ref, sums2_ref)):
        sums[which] = ref[...]
        sums[which, 12:13, :] = gs[7:8, :]
        sums[which, 13:14, :] = gdown_ref[0:1, :]
    rows_ref[0, 0:6, :] = gs[0:6, :].astype(bf16)
    rows_ref[0, 6:8, :] = silu_ref[0:2, :]

    def small_chain(rows, total, got):
        count = 1
        for level, bit in enumerate(bits):
            hop = copies.remote(rows.at[pl.ds(0, count)], rows.at[pl.ds(count, count)], wide_dev[bit])
            other = copies.remote(total, got.at[level], wide_dev[bit])
            yield
            hop.wait_recv()
            copies.settle(other)
            total[...] = total[...] + got[level]
            count *= 2
        hop = copies.remote(rows.at[pl.ds(0, count)], rows.at[pl.ds(count, count)], chip_dev)
        other = copies.remote(total.at[1], got.at[len(bits), 0], chip_dev)
        yield
        hop.wait_recv()
        other.wait_recv()
        yield total[0] + got[len(bits), 0]

    small = small_chain(rows_ref, sums, got_sums)
    step_on(small, up_chain)

    for load in loads_2:
        load.wait()

    def between_other(index):
        if index == 0:
            step_on(oth_dn_chain, small)
        if index == 1:
            for load in loads_own[1:]:
                load.wait()
            step_on(up_chain, own_dn_chain, small)

    attend_back(bias_ref, q2, k2, v2, do2, l2, (qm, gm, km), dq, dk, dv, between_other)
    matrix_grads(att2)
    att2_chains = [att_chain(att2, which, att_heads[which], att_tails[which]) for which in range(2)]
    step_on(*att2_chains)
    bias_grads(1)
    dnf[...] = norm_grads(wq2).astype(bf16)

    def pass_on(arrived, array, step):
        arrived.wait_recv()
        rows = whole_rows(1 - chip, step)
        return copies.remote(array.at[rows, :], array.at[rows, :], core_dev)

    out_passed = [pass_on(out_in[step], out_all, step) for step in range(half_steps)]

    for load in loads_1:
        load.wait()

    def between_own(index):
        if index == 0:
            step_on(up_chain, oth_dn_chain, small)
        if index == 1:
            step_on(own_dn_chain)

    attend_back(bias_ref, q1, k1, v1, do1, l1, (qm, gm, km), dq, dk, dv, between_own)
    dnf[...] = added(dnf[...], norm_grads(wq1))
    dn_in = []
    for step in range(steps):
        rows = pl.ds(pl.multiple_of(lax.rem((1 - core) * half_steps + step, steps) * block, block), block)
        dn_in.append(copies.remote(dnf.at[rows, :], dn_t.at[rows, :], core_dev))
    step_on(up_chain, att2_chains[1])
    matrix_grads(att1)
    att1_chains = [att_chain(att1, which, att_heads[2 + which], att_tails[2 + which]) for which in range(2)]
    step_on(*att1_chains)
    bias_grads(0)
    step_on(att2_chains[0])

    grad_in = []
    for step in range(steps):
        rows = rows_at(step)
        dn_in[step].wait_recv()
        grad_n = dnf[rows, :].astype(f32) + dn_t[rows, :].astype(f32)
        plain, inv_std = norm(x[rows, :].astype(f32))
        gs[0:1, :] += jnp.sum(grad_n, axis=0, keepdims=True)
        gs[1:2, :] += jnp.sum(grad_n * plain, axis=0, keepdims=True)
        part[rows, :] = (d_mid[rows, :] + norm_back(grad_n * (1.0 + mod_ref[1:2, :]), plain, inv_std)).astype(bf16)
        copies.save(part.at[rows, :], grad_all.at[whole_rows(chip, step), :])
        if step < half_steps:
            grad_in.append(copies.remote(part.at[rows, :], grad_all.at[whole_rows(chip, step), :], chip_dev))

    rows_late_ref[0] = gs[...].astype(bf16)
    last_small = small_chain(rows_late_ref, late, got_late)
    step_on(last_small)
    ada.append(load_ada(5, ada_bufs[5]))
    step_on(*att2_chains)
    oth_dn_left = rest_of(oth_dn_chain)
    hop_y_dn = copies.remote(oth_dn_left.at[0], got_y_ffn, chip_dev)
    step_on(last_small, *att1_chains)

    grads = jnp.concatenate((gs[0:6, :], jnp.zeros((2, model), f32)), axis=0).astype(bf16)
    total = jnp.zeros((8, model), f32)
    for i in range(6):
        ada[i].wait()
        row = jnp.broadcast_to(grads[i : i + 1, :], (8, model))
        total = total + dot_t(row, ada_bufs[i][0:model, :])
    step_on(last_small)
    att2_left = [rest_of(chain) for chain in att2_chains]
    hops_y = [copies.remote(left.at[0], got_y_att.at[which], chip_dev) for which, left in enumerate(att2_left)]
    step_on(*att1_chains)
    gcond[...] = total
    hop_cond = copies.remote(gcond, got_cond, chip_dev)
    for _ in bits[2:]:
        step_on(last_small)
    own_up_left = rest_of(up_chain)
    own_dn_left = rest_of(own_dn_chain)
    grad_passed = [pass_on(grad_in[step], grad_all, step) for step in range(half_steps)]
    att1_left = [rest_of(chain) for chain in att1_chains]
    gffn_ref[0] = own_up_left[0].astype(f32)
    hop_y_dn.wait_recv()
    gffn_ref[1] = own_dn_left[0].astype(f32) + got_y_ffn[...].astype(f32)
    for which in range(2):
        hops_y[which].wait_recv()
        gatt_ref[:, which * 2 * width : (which + 1) * 2 * width] = att1_left[which][0].astype(f32) + got_y_att[which].astype(f32)
    small_ref[0:16, :] = rest_of(small)
    small_ref[16:24, :] = rest_of(last_small)
    hop_cond.wait_recv()
    cond = cond_ref[...].astype(f32)
    sig = 1.0 / (1.0 + jnp.exp(-cond))
    here, there = total[0:1, :], got_cond[0:1, :]
    both = jnp.concatenate((jnp.where(chip == 0, here, there), jnp.where(chip == 0, there, here)), axis=0)
    gcond_ref[...] = both * (sig * (1.0 + cond * (1.0 - sig)))
    for copy in out_passed + grad_passed:
        copy.wait_recv()
    copies.finish()


def back(n_wide, tokens, cotangent, arrays, vectors):
    length, model = arrays[0].shape
    width, chans = arrays[19].shape[0], model
    assert len(arrays) == BACK_ANY_IN - 2 and len(vectors) == BACK_VMEM_IN
    share = model // n_wide
    high = n_wide // 4
    heads = width // HEAD_DIM
    latents = 2 * n_wide
    levels = n_wide.bit_length()
    tall = ((length, model), bf16)
    slim = ((length, width), bf16)
    slim32 = ((length, width), f32)
    lse = ((length, 8), f32)
    wq = ((3, width, model), bf16)
    wo = ((width, model), bf16)
    half = ((high, 2, share, chans), bf16)
    left = max(high - 1, 1)
    masked = ((heads, length, width), bf16)
    att = ((high, 2, 2, share, 4 * width), bf16)
    att_half = ((high, 2, share, 2 * width), bf16)
    att_quarter = ((high, share, 2 * width), bf16)
    att_last = ((left, share, 2 * width), bf16)
    scratch = [tall] * 9 + [slim] * 4 + [lse] + [slim] * 4 + [lse, wq, wq, wo, wo, ((length, LANES), f32)]
    quarter = ((high, share, chans), bf16)
    last = ((left, share, chans), bf16)
    scratch += [half] * 6 + [quarter] * 3 + [quarter, quarter, last, last] * 3
    scratch += [((length, model), f32), tall, slim, slim, masked, masked, masked, slim, slim32, slim32]
    scratch += [att, att] + [att_half] * 8 + [att_quarter, att_quarter, att_last, att_last] * 4
    scratch += [((share, chans), bf16), ((2, share, 2 * width), bf16), ((8, model), f32), ((8, model), f32)]
    scratch += [((2, 8, model), f32), ((levels, 2, 8, model), f32)]
    scratch += [tall, ((2, 16, model), f32), ((levels, 2, 16, model), f32), ((8, model), f32)]
    any_spec = pl.BlockSpec(memory_space=pl.ANY)
    vmem = pl.BlockSpec(memory_space=pltpu.VMEM)
    full = sds((2 * length, model), bf16)
    return pl.pallas_call(
        functools.partial(back_kernel, n_wide),
        in_specs=[any_spec] * BACK_ANY_IN + [vmem] * BACK_VMEM_IN,
        out_specs=[any_spec] * BACK_ANY_OUT + [vmem] * BACK_VMEM_OUT,
        out_shape=[full, full]
        + [sds((2, share, chans), f32), sds((share, 4 * width), f32), sds((24, model), f32)] + [sds((latents, 8, model), bf16)] * 2
        + [sds((2, model), f32)],
        scratch_shapes=[pltpu.VMEM(*s) for s in scratch]
        + [pltpu.SemaphoreType.DMA((96,)), pltpu.SemaphoreType.DMA((160,)), pltpu.SemaphoreType.DMA((160,))],
        compiler_params=pltpu.CompilerParams(vmem_limit_bytes=63 * MIB, collective_id=2, has_side_effects=True),
        cost_estimate=cost(65),
        name="back",
    )(tokens, cotangent, *arrays, *vectors)


def finish_kernel(
    wide_ref, grad_ref, block_ref, rows_ref, late_ref, gffn_ref, gatt_ref, small_ref,
    out_ref, blockout_ref, gada_ref, gbada_ref, gqkv_ref, gbqkv_ref, gwo_ref, gbo_ref, gup_ref, gbup_ref, gcw_ref, gcb_ref, gdown_ref, gbdown_ref,
    flat, turned,
):
    out_ref[...] = grad_ref[...].astype(f32)
    blockout_ref[...] = block_ref[...]

    step = pl.program_id(0)
    model = rows_ref.shape[2]
    share, width = gqkv_ref.shape[1:]
    wide = wide_ref[0]

    @pl.when(step == 0)
    def _():
        turned[...] = rows_ref[:, 6, :].astype(f32).T

    for i in range(3):

        @pl.when(step == i)
        def _():
            silu = turned[pl.ds(pl.multiple_of(wide * share, 8), share), :].astype(bf16)
            for part in range(2):
                at = 2 * i + part
                rows = (late_ref if at < 2 else rows_ref)[:, at, :]
                gada_ref[:, part * model : (part + 1) * model] = dot(silu, rows)
                flat[0:1, at * model : (at + 1) * model] = jnp.sum(rows.astype(f32), axis=0, keepdims=True)

    @pl.when(step == 3)
    def _():
        total = 6 * model
        size = gbada_ref.shape[0]
        gbada_ref[...] = pltpu.roll(flat[...], lax.rem(total - wide * size, total), 1)[0, :size]
        shift = lax.rem(model - wide * share, model)
        rolled = pltpu.roll(small_ref[8:16, :], shift, 1)
        gbo_ref[...] = rolled[4, :share]
        gbdown_ref[...] = rolled[5, :share]
        gbqkv_ref[0:1, :] = small_ref[16:17, :width]
        gbqkv_ref[1:2, :] = small_ref[16:17, width : 2 * width]
        gcw_ref[...] = small_ref[0:9, :]
        gcb_ref[...] = small_ref[9, :]
        gbup_ref[...] = small_ref[10, :]

    @pl.when(step == 1)
    def _():
        for k in range(3):
            gqkv_ref[k] = gatt_ref[:, k * width : (k + 1) * width]
        gwo_ref[...] = gatt_ref[:, 3 * width :].T
        gup_ref[...] = gffn_ref[0]
        gdown_ref[...] = gffn_ref[1]


def finish(wide, grad, block_out, rows, rows_late, g_ffn, g_att, small, width):
    latents, _, model = rows.shape
    share = g_att.shape[0]
    chans = g_ffn.shape[2]
    height = grad.shape[0]
    parts = 4
    block = height // parts

    def whole(shape):
        return pl.BlockSpec(shape, lambda i, w: tuple(0 for _ in shape))

    tall = pl.BlockSpec((block, model), lambda i, w: (i, 0))
    outs = [
        (share, 6 * model), (6 * model * share // model,), (3, share, width), (2, width), (width, share), (share,),
        (share, chans), (chans,), (9, chans), (chans,), (share, chans), (share,),
    ]
    return pl.pallas_call(
        finish_kernel,
        grid_spec=pltpu.PrefetchScalarGridSpec(
            num_scalar_prefetch=1,
            grid=(parts,),
            in_specs=[tall, tall, whole(rows.shape), whole(rows.shape), whole(g_ffn.shape), whole(g_att.shape), whole(small.shape)],
            out_specs=[tall, tall, pl.BlockSpec((share, 2 * model), lambda i, w: (0, jnp.minimum(i, 2)))] + [whole(o) for o in outs[1:]],
            scratch_shapes=[pltpu.VMEM((8, 6 * model), f32), pltpu.VMEM((model, latents), f32)],
        ),
        out_shape=[sds((height, model), f32), sds((height, model), bf16)] + [sds(o, f32) for o in outs],
        compiler_params=params(60),
        cost_estimate=cost(7),
        name="finish",
    )(wide, grad, block_out, rows, rows_late, g_ffn, g_att, small)


def on_device(
    n_wide, tokens, condition, validity, cotangent, w_ada, b_ada, w_qkv, b_qkv, w_out, b_out, w_up, b_up, conv_w, conv_b, w_down, b_down
):
    width = w_out.shape[0]
    w_qkv = w_qkv.transpose(0, 2, 1)
    (
        normed, q1, k1, v1, a1, l1, q2, k2, v2, a2, l2, wq2, pack2, wo2, part, theirs, dnf, dnf_t, ffn, ffn_t, gw, up1, dn1, val,
        mod, silu, bias, sums1, sums2, g_down, vec,
    ) = front(
        n_wide, tokens, condition, validity, cotangent, w_ada, b_ada, w_qkv, b_qkv, w_out, b_out, w_up, b_up, conv_w, conv_b, w_down, b_down
    )
    block_out, grad_x, g_ffn, g_att, small, rows, rows_late, grad_condition = back(
        n_wide,
        tokens,
        cotangent,
        (dnf, dnf_t, ffn, ffn_t, part, theirs, normed, q1, k1, v1, a1, l1, q2, k2, v2, a2, l2, w_qkv, wq2, w_out, wo2, gw, up1, dn1, val, w_ada),
        (mod, bias, vec, sums1, sums2, g_down, silu, condition),
    )
    wide = lax.axis_index("wide").astype(jnp.int32).reshape(1)
    (
        grad_tokens, block_out, grad_w_ada, grad_b_ada, grad_w_qkv, grad_b_qkv, grad_w_out, grad_b_out, grad_w_up, grad_b_up,
        grad_conv_w, grad_conv_b, grad_w_down, grad_b_down,
    ) = finish(wide, grad_x, block_out, rows, rows_late, g_ffn, g_att, small, width)
    return (
        block_out,
        grad_tokens,
        grad_condition,
        grad_w_ada,
        grad_b_ada,
        grad_w_qkv,
        grad_b_qkv,
        grad_w_out,
        grad_b_out,
        grad_w_up,
        grad_b_up,
        grad_conv_w,
        grad_conv_b,
        grad_w_down.T,
        grad_b_down,
    )


def solution(mesh):
    n_wide = mesh.shape["wide"]
    return jax.shard_map(
        functools.partial(on_device, n_wide),
        mesh=mesh,
        in_specs=(
            P("wide", None),
            P("wide", None),
            P("wide"),
            P("wide", None),
            P(),
            P(),
            P(None, None, "narrow"),
            P(None, "narrow"),
            P("narrow", None),
            P(),
            P(None, "narrow"),
            P("narrow"),
            P(None, "narrow"),
            P("narrow"),
            P("narrow", None),
            P(),
        ),
        out_specs=(
            P("wide", None),
            P("wide", None),
            P("wide", None),
            P("wide", None),
            P("wide"),
            P(None, "wide", "narrow"),
            P(None, "narrow"),
            P("narrow", "wide"),
            P("wide"),
            P("wide", "narrow"),
            P("narrow"),
            P(None, "narrow"),
            P("narrow"),
            P("narrow", "wide"),
            P("wide"),
        ),
        check_vma=False,
    )
```
